32 devices in a mesh: dp: 8 (over z, y), mp: 4 (over x, core).
Axes of the slice: x: 2, y: 2, z: 4, core: 2. Of those that a mesh axis runs over, the one named last changes fastest.
Arguments:
- x_in: bfloat16 [16384, 1024], P(('dp', 'mp')), may hold values from -6 to 6
- out_grad: bfloat16 [16384, 1024], P(('dp', 'mp')), may hold values from -6 to 6
- item_lengths: int32 [16, 8], P('dp'), may hold values from 0 to 512, as said below
- weight_store: float32 [4, 384, 128, 64], P('mp', 'dp'), may hold values from -2 to 2
- owner_perm: int32 [4, 384], P('mp'), may hold values from 0 to 383, as said below
- left_roots: float32 [4, 384, 128, 128], P('mp', 'dp'), may hold values from -8 to 24
- right_roots: float32 [4, 384, 64, 64], P('mp', 'dp'), may hold values from -8 to 24
- left_stats: float32 [4, 384, 128, 128], P('mp', 'dp'), may hold values from -2048 to 2048
- right_stats: float32 [4, 384, 64, 64], P('mp', 'dp'), may hold values from -2048 to 2048
- head_vectors: float32 [4, 512], P('mp', 'dp'), may hold values from -3 to 3
- head_first: float32 [4, 512], P('mp', 'dp'), may hold values from -98304 to 98304
- head_second: float32 [4, 512], P('mp', 'dp'), may hold values from 327 to 3276
- shared_vectors: float32 [10240], P(('dp', 'mp')), may hold values from -1 to 2
- shared_first: float32 [10240], P(('dp', 'mp')), may hold values from -98304 to 98304
- shared_second: float32 [10240], P(('dp', 'mp')), may hold values from 0 to 163
Outputs:
- layer_out: bfloat16 [16384, 1024], P(('dp', 'mp'))
- input_grad: float32 [16384, 1024], P(('dp', 'mp'))
- block_grads: float32 [4, 384, 128, 64], P('mp', 'dp')
- new_left: float32 [4, 384, 128, 128], P('mp', 'dp')
- new_right: float32 [4, 384, 64, 64], P('mp', 'dp')
- new_weights: float32 [4, 384, 128, 64], P('mp', 'dp')
- new_head_first: float32 [4, 512], P('mp', 'dp')
- new_head_second: float32 [4, 512], P('mp', 'dp')
- new_head: float32 [4, 512], P('mp', 'dp')
- new_shared_first: float32 [10240], P(('dp', 'mp'))
- new_shared_second: float32 [10240], P(('dp', 'mp'))
- new_shared: float32 [10240], P(('dp', 'mp'))
The draws below stay inside these ranges and needn't reach their ends.
Inputs may be any that keep to these rules, and one draw needn't show every extreme that they name: `item_lengths`: each row lists its items' lengths, each 128 or 512, in any order, then zeros; a row's lengths sum to 1024. `owner_perm`: each row is a permutation of the 384 blocks of that index's panel.
All inputs are finite; a program needn't handle non-finite values.
Results may differ from the reference program's by a relative error of at most 0.017.
Values may be sent and summed in bfloat16 or wider, within the bound.
No kernel may reach another device: no remote copies, remote signals or barrier semaphores. Data moves between devices by JAX's collectives and lax.ppermute only.
A program may use at most 256 MiB of HBM per device.

```python
import math
import jax
import jax.numpy as jnp
from jax import lax

D = 1024
H = 16
DH = 64
FF = 4096
SLOTS = 1024
SHORT = 128
LONG = 512
BR = 128
BC = 64
STEP = 10
MPW = 4
DL = 256
FL = 1024
C_MP = 3072
RG = 8
CG = 48
BLK_MP = 384
HEADV = 512
SHV = 10240
ITEMS = 8
ROWS = 16
TOKENS = 16384


stat_share = 0.08


def owner_layout(key):
    base_key = jax.random.fold_in(key, 71)
    subkeys = jax.random.split(base_key, MPW)

    def one_permutation(row_key):
        return jax.random.permutation(row_key, BLK_MP)
    return jax.vmap(one_permutation)(subkeys).astype(jnp.int32)


def block_kinds(permuted):
    column_start = permuted // RG * BC
    kinds_sum = (column_start >= DL).astype(jnp.int32) + (column_start >= 2 * DL).astype(jnp.int32) + (column_start >= 3 * DL).astype(jnp.int32) + (column_start >= 4 * DL).astype(jnp.int32) + (column_start >= 4 * DL + FL).astype(jnp.int32)
    return kinds_sum


def grad_sizes():
    return jnp.array([5.0, 5.0, 0.7, 0.085, 0.3, 0.55], jnp.float32)


def symmetric_blocks(key, lead_shape, order_n, base_scale, diag_low, diag_high, noise_factor):
    subkeys = jax.random.split(key, 2)
    diagonal = jnp.exp(jax.random.uniform(subkeys[0], lead_shape + (order_n,), jnp.float32, math.log(diag_low), math.log(diag_high)))
    raw_noise = jnp.clip(jax.random.normal(subkeys[1], lead_shape + (order_n, order_n), jnp.float32), -4.0, 4.0)
    identity = jnp.eye(order_n, dtype=jnp.float32)
    off_diag = (raw_noise + jnp.swapaxes(raw_noise, -1, -2)) * 0.5 ** 0.5 * (1.0 - identity)
    whole = diagonal[..., :, None] * identity + off_diag * (noise_factor / math.sqrt(order_n))
    return whole * base_scale[..., None, None]


def draw_owner_perm(key, part):
    return owner_layout(key)


def draw_weight_store(key, part):
    permuted = owner_layout(key)
    key = jax.random.fold_in(key, 2)
    scale_table = jnp.array([D ** (-0.5), D ** (-0.5), D ** (-0.5), (D // 16) ** (-0.5), D ** (-0.5), FF ** (-0.5)], jnp.float32)
    scales = jnp.take(scale_table, block_kinds(permuted))
    noise = jnp.clip(jax.random.normal(key, (MPW, BLK_MP, BR, BC), jnp.float32), -5.0, 5.0)
    return noise * scales[:, :, None, None]


def draw_left_stats(key, part):
    permuted = owner_layout(key)
    key = jax.random.fold_in(key, 3)
    sizes_now = jnp.take(grad_sizes(), block_kinds(permuted))
    return symmetric_blocks(key, (MPW, BLK_MP), BR, stat_share * BC * sizes_now * sizes_now, 1.0, 4.0, 1.0)


def draw_right_stats(key, part):
    permuted = owner_layout(key)
    key = jax.random.fold_in(key, 4)
    sizes_now = jnp.take(grad_sizes(), block_kinds(permuted))
    return symmetric_blocks(key, (MPW, BLK_MP), BC, stat_share * BR * sizes_now * sizes_now, 1.0, 4.0, 1.0)


def draw_left_roots(key, part):
    key = jax.random.fold_in(key, 5)
    ones_scale = jnp.ones((MPW, BLK_MP), jnp.float32)
    return symmetric_blocks(key, (MPW, BLK_MP), BR, ones_scale, 1.0, 4.0, 0.5)


def draw_right_roots(key, part):
    key = jax.random.fold_in(key, 6)
    ones_scale = jnp.ones((MPW, BLK_MP), jnp.float32)
    return symmetric_blocks(key, (MPW, BLK_MP), BC, ones_scale, 1.0, 4.0, 0.5)


def head_sizes():
    position = jnp.arange(HEADV)
    return jnp.where(position < DL, 5.0, 6.8).astype(jnp.float32) * math.sqrt(TOKENS)


def shared_sizes():
    position = jnp.arange(SHV)
    kinds_now = jnp.minimum(position // D, 6)
    size_table = jnp.array([0.85, 0.84, 1.0, 1.0, 1.0, 1.0, 0.3], jnp.float32)
    return jnp.take(size_table, kinds_now) * math.sqrt(TOKENS)


def draw_head_first(key, part):
    key = jax.random.fold_in(key, 7)
    noise = jnp.clip(jax.random.normal(key, (MPW, HEADV), jnp.float32), -6.0, 6.0)
    return noise * 0.111 * head_sizes()[None, :]


def draw_head_second(key, part):
    key = jax.random.fold_in(key, 8)
    factor = jnp.exp(jax.random.uniform(key, (MPW, HEADV), jnp.float32, 0.0, math.log(4.0)))
    sizes_now = head_sizes()
    return factor * 0.001001 * (sizes_now * sizes_now)[None, :]


def draw_shared_vectors(key, part):
    key = jax.random.fold_in(key, 9)
    noise = jnp.clip(jax.random.normal(key, (SHV,), jnp.float32), -5.0, 5.0)
    kinds_now = jnp.minimum(jnp.arange(SHV) // D, 6)
    is_gain = (kinds_now == 2) | (kinds_now == 4)
    return jnp.where(is_gain, 1.0 + 0.15 * noise, 0.2 * noise)


def draw_shared_first(key, part):
    key = jax.random.fold_in(key, 10)
    noise = jnp.clip(jax.random.normal(key, (SHV,), jnp.float32), -6.0, 6.0)
    return noise * 0.111 * shared_sizes()


def draw_shared_second(key, part):
    key = jax.random.fold_in(key, 11)
    factor = jnp.exp(jax.random.uniform(key, (SHV,), jnp.float32, 0.0, math.log(4.0)))
    sizes_now = shared_sizes()
    return factor * 0.001001 * sizes_now * sizes_now


def draw_item_lengths(key, part):
    key = jax.random.fold_in(key, 12)
    subkeys = jax.random.split(key, 2)
    long_count = jax.random.randint(subkeys[0], (ROWS,), 0, SLOTS // LONG + 1)
    first_row = jnp.arange(ROWS) == 0
    long_count = jnp.where(first_row, jnp.maximum(long_count, 1), long_count)
    item_count = long_count + (SLOTS - long_count * LONG) // SHORT
    row_keys = jax.random.split(subkeys[1], ROWS)

    def one_order(row_key):
        return jax.random.permutation(row_key, ITEMS)
    order_values = jax.vmap(one_order)(row_keys)
    slot_index = jnp.arange(ITEMS)
    is_live = slot_index[None, :] < item_count[:, None]
    is_below = (order_values[:, :, None] < order_values[:, None, :]) & is_live[:, :, None]
    item_rank = jnp.sum(is_below.astype(jnp.int32), axis=1)
    is_long = is_live & (item_rank < long_count[:, None])
    return jnp.where(is_long, LONG, jnp.where(is_live, SHORT, 0)).astype(jnp.int32)


def with_spikes(drawn, own_key, source, target, parts, factor):
    owner, partner = [(jnp.arange(drawn.shape[dim]) // (drawn.shape[dim] // parts)).reshape([-1 if axis == dim else 1 for axis in range(drawn.ndim)]) for dim in (source, target)]
    chosen = jax.random.permutation(own_key, parts)[partner]
    strong = (owner == chosen) | (owner == (partner + parts // 2) % parts)
    return jnp.where(strong, factor * drawn, drawn)


def levels(rng, shape, cuts, least, top_value):
    factor_of, own = 1.0, jax.random.fold_in(rng, 6)
    for axis_at, blocks in cuts:
        heights = jnp.exp(jax.random.uniform(jax.random.fold_in(own, axis_at), (blocks,), jnp.float32, least / len(cuts), top_value / len(cuts)))
        factor_of = factor_of * jnp.repeat(heights, shape[axis_at] // blocks).reshape([-1 if axis == axis_at else 1 for axis in range(len(shape))])
    return factor_of


def scatter_about(own_key, dims, scale, most, pieces=(), kind=jnp.bfloat16):
    factor_of = levels(own_key, dims, pieces, -0.22, 0.18) if pieces else 1.0
    values = jax.random.normal(own_key, dims, jnp.float32) * scale * factor_of
    return jnp.minimum(jnp.maximum(values, -most), most).astype(kind)


def noise_with(stream_key, dims, scale, limit, pieces, heavy, kind=jnp.bfloat16):
    values = scale * jax.random.normal(stream_key, dims, jnp.float32)
    if pieces:
        values = values * levels(stream_key, dims, pieces, -0.22, 0.18)
    return jnp.clip(with_spikes(values, jax.random.fold_in(stream_key, 3), *heavy), -limit, limit).astype(kind)


def setup_inputs(seed: int = 0) -> dict:
    streams_of = jax.random.split(jax.random.key(seed), 16)
    x_in = scatter_about(streams_of[0], (TOKENS, D), 1.0, 6.0, ((0, 32),))
    out_grad = noise_with(streams_of[1], (TOKENS, D), 1.0, 6.0, ((0, 32),), (0, 1, 32, 2.75))
    item_lengths = draw_item_lengths(jax.random.fold_in(streams_of[15], 71), 0)
    weight_store = draw_weight_store(jax.random.fold_in(streams_of[15], 71), 0)
    owner_perm = draw_owner_perm(jax.random.fold_in(streams_of[15], 71), 0)
    left_roots = draw_left_roots(jax.random.fold_in(streams_of[15], 71), 0)
    right_roots = draw_right_roots(jax.random.fold_in(streams_of[15], 71), 0)
    left_stats = draw_left_stats(jax.random.fold_in(streams_of[15], 71), 0)
    right_stats = draw_right_stats(jax.random.fold_in(streams_of[15], 71), 0)
    head_vectors = scatter_about(streams_of[9], (MPW, HEADV), 0.2, 3.0, ((0, 4), (1, 8)), jnp.float32)
    head_first = draw_head_first(jax.random.fold_in(streams_of[15], 71), 0)
    head_second = draw_head_second(jax.random.fold_in(streams_of[15], 71), 0)
    shared_vectors = draw_shared_vectors(jax.random.fold_in(streams_of[15], 71), 0)
    shared_first = draw_shared_first(jax.random.fold_in(streams_of[15], 71), 0)
    shared_second = draw_shared_second(jax.random.fold_in(streams_of[15], 71), 0)
    return dict(x_in=x_in, out_grad=out_grad, item_lengths=item_lengths, weight_store=weight_store, owner_perm=owner_perm, left_roots=left_roots, right_roots=right_roots, left_stats=left_stats, right_stats=right_stats, head_vectors=head_vectors, head_first=head_first, head_second=head_second, shared_vectors=shared_vectors, shared_first=shared_first, shared_second=shared_second)


@jax.custom_vjp
def low(v):
    return lax.optimization_barrier(v.astype(jnp.bfloat16)).astype(jnp.float32)

@jax.custom_vjp
def low_back(v):
    return v

def low_keep(v):
    return (low(v), None)

def low_pass(kept, grad):
    return (grad,)

def back_keep(v):
    return (v, None)

def back_low(kept, grad):
    return (low(grad),)
low.defvjp(low_keep, low_pass)
low_back.defvjp(back_keep, back_low)

def product(left_side, right_side):
    return jnp.dot(left_side, right_side, precision=lax.Precision.HIGHEST, preferred_element_type=jnp.float32)

def normalize(inputs, gain, shift):
    center = inputs - lax.optimization_barrier(jnp.mean(inputs, axis=-1, keepdims=True))
    spread = lax.optimization_barrier(jnp.mean(center * center, axis=-1, keepdims=True))
    return center * lax.rsqrt(spread + 1e-05) * gain + shift

def segment_ids(lengths):
    bounds = jnp.cumsum(lengths, axis=-1).astype(jnp.int32)
    position = jnp.arange(SLOTS, dtype=jnp.int32)
    return lax.optimization_barrier(jnp.sum((position[None, :, None] >= bounds[:, None, :]).astype(jnp.int32), axis=2)).astype(jnp.int32)

def layer_row(row_input, segment, params):
    w_query, w_key, w_value, w_output, w_inner, w_outer, bias_query, bias_value, bias_output, bias_outer, gain_one, shift_one, gain_two, shift_two, bias_inner = params
    scaling = DH ** (-0.5)
    inputs = low(row_input)
    queries = low(low_back(product(inputs, low(w_query)) + bias_query)).reshape(SLOTS, H, DH)
    key_rows = low(low_back(product(inputs, low(w_key)))).reshape(SLOTS, H, DH)
    value_rows = low(low_back(product(inputs, low(w_value)) + bias_value)).reshape(SLOTS, H, DH)
    scores = low_back(jnp.einsum('qhd,khd->hqk', queries, key_rows, precision=lax.Precision.HIGHEST, preferred_element_type=jnp.float32) * scaling)
    same_item = segment[:, None] == segment[None, :]
    masked = jnp.where(same_item[None], scores, -1e+30)
    maximum = lax.optimization_barrier(jnp.max(masked, axis=-1, keepdims=True))
    exponent = jnp.exp(masked - maximum)
    attention = low(exponent / lax.optimization_barrier(jnp.sum(exponent, axis=-1, keepdims=True)))
    context = jnp.einsum('hqk,khd->qhd', attention, value_rows, precision=lax.Precision.HIGHEST, preferred_element_type=jnp.float32).reshape(SLOTS, D)
    context = low(low_back(context))
    hidden = row_input + low_back(product(context, low(w_output))) + bias_output
    middle = normalize(hidden, gain_one, shift_one)
    before = low_back(product(low(middle), low(w_inner)) + bias_inner)
    activated = low(jax.nn.gelu(before, approximate=False))
    ffn_result = low_back(product(activated, low(w_outer)))
    return normalize(middle + ffn_result + bias_outer, gain_two, shift_two)

def adam_update(current, moment_one, moment_two, gradient):
    first_new = 0.9 * moment_one + 0.1 * gradient
    second_new = 0.999 * moment_two + 0.001 * gradient * gradient
    stepped = first_new / (1.0 - 0.9 ** STEP) / (jnp.sqrt(second_new / (1.0 - 0.999 ** STEP)) + 1e-08)
    return (first_new, second_new, current - 0.3 * stepped)

def reference(x_in, out_grad, item_lengths, weight_store, owner_perm, left_roots, right_roots, left_stats, right_stats, head_vectors, head_first, head_second, shared_vectors, shared_first, shared_second):
    indices = jnp.arange(BLK_MP, dtype=jnp.int32)
    inverse = lax.optimization_barrier(jnp.sum(jnp.where(owner_perm[:, :, None] == indices[None, None, :], indices[None, :, None], 0), axis=1)).astype(jnp.int32)
    natural = jnp.take_along_axis(weight_store, inverse[:, :, None, None], axis=1)
    panels = natural.reshape(MPW, CG, RG, BR, BC).transpose(0, 2, 3, 1, 4).reshape(MPW, D, C_MP)

    def columns(begin_at, width_of):
        return panels[:, :, begin_at:begin_at + width_of].transpose(1, 0, 2).reshape(D, MPW * width_of)
    w_query = columns(0, DL)
    w_key = columns(DL, DL)
    w_value = columns(2 * DL, DL)
    w_output = columns(3 * DL, DL).T
    w_inner = columns(4 * DL, FL)
    w_outer = columns(4 * DL + FL, FL).T
    bias_query = head_vectors[:, :DL].reshape(D)
    bias_value = head_vectors[:, DL:].reshape(D)
    bias_output = shared_vectors[0:D]
    bias_outer = shared_vectors[D:2 * D]
    gain_one = shared_vectors[2 * D:3 * D]
    shift_one = shared_vectors[3 * D:4 * D]
    gain_two = shared_vectors[4 * D:5 * D]
    shift_two = shared_vectors[5 * D:6 * D]
    bias_inner = shared_vectors[6 * D:]
    params = (w_query, w_key, w_value, w_output, w_inner, w_outer, bias_query, bias_value, bias_output, bias_outer, gain_one, shift_one, gain_two, shift_two, bias_inner)
    segments = segment_ids(item_lengths)
    rows_in = x_in.astype(jnp.float32).reshape(ROWS, SLOTS, D)
    saved_row = jax.checkpoint(layer_row)

    def forward(rows_now, weights_now):

        def mapped(paired):
            return saved_row(paired[0], paired[1], weights_now)
        return lax.map(mapped, (rows_now, segments))
    result, pullback = jax.vjp(forward, rows_in, params)
    rows_grad, param_grads = pullback(out_grad.astype(jnp.float32).reshape(ROWS, SLOTS, D))
    grad_query, grad_key, grad_value, grad_output, grad_inner, grad_outer, grad_bias_query, grad_bias_value, grad_bias_output, grad_bias_outer, grad_gain_one, grad_shift_one, grad_gain_two, grad_shift_two, grad_bias_inner = param_grads

    def split_cols(matrix, width_of):
        return matrix.reshape(D, MPW, width_of).transpose(1, 0, 2)
    grad_panel = jnp.concatenate([split_cols(grad_query, DL), split_cols(grad_key, DL), split_cols(grad_value, DL), split_cols(grad_output.T, DL), split_cols(grad_inner, FL), split_cols(grad_outer.T, FL)], axis=2)
    grad_natural = grad_panel.reshape(MPW, RG, BR, CG, BC).transpose(0, 3, 1, 2, 4).reshape(MPW, BLK_MP, BR, BC)
    block_grads = jnp.take_along_axis(grad_natural, owner_perm[:, :, None, None], axis=1)
    precise = lax.Precision.HIGHEST
    scaled_grads = block_grads * TOKENS ** (-0.5)
    new_left = 0.5 * left_stats + 0.5 * jnp.einsum('mbij,mbkj->mbik', scaled_grads, scaled_grads, precision=precise)
    new_right = 0.5 * right_stats + 0.5 * jnp.einsum('mbji,mbjk->mbik', scaled_grads, scaled_grads, precision=precise)
    direction = jnp.einsum('mbij,mbjk->mbik', left_roots, block_grads, precision=precise)
    direction = jnp.einsum('mbij,mbjk->mbik', direction, right_roots, precision=precise)
    weight_size = jnp.sqrt(lax.optimization_barrier(jnp.mean(weight_store * weight_store, axis=(2, 3), keepdims=True)) + 1e-06)
    step_size = jnp.sqrt(lax.optimization_barrier(jnp.mean(direction * direction, axis=(2, 3), keepdims=True)) + 1e-06)
    new_weights = weight_store - 0.3 * weight_size * direction / step_size
    head_grad = jnp.concatenate([grad_bias_query.reshape(MPW, DL), grad_bias_value.reshape(MPW, DL)], axis=1)
    shared_grad = jnp.concatenate([grad_bias_output, grad_bias_outer, grad_gain_one, grad_shift_one, grad_gain_two, grad_shift_two, grad_bias_inner])
    head_one, head_two, head_new = adam_update(head_vectors, head_first, head_second, head_grad)
    shared_one, shared_two, shared_new = adam_update(shared_vectors, shared_first, shared_second, shared_grad)
    return (result.reshape(TOKENS, D).astype(jnp.bfloat16), rows_grad.reshape(TOKENS, D), block_grads, new_left, new_right, new_weights, head_one, head_two, head_new, shared_one, shared_two, shared_new)
```

```python
from functools import partial

import jax
import jax.numpy as jnp
from jax import lax
from jax.experimental import pallas as pl
from jax.experimental.pallas import tpu as pltpu
from jax.sharding import PartitionSpec as P

DH = 64
SLOTS = 1024
STEP = 10
SHORT = 128
LONG = 512
EXTRA = 16
LOW = jnp.bfloat16
BOTH = ("dp", "mp")
ANY = pl.BlockSpec(memory_space=pl.ANY)
VMEM = pl.BlockSpec(memory_space=pltpu.VMEM)


def normalize_keep(inputs, gain, shift):
    center = inputs - jnp.mean(inputs, axis=-1, keepdims=True)
    spread = jnp.mean(center * center, axis=-1, keepdims=True)
    inverse = lax.rsqrt(spread + 1e-05)
    scaled = center * inverse
    return (scaled * gain + shift, scaled, inverse)


def normalize_back(upstream, scaled, inverse, gain):
    gained = upstream * gain
    result = inverse * (
        gained
        - jnp.mean(gained, axis=-1, keepdims=True)
        - scaled * jnp.mean(gained * scaled, axis=-1, keepdims=True)
    )
    return (result, jnp.sum(upstream * scaled, axis=0), jnp.sum(upstream, axis=0))


def product(left, right, left_dim, right_dim):
    return lax.dot_general(
        left, right, (((left_dim,), (right_dim,)), ((), ())), preferred_element_type=jnp.float32
    )


def adam_update(current, moment_one, moment_two, gradient):
    first_new = 0.9 * moment_one + 0.1 * gradient
    second_new = 0.999 * moment_two + 0.001 * gradient * gradient
    stepped = first_new / (1.0 - 0.9**STEP) / (jnp.sqrt(second_new / (1.0 - 0.999**STEP)) + 1e-08)
    return (first_new, second_new, current - 0.3 * stepped)


def gelu_pair(before):
    below = 0.5 + 0.5 * lax.erf(before * 0.5**0.5)
    slope = below + before * jnp.exp(before * before * -0.5) * 0.3989422804014327
    return before * below, slope


def attend_kernel(start_ref, length_ref, qkv_ref, ctx_ref, lse_ref):
    def item(begin, size):
        width = min(size, 256)
        keys = qkv_ref[1, :, pl.ds(begin, size)]
        values = qkv_ref[2, :, pl.ds(begin, size)]
        for at in range(0, size, width):
            here = pl.ds(begin + at, width)
            scores = product(keys, qkv_ref[0, :, here], 0, 0)
            top = jnp.max(scores, axis=0, keepdims=True)
            expo = jnp.exp(scores - top)
            total = jnp.sum(expo, axis=0, keepdims=True)
            ctx = product(values, expo.astype(LOW), 1, 0) / total
            ctx_ref[:, here] = ctx.astype(LOW)
            lse_ref[0, :, here] = top + jnp.log(total)

    each_item(start_ref, length_ref, item)


def each_item(start_ref, length_ref, item):
    @pl.loop(0, start_ref.shape[0])
    def _(i):
        begin = pl.multiple_of(start_ref[i], SHORT)

        @pl.when(length_ref[i] == LONG)
        def _():
            item(begin, LONG)

        @pl.when(length_ref[i] == SHORT)
        def _():
            item(begin, SHORT)


def attend_back_kernel(start_ref, length_ref, qkv_ref, ctx_ref, dctx_ref, lse_ref, out_ref):
    def item(begin, size):
        width = min(size, 256)
        keys = qkv_ref[1, :, pl.ds(begin, size)]
        values = qkv_ref[2, :, pl.ds(begin, size)]
        dkeys = jnp.zeros((DH, size), jnp.float32)
        dvalues = jnp.zeros((DH, size), jnp.float32)
        for at in range(0, size, width):
            here = pl.ds(begin + at, width)
            queries = qkv_ref[0, :, here]
            dctx = dctx_ref[:, here]
            probs = jnp.exp(product(keys, queries, 0, 0) - lse_ref[0, :, here])
            dprobs = product(values, dctx, 0, 0)
            delta = jnp.sum(
                dctx.astype(jnp.float32) * ctx_ref[:, here].astype(jnp.float32),
                axis=0,
                keepdims=True,
            )
            dscores = (probs * (dprobs - delta)).astype(LOW)
            out_ref[0, :, here] = (product(keys, dscores, 1, 0) * DH**-0.5).astype(LOW)
            dkeys += product(queries, dscores, 1, 1)
            dvalues += product(dctx, probs.astype(LOW), 1, 1)
        out_ref[1, :, pl.ds(begin, size)] = dkeys.astype(LOW)
        out_ref[2, :, pl.ds(begin, size)] = dvalues.astype(LOW)

    each_item(start_ref, length_ref, item)


def attend(starts, lengths, qkv):
    heads = qkv.shape[1] // DH
    return pl.pallas_call(
        attend_kernel,
        out_shape=(
            jax.ShapeDtypeStruct(qkv.shape[1:], LOW),
            jax.ShapeDtypeStruct((heads, 1, SLOTS), jnp.float32),
        ),
        grid_spec=pltpu.PrefetchScalarGridSpec(
            num_scalar_prefetch=2,
            grid=(heads,),
            in_specs=[pl.BlockSpec((3, DH, SLOTS), lambda h, *_: (0, h, 0))],
            out_specs=(
                pl.BlockSpec((DH, SLOTS), lambda h, *_: (h, 0)),
                pl.BlockSpec((1, 1, SLOTS), lambda h, *_: (h, 0, 0)),
            ),
        ),
        compiler_params=pltpu.CompilerParams(vmem_limit_bytes=32 * 2**20),
        cost_estimate=pl.CostEstimate(
            flops=heads * SLOTS * LONG * 1024, bytes_accessed=2**22, transcendentals=heads * 2**19
        ),
    )(starts, lengths, qkv)


def attend_back(starts, lengths, qkv, ctx, dctx, lse):
    heads = qkv.shape[1] // DH
    one = pl.BlockSpec((DH, SLOTS), lambda h, *_: (h, 0))
    three = pl.BlockSpec((3, DH, SLOTS), lambda h, *_: (0, h, 0))
    return pl.pallas_call(
        attend_back_kernel,
        out_shape=jax.ShapeDtypeStruct(qkv.shape, LOW),
        grid_spec=pltpu.PrefetchScalarGridSpec(
            num_scalar_prefetch=2,
            grid=(heads,),
            in_specs=[three, one, one, pl.BlockSpec((1, 1, SLOTS), lambda h, *_: (h, 0, 0))],
            out_specs=three,
        ),
        compiler_params=pltpu.CompilerParams(vmem_limit_bytes=32 * 2**20),
        cost_estimate=pl.CostEstimate(
            flops=heads * SLOTS * LONG * 2560, bytes_accessed=2**23, transcendentals=heads * 2**19
        ),
    )(starts, lengths, qkv, ctx, dctx, lse)


def tile_at(ref, place, groups):
    row = pl.multiple_of(lax.div(place, groups) * DH, DH)
    col = pl.multiple_of(lax.rem(place, groups) * 128, 128)
    return ref.at[pl.ds(row, DH), pl.ds(col, 128)]


def place_kernel(pieces, count, groups, chained, table_ref, *refs):
    sources = refs[:count]
    out_ref, sems = refs[count + chained], refs[count + chained + 1]
    for source, sem, parts in zip(sources, range(count), pieces):
        for row, entry, first, blocks in parts:

            @pl.loop(0, blocks)
            def _(j):
                pltpu.make_async_copy(
                    source.at[pl.ds(pl.multiple_of(row + j * DH, 16), DH), :],
                    tile_at(out_ref, table_ref[entry, first + j], groups),
                    sems.at[sem],
                ).start()

    for source, sem, parts in zip(sources, range(count), pieces):
        total = sum(part[3] for part in parts) * DH
        fits = total <= out_ref.shape[0]
        landed = out_ref.at[pl.ds(0, total), pl.ds(0, 128)] if fits else out_ref
        pltpu.make_async_copy(landed, landed, sems.at[sem]).wait()


def place(table, sources, pieces, shape, previous=None):
    chained = previous is not None
    operands = list(sources) + ([previous] if chained else [])
    return pl.pallas_call(
        partial(place_kernel, pieces, len(sources), shape[1] // 128, int(chained)),
        out_shape=jax.ShapeDtypeStruct(shape, LOW),
        grid_spec=pltpu.PrefetchScalarGridSpec(
            num_scalar_prefetch=1,
            grid=(),
            in_specs=[VMEM] * len(sources) + [ANY] * int(chained),
            out_specs=ANY,
            scratch_shapes=[pltpu.SemaphoreType.DMA((len(sources),))],
        ),
        compiler_params=pltpu.CompilerParams(vmem_limit_bytes=32 * 2**20),
        input_output_aliases={len(operands): 0} if chained else {},
    )(table, *operands)


def fetch_kernel(pieces, groups, table_ref, grad_ref, extra_ref, *refs):
    outs, sems = refs[: len(pieces)], refs[len(pieces)]
    for out, sem, parts in zip(outs, range(len(pieces)), pieces):
        for row, entry, first, blocks in parts:
            if blocks == 0:
                pltpu.make_async_copy(
                    extra_ref.at[entry], out.at[pl.ds(row, EXTRA), :], sems.at[sem]
                ).start()
                continue

            @pl.loop(0, blocks)
            def _(j):
                pltpu.make_async_copy(
                    tile_at(grad_ref, table_ref[entry, first + j], groups),
                    out.at[pl.ds(pl.multiple_of(row + j * DH, 16), DH), :],
                    sems.at[sem],
                ).start()

    for out, sem in zip(outs, range(len(pieces))):
        pltpu.make_async_copy(out, out, sems.at[sem]).wait()


def fetch(table, grad, extra, pieces):
    rows = [sum(part[3] * DH or EXTRA for part in parts) for parts in pieces]
    return pl.pallas_call(
        partial(fetch_kernel, pieces, grad.shape[1] // 128),
        out_shape=tuple(jax.ShapeDtypeStruct((n, 128), LOW) for n in rows),
        grid_spec=pltpu.PrefetchScalarGridSpec(
            num_scalar_prefetch=1,
            grid=(),
            in_specs=[ANY] * 2,
            out_specs=(VMEM,) * len(pieces),
            scratch_shapes=[pltpu.SemaphoreType.DMA((len(pieces),))],
        ),
        compiler_params=pltpu.CompilerParams(vmem_limit_bytes=32 * 2**20),
    )(table, grad, extra)


class Fabric:
    def __init__(self, sizes, row_ways):
        self.batch, self.model = sizes
        self.ways = row_ways
        self.panels = self.model // row_ways
        self.wide = row_ways == 2 and self.panels == 2 and self.batch % 2 == 0
        self.row_groups = [
            list(range(i, i + row_ways)) for i in range(0, self.model, row_ways)
        ]
        self.same_groups = [list(range(t, self.model, row_ways)) for t in range(row_ways)]

    def send(self, value, move):
        pairs = []
        for d in range(self.batch):
            for m in range(self.model):
                e, n = move(d, m)
                pairs.append((d * self.model + m, (e % self.batch) * self.model + n))
        return lax.ppermute(value, BOTH, pairs)

    def to_core(self, value):
        return self.send(value, lambda d, m: (d, m ^ 1))

    def to_x(self, value):
        return self.send(value, lambda d, m: (d, m ^ 2))

    def to_y(self, value):
        return self.send(value, lambda d, m: (d ^ 1, m))

    def to_z(self, value):
        return self.send(value, lambda d, m: (d + 2, m))

    def row_gather(self, own):
        if self.wide:
            other = self.to_core(own)
            first = lax.rem(lax.axis_index("mp"), 2) == 0
            return jnp.concatenate(
                [jnp.where(first, own, other), jnp.where(first, other, own)], axis=0
            )
        return lax.all_gather(own, "mp", axis=0, tiled=True, axis_index_groups=self.row_groups)

    def row_scatter(self, whole):
        rows = whole.shape[0] // self.ways
        if self.wide:
            core = lax.rem(lax.axis_index("mp"), 2)
            mine = lax.dynamic_slice_in_dim(whole, core * rows, rows, 0)
            theirs = lax.dynamic_slice_in_dim(whole, (1 - core) * rows, rows, 0)
            return mine.astype(jnp.float32) + self.to_core(theirs.astype(LOW)).astype(jnp.float32)
        return lax.psum_scatter(
            whole.astype(LOW),
            "mp",
            scatter_dimension=0,
            tiled=True,
            axis_index_groups=self.row_groups,
        ).astype(jnp.float32)

    def row_sum(self, value):
        if self.wide:
            return value + self.to_core(value)
        return lax.psum(value, "mp", axis_index_groups=self.row_groups)


def shards(
    sizes,
    x_in,
    out_grad,
    item_lengths,
    weight_store,
    owner_perm,
    left_roots,
    right_roots,
    left_stats,
    right_stats,
    head_vectors,
    head_first,
    head_second,
    shared_vectors,
    shared_first,
    shared_second,
):
    batch_ways, model_ways = sizes
    shard_rows, model_width = x_in.shape
    fabric = Fabric(sizes, SLOTS // shard_rows)
    ways, panels, wide = fabric.ways, fabric.panels, fabric.wide
    dp_at, mp_at = lax.axis_index("dp"), lax.axis_index("mp")
    row_at, place_at = lax.div(mp_at, ways), lax.rem(mp_at, ways)

    owned, row_block, col_block = weight_store.shape[1:]
    head_part, shared_part = head_vectors.shape[1], shared_vectors.shape[0]
    head_count, shared_count = head_part * batch_ways, shared_part * batch_ways * model_ways
    block_count = owner_perm.shape[1]
    row_groups = model_width // row_block
    head_width = model_width // model_ways
    ffn_total = shared_count - 6 * model_width
    ffn_width = ffn_total // model_ways
    heads64, ffn64 = head_width // DH, ffn_width // DH
    hidden_rows = panels * (4 * head_width + 2 * ffn_width)
    panel_shape = (hidden_rows, model_width)
    half_a = (owned // 2) * DH + EXTRA
    blocks_a, blocks_b = owned // 2, owned - owned // 2

    def two_parts(value):
        high = lax.reduce_precision(value, 8, 7)
        return jnp.concatenate([high.astype(LOW), (value - high).astype(LOW)])

    blocks_low = jnp.swapaxes(weight_store[0], 1, 2).astype(LOW).reshape(owned * DH, 128)
    vectors = jnp.concatenate([two_parts(head_vectors[0]), two_parts(shared_vectors)])
    vectors = jnp.pad(vectors, (0, EXTRA * 128 - vectors.shape[0])).reshape(EXTRA, 128)
    own = jnp.concatenate(
        [blocks_low[: blocks_a * DH], vectors, blocks_low[blocks_a * DH :]], axis=0
    )

    if wide:
        perm_two = jnp.concatenate([owner_perm, fabric.to_x(owner_perm)], axis=0)
    else:
        perm_two = lax.all_gather(
            owner_perm, "mp", axis=0, tiled=True, axis_index_groups=fabric.same_groups
        )

    def place_of(perm, panel):
        col, row = lax.div(perm, row_groups), lax.rem(perm, row_groups)
        in_ffn = col - 4 * heads64
        at_head = lax.div(col, heads64) * panels * heads64 + panel * heads64 + lax.rem(col, heads64)
        at_ffn = (
            (4 * heads64 + lax.div(in_ffn, ffn64) * ffn64) * panels
            + panel * ffn64
            + lax.rem(in_ffn, ffn64)
        )
        return jnp.where(in_ffn < 0, at_head, at_ffn) * row_groups + row

    if wide:
        panel_ids = jnp.array([0, 1], jnp.int32)[:, None]
        panel_ids = lax.rem(panel_ids + row_at, 2)
    else:
        panel_ids = jnp.arange(panels, dtype=jnp.int32)[:, None]
    places = place_of(perm_two, panel_ids).reshape(panels, batch_ways, owned)

    if wide:
        rings = batch_ways // 2
        z_at, y_at = lax.div(dp_at, 2), lax.rem(dp_at, 2)
        step = jnp.arange(rings, dtype=jnp.int32)
        face = jnp.arange(2, dtype=jnp.int32)

        def owner_table(sign):
            z_of = lax.rem(z_at + sign * step + rings, rings)
            dp_of = z_of[:, None] * 2 + lax.rem(y_at + face, 2)[None, :]
            chosen = jnp.take(places, dp_of.reshape(-1), axis=1)
            chosen = chosen.reshape(2, rings, 2, owned).transpose(1, 2, 0, 3)
            return chosen.reshape(rings * 4, owned), dp_of

        table, dp_of = owner_table(-1)
        weights = None
        extras = []
        ring = own
        for k in range(rings):
            if k:
                ring = fabric.to_z(ring)
            by_x, by_y = fabric.to_x(ring), fabric.to_y(ring)
            far_a, far_b = fabric.to_x(by_y[:half_a]), fabric.to_y(by_x[half_a:])
            low_half, high_half = (0, 0, blocks_a), (half_a, blocks_a, blocks_b)

            def piece(entry, *halves):
                return [(row, entry, first, count) for row, first, count in halves]

            both = (low_half, high_half)
            weights = place(
                table,
                [ring, by_x, by_y, far_a, far_b],
                [
                    piece(4 * k, *both),
                    piece(4 * k + 1, *both),
                    piece(4 * k + 2, *both),
                    piece(4 * k + 3, low_half),
                    piece(4 * k + 3, (0, blocks_a, blocks_b)),
                ],
                panel_shape,
                weights,
            )
            cut = slice(blocks_a * DH, half_a)
            extras += [ring[cut], by_x[cut], by_y[cut], far_a[cut]]
        extras = jnp.stack(extras).reshape(rings, 2, 2, EXTRA, 128)
        extras = jnp.take(extras, lax.rem(z_at - step + rings, rings), axis=0)
        extras = jnp.take(extras, lax.rem(y_at + face, 2), axis=1)
        extras = jnp.take(extras, lax.rem(row_at + face, 2), axis=2)
        extras = extras.reshape(batch_ways, 2, EXTRA, 128)
    else:
        gathered = lax.all_gather(own, "mp", axis=0, axis_index_groups=fabric.same_groups)
        gathered = lax.all_gather(gathered, "dp", axis=0)
        table = places.transpose(1, 0, 2).reshape(batch_ways * panels, owned)
        extras = gathered[:, :, blocks_a * DH : half_a]
        stride = own.shape[0]
        flat = gathered.reshape(-1, 128)
        pieces = []
        for i in range(batch_ways * panels):
            pieces += [(i * stride, i, 0, blocks_a), (i * stride + half_a, i, blocks_a, blocks_b)]
        weights = place(table, [flat], [pieces], panel_shape)

    extras = extras.reshape(batch_ways, panels, EXTRA * 128).astype(jnp.float32)
    head_all = extras[:, :, :head_part] + extras[:, :, head_part : 2 * head_part]
    begin = 2 * head_part
    shared_all = (
        extras[:, :, begin : begin + shared_part]
        + extras[:, :, begin + shared_part : begin + 2 * shared_part]
    )
    head_all = head_all.transpose(1, 0, 2).reshape(panels, head_count)
    if wide:
        shared_other = fabric.to_core(shared_all)
        first = place_at == 0
        shared = jnp.stack(
            [
                jnp.where(first, shared_all, shared_other),
                jnp.where(first, shared_other, shared_all),
            ],
            axis=2,
        )
    else:
        shared = lax.all_gather(
            shared_all, "mp", axis=0, axis_index_groups=fabric.row_groups
        ).transpose(1, 2, 0, 3)
    shared = shared.reshape(shared_count)

    q_rows, f_rows = panels * head_width, panels * ffn_width
    w_qkv = weights[: 3 * q_rows]
    w_out = weights[3 * q_rows : 4 * q_rows]
    w_one = weights[4 * q_rows : 4 * q_rows + f_rows]
    w_two = weights[4 * q_rows + f_rows :]
    bias_query = head_all[:, :head_width].reshape(q_rows)
    bias_value = head_all[:, head_width:].reshape(q_rows)
    bias_qkv = jnp.concatenate([bias_query, jnp.zeros((q_rows,), jnp.float32), bias_value])
    scale_qkv = jnp.concatenate(
        [jnp.full((q_rows,), DH**-0.5, jnp.float32), jnp.ones((2 * q_rows,), jnp.float32)]
    )
    bias_output, bias_outer, gain_one, shift_one, gain_two, shift_two = (
        shared[i * model_width : (i + 1) * model_width] for i in range(6)
    )
    bias_inner = shared[6 * model_width :].reshape(panels, ways, ffn_width)
    bias_local = lax.dynamic_index_in_dim(bias_inner, place_at, 1, keepdims=False).reshape(f_rows)

    lengths = lax.dynamic_index_in_dim(item_lengths, row_at, 0, keepdims=False)
    starts = jnp.cumsum(lengths) - lengths

    x_row = fabric.row_gather(x_in)
    qkv = product(w_qkv, x_row, 1, 1) + bias_qkv[:, None]
    qkv = (qkv.astype(LOW) * scale_qkv[:, None].astype(LOW)).reshape(3, q_rows, SLOTS)
    context, log_total = attend(starts, lengths, qkv)
    attended = fabric.row_scatter(product(context, w_out, 0, 0))
    hidden = x_in.astype(jnp.float32) + attended + bias_output
    middle, middle_scaled, middle_inverse = normalize_keep(hidden, gain_one, shift_one)
    middle_row = fabric.row_gather(middle.astype(LOW))
    activated, slope = gelu_pair(product(middle_row, w_one, 1, 1) + bias_local)
    activated, slope = activated.astype(LOW), slope.astype(LOW)
    ffn_result = fabric.row_scatter(product(activated, w_two, 1, 0))
    outer_sum = middle + ffn_result + bias_outer
    layer_value, out_scaled, out_inverse = normalize_keep(outer_sum, gain_two, shift_two)

    resid_grad, grad_gain_two, grad_shift_two = normalize_back(
        out_grad.astype(jnp.float32), out_scaled, out_inverse, gain_two
    )
    grad_bias_outer = jnp.sum(resid_grad, axis=0)
    resid_row = fabric.row_gather(resid_grad.astype(LOW))
    before_grad = (product(resid_row, w_two, 1, 1) * slope.astype(jnp.float32)).astype(LOW)
    grad_w_two = product(activated, resid_row, 0, 0).astype(LOW)
    grad_w_one = product(before_grad, middle_row, 0, 0).astype(LOW)
    grad_bias_inner = jnp.sum(before_grad.astype(jnp.float32), axis=0)
    middle_grad = resid_grad + fabric.row_scatter(product(before_grad, w_one, 1, 0))
    hidden_grad, grad_gain_one, grad_shift_one = normalize_back(
        middle_grad, middle_scaled, middle_inverse, gain_one
    )
    grad_bias_output = jnp.sum(hidden_grad, axis=0)
    hidden_row = fabric.row_gather(hidden_grad.astype(LOW))
    grad_w_out = product(context, hidden_row, 1, 0).astype(LOW)
    dcontext = product(w_out, hidden_row, 1, 1).astype(LOW)
    qkv_grad = attend_back(starts, lengths, qkv, context, dcontext, log_total)
    qkv_grad = qkv_grad.reshape(3 * q_rows, SLOTS)
    grad_w_qkv = product(qkv_grad, x_row, 1, 0).astype(LOW)
    input_grad = hidden_grad + fabric.row_scatter(product(qkv_grad, w_qkv, 0, 0))
    column_sums = jnp.sum(qkv_grad.astype(jnp.float32), axis=1)

    head_grad = jnp.concatenate(
        [
            column_sums[:q_rows].reshape(panels, head_width),
            column_sums[2 * q_rows :].reshape(panels, head_width),
        ],
        axis=1,
    )
    inner_all = lax.dynamic_update_slice(
        jnp.zeros((panels, ways, ffn_width), jnp.float32),
        grad_bias_inner.reshape(panels, 1, ffn_width),
        (0, place_at, 0),
    )
    shared_grad = fabric.row_sum(
        jnp.concatenate(
            [
                grad_bias_output,
                grad_bias_outer,
                grad_gain_one,
                grad_shift_one,
                grad_gain_two,
                grad_shift_two,
                inner_all.reshape(ffn_total),
            ]
        )
    )
    shared_grad = shared_grad.reshape(batch_ways, panels, ways, shared_part)
    shared_grad = lax.dynamic_index_in_dim(shared_grad, place_at, 2, keepdims=False)
    head_grad = head_grad.reshape(panels, batch_ways, head_part).transpose(1, 0, 2)
    extra_grad = jnp.concatenate([head_grad, shared_grad], axis=2).astype(LOW)
    extra_grad = jnp.pad(
        extra_grad, ((0, 0), (0, 0), (0, EXTRA * 128 - head_part - shared_part))
    ).reshape(batch_ways, panels, EXTRA, 128)
    grads = jnp.concatenate([grad_w_qkv, grad_w_out, grad_w_one, grad_w_two], axis=0)

    if wide:
        table, dp_of = owner_table(1)
        extra_grad = jnp.take(extra_grad, dp_of.reshape(-1), axis=0)
        extra_grad = jnp.take(extra_grad, lax.rem(row_at + face, 2), axis=1)
        extra_grad = extra_grad.reshape(rings * 4, EXTRA, 128)
        running = None
        wide_type = jnp.float32
        for k in range(rings - 1, -1, -1):

            def low_of(entries):
                parts = []
                for i, entry in enumerate(entries):
                    parts.append((i * half_a, 4 * k + entry, 0, blocks_a))
                    parts.append((i * half_a + blocks_a * DH, 4 * k + entry, 0, 0))
                return parts

            def high_of(entries):
                return [
                    (i * blocks_b * DH, 4 * k + entry, blocks_a, blocks_b)
                    for i, entry in enumerate(entries)
                ]

            send_x, send_y, keep_a, keep_b = fetch(
                table,
                grads,
                extra_grad,
                [low_of((1, 3)), high_of((2, 3)), low_of((0, 2)), high_of((0, 1))],
            )
            got_x, got_y = fabric.to_x(send_x), fabric.to_y(send_y)
            half_b = blocks_b * DH
            sum_a = keep_a.astype(wide_type) + got_x.astype(wide_type)
            sum_b = keep_b.astype(wide_type) + got_y.astype(wide_type)
            far_a = fabric.to_y(sum_a[half_a:].astype(LOW))
            far_b = fabric.to_x(sum_b[half_b:].astype(LOW))
            here = jnp.concatenate(
                [
                    sum_a[:half_a] + far_a.astype(wide_type),
                    sum_b[:half_b] + far_b.astype(wide_type),
                ],
                axis=0,
            )
            if running is not None:
                here = here + running.astype(wide_type)
            if k:
                running = fabric.to_z(here.astype(LOW))
        reduced = here
    else:
        pieces = []
        for i in range(batch_ways * panels):
            base = i * own.shape[0]
            pieces += [
                (base, i, 0, blocks_a),
                (base + blocks_a * DH, i, 0, 0),
                (base + half_a, i, blocks_a, blocks_b),
            ]
        (chunks,) = fetch(
            table, grads, extra_grad.reshape(batch_ways * panels, EXTRA, 128), [pieces]
        )
        chunks = chunks.reshape(batch_ways, panels, own.shape[0], 128)
        chunks = lax.psum_scatter(chunks, "dp", scatter_dimension=0, tiled=False)
        reduced = lax.psum_scatter(
            chunks,
            "mp",
            scatter_dimension=0,
            tiled=False,
            axis_index_groups=fabric.same_groups,
        ).astype(jnp.float32)

    block_grads = jnp.concatenate([reduced[: blocks_a * DH], reduced[half_a:]], axis=0)
    block_grads = block_grads.reshape(owned, DH, 128)
    vector_grads = reduced[blocks_a * DH : half_a].reshape(EXTRA * 128)
    head_grad_mine = vector_grads[:head_part]
    shared_grad_mine = vector_grads[head_part : head_part + shared_part]

    precise = lax.Precision.HIGHEST
    weights_here = jnp.swapaxes(weight_store[0], 1, 2)
    token_total = shard_rows * model_ways * batch_ways
    scaled_grads = block_grads * token_total ** (-0.5)
    new_left = 0.5 * left_stats[0] + 0.5 * jnp.einsum(
        "bji,bjk->bik", scaled_grads, scaled_grads, precision=precise
    )
    new_right = 0.5 * right_stats[0] + 0.5 * jnp.einsum(
        "bij,bkj->bik", scaled_grads, scaled_grads, precision=precise
    )
    direction = jnp.einsum("bkj,bij->bki", block_grads, left_roots[0], precision=precise)
    direction = jnp.einsum("bkl,bki->bli", right_roots[0], direction, precision=precise)
    weight_size = jnp.sqrt(
        jnp.mean(weights_here * weights_here, axis=(1, 2), keepdims=True) + 1e-06
    )
    step_size = jnp.sqrt(jnp.mean(direction * direction, axis=(1, 2), keepdims=True) + 1e-06)
    new_weights = weights_here - 0.3 * weight_size * direction / step_size
    head_one, head_two, head_new = adam_update(
        head_vectors[0], head_first[0], head_second[0], head_grad_mine
    )
    shared_one, shared_two, shared_new = adam_update(
        shared_vectors, shared_first, shared_second, shared_grad_mine
    )
    return (
        layer_value.astype(LOW),
        input_grad,
        jnp.swapaxes(block_grads, 1, 2)[None],
        new_left[None],
        new_right[None],
        jnp.swapaxes(new_weights, 1, 2)[None],
        head_one[None],
        head_two[None],
        head_new[None],
        shared_one,
        shared_two,
        shared_new,
    )


def solution(mesh):
    rows, blocks, vector, head = P(BOTH, None), P("mp", "dp", None, None), P(BOTH), P("mp", "dp")
    return jax.shard_map(
        partial(shards, (mesh.shape["dp"], mesh.shape["mp"])),
        mesh=mesh,
        in_specs=(rows, rows, P("dp", None), blocks, P("mp", None))
        + (blocks,) * 4
        + (head,) * 3
        + (vector,) * 3,
        out_specs=(rows, rows) + (blocks,) * 4 + (head,) * 3 + (vector,) * 3,
        check_vma=False,
    )
```

```python
from functools import partial

import jax
import jax.numpy as jnp
from jax import lax
from jax.experimental import pallas as pl
from jax.experimental.pallas import tpu as pltpu
from jax.sharding import PartitionSpec as P

DH = 64
SLOTS = 1024
STEP = 10
SHORT = 128
LONG = 512
EXTRA = 16
SCOPED = 14
LOW = jnp.bfloat16
BOTH = ("dp", "mp")
ANY = pl.BlockSpec(memory_space=pl.ANY)
VMEM = pl.BlockSpec(memory_space=pltpu.VMEM)
SMEM = pl.BlockSpec(memory_space=pltpu.SMEM)
FREE = pl.CostEstimate(flops=0, bytes_accessed=0, transcendentals=0)


def in_hbm(value):
    return pltpu.with_memory_space_constraint(value, pltpu.HBM)


def product(left, right, left_dim, right_dim):
    return lax.dot_general(
        left, right, (((left_dim,), (right_dim,)), ((), ())), preferred_element_type=jnp.float32
    )


def adam_update(current, moment_one, moment_two, gradient):
    first_new = 0.9 * moment_one + 0.1 * gradient
    second_new = 0.999 * moment_two + 0.001 * gradient * gradient
    stepped = first_new / (1.0 - 0.9**STEP) / (jnp.sqrt(second_new / (1.0 - 0.999**STEP)) + 1e-08)
    return (first_new, second_new, current - 0.3 * stepped)


def gelu_pair(before):
    below = 0.5 + 0.5 * lax.erf(before * 0.5**0.5)
    slope = below + before * jnp.exp(before * before * -0.5) * 0.3989422804014327
    return before * below, slope


def attend_kernel(start_ref, length_ref, qkv_ref, ctx_ref, lse_ref):
    def item(begin, size):
        here = pl.ds(begin, size)
        for g in range(lse_ref.shape[0]):
            head = pl.ds(g * DH, DH)
            scores = product(qkv_ref[1, head, here], qkv_ref[0, head, here], 0, 0)
            top = jnp.max(scores, axis=0, keepdims=True)
            expo = jnp.exp(scores - top)
            total = jnp.sum(expo, axis=0, keepdims=True)
            ctx = product(qkv_ref[2, head, here], expo.astype(LOW), 1, 0) / total
            ctx_ref[head, here] = ctx.astype(LOW)
            lse_ref[g, :, here] = top + jnp.log(total)

    each_item(start_ref, length_ref, item)


def each_item(start_ref, length_ref, item):
    @pl.loop(0, start_ref.shape[0])
    def _(i):
        begin = pl.multiple_of(start_ref[i], SHORT)

        @pl.when(length_ref[i] == LONG)
        def _():
            item(begin, LONG)

        @pl.when(length_ref[i] == SHORT)
        def _():
            item(begin, SHORT)


def attend_back_kernel(
    start_ref, length_ref, qkv_ref, ctx_ref, dctx_ref, lse_ref, out_ref
):
    def item(begin, size):
        here = pl.ds(begin, size)
        for g in range(lse_ref.shape[0]):
            head = pl.ds(g * DH, DH)
            queries, keys, values = (qkv_ref[i, head, here] for i in range(3))
            dctx = dctx_ref[head, here]
            probs = jnp.exp(product(keys, queries, 0, 0) - lse_ref[g, :, here])
            dprobs = product(values, dctx, 0, 0)
            delta = jnp.sum(
                dctx.astype(jnp.float32) * ctx_ref[head, here].astype(jnp.float32),
                axis=0,
                keepdims=True,
            )
            dscores = (probs * (dprobs - delta)).astype(LOW)
            out_ref[0, head, here] = (product(keys, dscores, 1, 0) * DH**-0.5).astype(LOW)
            out_ref[1, head, here] = product(queries, dscores, 1, 1).astype(LOW)
            out_ref[2, head, here] = product(dctx, probs.astype(LOW), 1, 1).astype(LOW)

    each_item(start_ref, length_ref, item)


def attend(starts, lengths, qkv):
    heads = qkv.shape[1] // DH
    group = min(heads, 2)
    return pl.pallas_call(
        attend_kernel,
        out_shape=(
            jax.ShapeDtypeStruct(qkv.shape[1:], LOW),
            jax.ShapeDtypeStruct((heads, 1, SLOTS), jnp.float32),
        ),
        grid_spec=pltpu.PrefetchScalarGridSpec(
            num_scalar_prefetch=2,
            grid=(heads // group,),
            in_specs=[pl.BlockSpec((3, group * DH, SLOTS), lambda h, *_: (0, h, 0))],
            out_specs=(
                pl.BlockSpec((group * DH, SLOTS), lambda h, *_: (h, 0)),
                pl.BlockSpec((group, 1, SLOTS), lambda h, *_: (h, 0, 0)),
            ),
        ),
        compiler_params=pltpu.CompilerParams(vmem_limit_bytes=12 * 2**20),
        cost_estimate=pl.CostEstimate(
            flops=heads * SLOTS * LONG * 1024, bytes_accessed=2**22, transcendentals=heads * 2**19
        ),
    )(starts, lengths, qkv)


def attend_back(starts, lengths, qkv, ctx, dctx, lse):
    heads = qkv.shape[1] // DH
    group = min(heads, 2)
    one = pl.BlockSpec((group * DH, SLOTS), lambda h, *_: (h, 0))
    three = pl.BlockSpec((3, group * DH, SLOTS), lambda h, *_: (0, h, 0))
    return pl.pallas_call(
        attend_back_kernel,
        out_shape=jax.ShapeDtypeStruct(qkv.shape, LOW),
        grid_spec=pltpu.PrefetchScalarGridSpec(
            num_scalar_prefetch=2,
            grid=(heads // group,),
            in_specs=[three, one, one, pl.BlockSpec((group, 1, SLOTS), lambda h, *_: (h, 0, 0))],
            out_specs=three,
        ),
        compiler_params=pltpu.CompilerParams(vmem_limit_bytes=14 * 2**20),
        cost_estimate=pl.CostEstimate(
            flops=heads * SLOTS * LONG * 2560, bytes_accessed=2**23, transcendentals=heads * 2**19
        ),
    )(starts, lengths, qkv, ctx, dctx, lse)


def tile_at(ref, place, groups):
    row = pl.multiple_of(lax.div(place, groups) * DH, DH)
    col = pl.multiple_of(lax.rem(place, groups) * 128, 128)
    return ref.at[pl.ds(row, DH), pl.ds(col, 128)]


def place_kernel(pieces, extra_rows, count, more, table_ref, *refs):
    sources = refs[:count]
    near_ref, ffn_ref, extra_ref, sems = refs[count + more :]
    groups = near_ref.shape[1] // 128
    bound = near_ref.shape[0] // DH * groups
    owned = table_ref.shape[1] - 16
    for i, (source, parts) in enumerate(zip(sources, pieces)):
        for row, entry, first, blocks in parts:

            @pl.loop(0, blocks)
            def _(j):
                at = table_ref[entry, first + j]
                block = source.at[pl.ds(pl.multiple_of(row + j * DH, 16), DH), :]

                @pl.when(at < bound)
                def _():
                    target = tile_at(near_ref, at, groups)
                    pltpu.make_async_copy(block, target, sems.at[i]).start()

                @pl.when(at >= bound)
                def _():
                    target = tile_at(ffn_ref, at - bound, groups)
                    pltpu.make_async_copy(block, target, sems.at[i]).start()

        if extra_rows[i] is not None:
            pltpu.make_async_copy(
                source.at[pl.ds(extra_rows[i], EXTRA), :],
                extra_ref.at[table_ref[parts[0][1], owned]],
                sems.at[count + i],
            ).start()

    for i, parts in enumerate(pieces):
        total = sum(part[3] for part in parts) * DH
        if total <= ffn_ref.shape[0]:
            landed = [ffn_ref.at[pl.ds(0, total), pl.ds(0, 128)]]
        else:
            landed = [near_ref, ffn_ref]
        for ref in landed:
            pltpu.make_async_copy(ref, ref, sems.at[i]).wait()
        if extra_rows[i] is not None:
            pltpu.make_async_copy(extra_ref.at[0], extra_ref.at[0], sems.at[count + i]).wait()


def place(table, sources, pieces, extra_rows, shapes, previous=None, deps=()):
    chained = previous is not None
    more = [in_hbm(v) for v in previous] if chained else []
    count = len(sources)
    return pl.pallas_call(
        partial(place_kernel, pieces, extra_rows, count, len(more) + len(deps)),
        out_shape=tuple(pltpu.HBM(shape, LOW) for shape in shapes)
        + (pltpu.HBM((table.shape[0], EXTRA, 128), LOW),),
        grid_spec=pltpu.PrefetchScalarGridSpec(
            num_scalar_prefetch=1,
            grid=(),
            in_specs=[VMEM] * count + [ANY] * (len(more) + len(deps)),
            out_specs=(ANY,) * 3,
            scratch_shapes=[pltpu.SemaphoreType.DMA((2 * count,))],
        ),
        cost_estimate=FREE,
        compiler_params=pltpu.CompilerParams(vmem_limit_bytes=12 * 2**20),
        input_output_aliases={1 + count + i: i for i in range(3)} if chained else {},
    )(table, *sources, *more, *deps)


def gate_kernel(*refs):
    pass


def gate(value, deps):
    return pl.pallas_call(
        gate_kernel,
        out_shape=jax.ShapeDtypeStruct(value.shape, value.dtype),
        in_specs=[ANY] * (1 + len(deps)),
        out_specs=ANY,
        cost_estimate=FREE,
        input_output_aliases={0: 0},
    )(value, *deps)


def halves_kernel(low, high, *refs):
    out_low, out_high = refs[-2:]
    out_low[...] = low[pl.ds(0, out_low.shape[0])]
    out_high[...] = high[pl.ds(low.shape[0] - out_high.shape[0], out_high.shape[0])]


def halves(low, high, rows, deps=()):
    rest = high.shape[0] - rows
    return pl.pallas_call(
        halves_kernel,
        out_shape=tuple(jax.ShapeDtypeStruct((n, 128), LOW) for n in (rows, rest)),
        in_specs=[VMEM] * 2 + [ANY] * len(deps),
        out_specs=(VMEM,) * 2,
        cost_estimate=FREE,
        compiler_params=pltpu.CompilerParams(vmem_limit_bytes=12 * 2**20),
    )(low, high, *deps)


def fetch_kernel(pieces, deps, table_ref, near_ref, ffn_ref, other_ref, zero_ref, extra_ref, *refs):
    count = len(pieces)
    outs, others, sems = refs[deps : deps + count], refs[deps + count : -1], refs[-1]
    groups = near_ref.shape[1] // 128
    bound = near_ref.shape[0] // DH * groups
    owned = table_ref.shape[1] - 16
    for i, parts in enumerate(pieces):
        for row, entry, first, blocks in parts:
            if blocks == 0:
                pltpu.make_async_copy(
                    extra_ref.at[table_ref[entry, owned]],
                    outs[i].at[pl.ds(row, EXTRA), :],
                    sems.at[i],
                ).start()
                continue

            @pl.loop(0, blocks)
            def _(j):
                at = table_ref[entry, first + j]
                here = pl.ds(pl.multiple_of(row + j * DH, 16), DH)

                def take(source, other):
                    pltpu.make_async_copy(source, outs[i].at[here, :], sems.at[i]).start()
                    pltpu.make_async_copy(
                        other, others[i].at[here, :], sems.at[count + i]
                    ).start()

                @pl.when(at < bound)
                def _():
                    take(tile_at(near_ref, at, groups), zero_ref)

                @pl.when(at >= bound)
                def _():
                    take(
                        tile_at(ffn_ref, at - bound, groups),
                        tile_at(other_ref, at - bound, groups),
                    )

    for i, parts in enumerate(pieces):
        pltpu.make_async_copy(outs[i], outs[i], sems.at[i]).wait()
        rows = sum(part[3] for part in parts) * DH
        landed = others[i].at[pl.ds(0, rows), :]
        pltpu.make_async_copy(landed, landed, sems.at[count + i]).wait()
        for row, _, _, blocks in parts:
            if blocks:
                here = pl.ds(row, blocks * DH)
                value = outs[i][here].astype(jnp.float32) + others[i][here].astype(jnp.float32)
                outs[i][here] = value.astype(LOW)


def fetch(table, grads, extra, pieces, deps=()):
    rows = [sum(part[3] * DH or EXTRA for part in parts) for parts in pieces]
    zero = jnp.zeros((DH, 128), LOW)
    return pl.pallas_call(
        partial(fetch_kernel, pieces, len(deps)),
        out_shape=tuple(jax.ShapeDtypeStruct((n, 128), LOW) for n in rows),
        grid_spec=pltpu.PrefetchScalarGridSpec(
            num_scalar_prefetch=1,
            grid=(),
            in_specs=[ANY] * (5 + len(deps)),
            out_specs=(VMEM,) * len(pieces),
            scratch_shapes=[pltpu.VMEM((n, 128), LOW) for n in rows]
            + [pltpu.SemaphoreType.DMA((2 * len(pieces),))],
        ),
        cost_estimate=FREE,
        compiler_params=pltpu.CompilerParams(vmem_limit_bytes=12 * 2**20),
    )(table, *[in_hbm(g) for g in grads], zero, extra, *deps)


def fetch_all_kernel(pieces, table_ref, grad_ref, extra_ref, out, sem):
    groups = grad_ref.shape[1] // 128
    owned = table_ref.shape[1] - 16
    for row, entry, first, blocks in pieces:
        if blocks == 0:
            pltpu.make_async_copy(
                extra_ref.at[table_ref[entry, owned]], out.at[pl.ds(row, EXTRA), :], sem.at[0]
            ).start()
            continue

        @pl.loop(0, blocks)
        def _(j):
            pltpu.make_async_copy(
                tile_at(grad_ref, table_ref[entry, first + j], groups),
                out.at[pl.ds(pl.multiple_of(row + j * DH, 16), DH), :],
                sem.at[0],
            ).start()

    pltpu.make_async_copy(out, out, sem.at[0]).wait()


def fetch_all(table, grad, extra, pieces):
    rows = sum(part[3] * DH or EXTRA for part in pieces)
    return pl.pallas_call(
        partial(fetch_all_kernel, pieces),
        out_shape=jax.ShapeDtypeStruct((rows, 128), LOW),
        grid_spec=pltpu.PrefetchScalarGridSpec(
            num_scalar_prefetch=1,
            grid=(),
            in_specs=[ANY] * 2,
            out_specs=VMEM,
            scratch_shapes=[pltpu.SemaphoreType.DMA((1,))],
        ),
        compiler_params=pltpu.CompilerParams(vmem_limit_bytes=16 * 2**20),
    )(table, in_hbm(grad), extra)


def turn_kernel(deps, keep_a, got_a, keep_b, got_b, *refs):
    for keep, got, out in zip((keep_a, keep_b), (got_a, got_b), refs[deps:]):
        there = pl.ds(out.shape[0], out.shape[0])
        out[...] = (keep[there].astype(jnp.float32) + got[there].astype(jnp.float32)).astype(LOW)


def turn(keep_a, got_a, keep_b, got_b, deps=()):
    return pl.pallas_call(
        partial(turn_kernel, len(deps)),
        out_shape=tuple(
            jax.ShapeDtypeStruct((keep.shape[0] // 2, 128), LOW) for keep in (keep_a, keep_b)
        ),
        in_specs=[VMEM] * 4 + [ANY] * len(deps),
        out_specs=(VMEM,) * 2,
        cost_estimate=FREE,
        compiler_params=pltpu.CompilerParams(vmem_limit_bytes=12 * 2**20),
    )(keep_a, got_a, keep_b, got_b, *deps)


def total_kernel(extra_at, chained, deps, *refs):
    running = refs[6] if chained else None
    outs = refs[6 + chained + deps :]
    start = 0
    for half, (keep, got, far) in enumerate((refs[:3], refs[3:6])):
        size = far.shape[0]
        pieces = [(0, size, outs[0], start)]
        if len(outs) == 2:
            pieces = [(0, size, outs[0], extra_at)]
            if half == 0:
                pieces = [(0, extra_at, outs[0], 0), (extra_at, size - extra_at, outs[1], 0)]
        for row, rows, out, to in pieces:
            here = pl.ds(row, rows)
            result = sum(ref[here].astype(jnp.float32) for ref in (keep, got, far))
            if chained:
                result = result + running[pl.ds(start + row, rows)].astype(jnp.float32)
            out[pl.ds(to, rows)] = result.astype(out.dtype)
        start += size


def total(half_a, half_b, running, last, deps=()):
    chain = [] if running is None else [running]
    rows_a, rows_b = half_a[2].shape[0], half_b[2].shape[0]
    shape = jax.ShapeDtypeStruct((rows_a + rows_b, 128), LOW)
    if last:
        shape = (
            jax.ShapeDtypeStruct((rows_a - EXTRA + rows_b, 128), jnp.float32),
            jax.ShapeDtypeStruct((EXTRA, 128), jnp.float32),
        )
    return pl.pallas_call(
        partial(total_kernel, rows_a - EXTRA, len(chain), len(deps)),
        out_shape=shape,
        in_specs=[VMEM] * (6 + len(chain)) + [ANY] * len(deps),
        out_specs=(VMEM, VMEM) if last else VMEM,
        cost_estimate=FREE,
        compiler_params=pltpu.CompilerParams(vmem_limit_bytes=12 * 2**20),
    )(*half_a, *half_b, *chain, *deps)


def divided(value, by):
    shift = by.bit_length() - 1
    assert by == 1 << shift
    return lax.shift_right_logical(value, jnp.full_like(value, shift)), value & (by - 1)


def places_of(perm, panel, panels, heads64, ffn64, row_groups):
    col, row = divided(perm, row_groups)
    in_ffn = jnp.maximum(col - 4 * heads64, 0)
    kind, at = divided(col, heads64)
    ffn_kind, ffn_at = divided(in_ffn, ffn64)
    at_head = (kind * panels + panel) * heads64 + at
    at_ffn = 4 * heads64 * panels + (ffn_kind * panels + panel) * ffn64 + ffn_at
    return jnp.where(col < 4 * heads64, at_head, at_ffn) * row_groups + row


def tables_kernel(rings, sizes, at_ref, own_ref, other_ref, come_ref, go_ref):
    z_at, y_at, x_at = at_ref[0], at_ref[1], at_ref[2]
    owned = own_ref.shape[1]
    for sign, out in ((-1, come_ref), (1, go_ref)):
        for k in range(rings):
            z = lax.rem(z_at + sign * k + rings, rings)
            for y in range(2):
                dp = z * 2 + (y_at ^ y)
                for x, perm in enumerate((own_ref, other_ref)):
                    panel = x_at ^ x
                    entry = 4 * k + 2 * y + x
                    out[pl.ds(entry, 1), :] = jnp.full((1, out.shape[1]), dp * 2 + panel, jnp.int32)
                    out[pl.ds(entry, 1), pl.ds(0, owned)] = places_of(
                        perm[pl.ds(dp, 1), :], panel, 2, *sizes
                    )


def tables(at, own, other, rings, sizes):
    shape = jax.ShapeDtypeStruct((rings * 4, own.shape[1] + 16), jnp.int32)
    return pl.pallas_call(
        partial(tables_kernel, rings, sizes),
        out_shape=(shape, shape),
        in_specs=[SMEM, VMEM, VMEM],
        out_specs=(VMEM, VMEM),
        cost_estimate=FREE,
    )(at, own, other)


class Rows:
    def __init__(self, source, target, sems, first=0):
        rows = min(source.shape[0], target.shape[0])
        self.chunk = rows // sems.shape[0]
        self.copies = []
        for i in range(sems.shape[0]):
            here = pl.ds(i * self.chunk, self.chunk)
            there = pl.ds(first + i * self.chunk, self.chunk)
            self.copies.append(pltpu.make_async_copy(source.at[there], target.at[here], sems.at[i]))
        self.done = 0

    def start(self):
        for copy in self.copies:
            copy.start()
        return self

    def upto(self, rows):
        while self.done * self.chunk < rows and self.done < len(self.copies):
            self.copies[self.done].wait()
            self.done += 1

    def whole(self):
        self.upto(self.chunk * len(self.copies))


class Stream:
    def __init__(self, chunks, buffer, sems):
        slots = buffer.shape[0]
        self.buffer = buffer
        self.copies = [
            pltpu.make_async_copy(chunk, buffer.at[i % slots], sems.at[i % slots])
            for i, chunk in enumerate(chunks)
        ]
        self.used = 0
        for copy in self.copies[:slots]:
            copy.start()

    def next(self):
        slots = self.buffer.shape[0]
        ahead = self.used - 1 + slots
        if self.used and ahead < len(self.copies):
            self.copies[ahead].start()
        self.copies[self.used].wait()
        self.used += 1
        return self.buffer.at[(self.used - 1) % slots]


def row_chunks(weight, row, rows, size):
    return [weight.at[pl.ds(row + at, size), :] for at in range(0, rows, size)]


def column_chunks(weight, row, rows, size):
    return [weight.at[pl.ds(row, rows), pl.ds(at, size)] for at in range(0, weight.shape[1], size)]


class Tiles:
    def __init__(self, buffer, sems):
        self.buffer, self.sems, self.under_way = buffer, sems, []

    def put(self, value, target):
        slot = len(self.under_way) % 2
        if len(self.under_way) >= 2:
            self.under_way[-2].wait()
        self.buffer[slot] = value
        copy = pltpu.make_async_copy(self.buffer.at[slot], target, self.sems.at[slot])
        copy.start()
        self.under_way.append(copy)

    def drain(self):
        for copy in self.under_way[-2:]:
            copy.wait()


def sems(n):
    return pltpu.SemaphoreType.DMA((n,))


def vmem(*shape, dtype=LOW):
    return pltpu.VMEM(shape, dtype)


def megabytes(n):
    return pltpu.CompilerParams(vmem_limit_bytes=n * 2**20)


def work(flops, moved=2**22, transcendentals=0):
    return pl.CostEstimate(flops=flops, bytes_accessed=moved, transcendentals=transcendentals)


def project_in_kernel(q_rows, weight, x, bias, out, w, w_sems):
    rows, tile = out.shape[0], w.shape[1]
    chunks = Stream(row_chunks(weight, 0, rows, tile), w, w_sems)
    for at in range(0, rows, tile):
        here = pl.ds(at, tile)
        value = product(chunks.next()[...], x[...], 1, 1) + jnp.transpose(bias[:, here])[:, :1]
        out[here, :] = (value * (DH**-0.5 if at < q_rows else 1.0)).astype(LOW)


def project_in(weights, x, bias):
    rows, width = bias.shape[1], weights.shape[1]
    return pl.pallas_call(
        partial(project_in_kernel, rows // 3),
        out_shape=jax.ShapeDtypeStruct((rows, x.shape[0]), LOW),
        in_specs=[ANY, VMEM, VMEM],
        out_specs=VMEM,
        scratch_shapes=[vmem(3, min(rows // 3, 256), width), sems(3)],
        compiler_params=megabytes(12),
        cost_estimate=work(2 * rows * x.shape[0] * x.shape[1]),
    )(in_hbm(weights), x, bias)


def project_kernel(row, where_ref, context, weight, mine, theirs, w, w_sems, tiles, tile_sems):
    loader = Rows(weight, w, w_sems, row).start()
    loader.whole()
    half = mine.shape[0]
    leaving = Tiles(tiles, tile_sems)
    for i, out in ((1, theirs), (0, mine)):
        at = pl.multiple_of((where_ref[0] ^ i) * half, half)
        leaving.put(product(context[:, pl.ds(at, half)], w[...], 0, 0).astype(LOW), out)
    leaving.drain()


def project(where, context, weights, row):
    features, tokens = context.shape
    width = weights.shape[1]
    out = pltpu.HBM((tokens // 2, width), LOW)
    return pl.pallas_call(
        partial(project_kernel, row),
        out_shape=(out, out),
        in_specs=[SMEM, VMEM, ANY],
        out_specs=(ANY, ANY),
        scratch_shapes=[
            vmem(features, width),
            sems(4),
            vmem(2, tokens // 2, width),
            sems(2),
        ],
        compiler_params=megabytes(14),
        cost_estimate=work(2 * features * tokens * width),
    )(where[None], context, in_hbm(weights))


def ffn_kernel(parts, row, *refs):
    inputs, (weight, bias), refs = refs[:parts], refs[parts : parts + 2], refs[parts + 2 :]
    values, slopes, outs = refs[:parts], refs[parts : 2 * parts], refs[2 * parts : 3 * parts]
    first, first_sems, second, second_sems = refs[3 * parts :]
    hidden, tile = bias.shape[1], first.shape[1]
    chunks = Stream(row_chunks(weight, row, hidden, tile), first, first_sems)
    columns = Stream(
        column_chunks(weight, row + hidden, hidden, second.shape[2]), second, second_sems
    )
    for at in range(0, hidden, tile):
        here = pl.ds(at, tile)
        w = chunks.next()
        for i, x in enumerate(inputs):
            before = product(x[...], w[...], 1, 1) + bias[:, here]
            result, derivative = gelu_pair(before)
            values[i][:, here] = result.astype(LOW)
            slopes[i][:, here] = derivative.astype(LOW)
    finish_ffn(columns, values, outs)


def finish_ffn(columns, values, outs):
    tile = columns.buffer.shape[2]
    for at in range(0, outs[0].shape[1], tile):
        w = columns.next()
        for value, out in zip(values, outs):
            out[:, pl.ds(at, tile)] = product(value[...], w[...], 1, 0).astype(LOW)


def ffn_shapes(parts, hidden, width):
    tokens = parts[0].shape[0]
    low = [jax.ShapeDtypeStruct((tokens, hidden), LOW)] * len(parts)
    outs = [jax.ShapeDtypeStruct((tokens, width), LOW)] * len(parts)
    scratch = [vmem(2, min(hidden, 512), width), sems(2), vmem(2, hidden, 256), sems(2)]
    return low, outs, scratch


def ffn(parts, weights, row, bias):
    hidden, width, n = bias.shape[1], weights.shape[1], len(parts)
    low, outs, scratch = ffn_shapes(parts, hidden, width)
    result = pl.pallas_call(
        partial(ffn_kernel, n, row),
        out_shape=tuple(low + low + outs),
        in_specs=[VMEM] * n + [ANY, VMEM],
        out_specs=(VMEM,) * (3 * n),
        scratch_shapes=scratch,
        compiler_params=megabytes(SCOPED),
        cost_estimate=work(4 * SLOTS * hidden * width, 2**24, SLOTS * hidden),
    )(*parts, in_hbm(weights), bias)
    return result[:n], result[n : 2 * n], result[2 * n :]


def ffn_back_kernel(parts, row, *refs):
    inputs, weight, slopes = refs[:parts], refs[parts], refs[parts + 1 : 2 * parts + 1]
    refs = refs[2 * parts + 1 :]
    grads, outs, sums = refs[:parts], refs[parts : 2 * parts], refs[2 * parts]
    first, first_sems, second, second_sems = refs[2 * parts + 1 :]
    hidden, tile = sums.shape[1], first.shape[1]
    chunks = Stream(row_chunks(weight, row + hidden, hidden, tile), first, first_sems)
    columns = Stream(column_chunks(weight, row, hidden, second.shape[2]), second, second_sems)
    for at in range(0, hidden, tile):
        here = pl.ds(at, tile)
        w = chunks.next()
        total = 0.0
        for x, slope, grad in zip(inputs, slopes, grads):
            result = product(x[...], w[...], 1, 1) * slope[:, here].astype(jnp.float32)
            grad[:, here] = result.astype(LOW)
            total = total + jnp.sum(result, axis=0, keepdims=True)
        sums[:, here] = jnp.broadcast_to(total, (sums.shape[0], tile))
    finish_ffn(columns, grads, outs)


def ffn_back(parts, weights, row, slopes):
    hidden, width, n = slopes[0].shape[1], weights.shape[1], len(parts)
    low, outs, scratch = ffn_shapes(parts, hidden, width)
    result = pl.pallas_call(
        partial(ffn_back_kernel, n, row),
        out_shape=tuple(low + outs) + (jax.ShapeDtypeStruct((8, hidden), jnp.float32),),
        in_specs=[VMEM] * n + [ANY] + [VMEM] * n,
        out_specs=(VMEM,) * (2 * n + 1),
        scratch_shapes=scratch,
        compiler_params=megabytes(SCOPED),
        cost_estimate=work(4 * SLOTS * hidden * width, 2**24),
    )(*parts, in_hbm(weights), *slopes)
    return result[:n], result[n : 2 * n], result[-1]


def ffn_grad_kernel(parts, row, *refs):
    values, upper, grads, lower = (refs[i * parts : (i + 1) * parts] for i in range(4))
    out, tiles, tile_sems = refs[4 * parts :]
    leaving = Tiles(tiles, tile_sems)
    hidden, tile = values[0].shape[1], tiles.shape[1]
    for lefts, rights, begin in ((values, upper, row + hidden), (grads, lower, row)):
        for at in range(0, hidden, tile):
            here = pl.ds(at, tile)
            value = sum(product(a[:, here], b[...], 0, 0) for a, b in zip(lefts, rights))
            leaving.put(value.astype(LOW), out.at[pl.ds(begin + at, tile), :])
    leaving.drain()


def ffn_grad(values, upper, grads, lower, shape, row):
    n, hidden, width = len(values), values[0].shape[1], shape[1]
    return pl.pallas_call(
        partial(ffn_grad_kernel, n, row),
        out_shape=pltpu.HBM(shape, LOW),
        in_specs=[VMEM] * (4 * n),
        out_specs=ANY,
        scratch_shapes=[vmem(2, min(hidden, 512), width), sems(2)],
        compiler_params=megabytes(SCOPED),
        cost_estimate=work(4 * SLOTS * hidden * width, 2**24),
    )(*values, *upper, *grads, *lower)


def project_back_kernel(
    row, where_ref, weight, context, own, other, out, grad, w, w_sems, b, sem
):
    Rows(weight, w, w_sems, row).start().whole()
    half = own.shape[0]
    columns = [pl.ds(pl.multiple_of((where_ref[0] ^ i) * half, half), half) for i in range(2)]
    b[...] = sum(
        product(context[:, at], part[...], 1, 0) for at, part in zip(columns, (own, other))
    ).astype(LOW)
    copy = pltpu.make_async_copy(b, grad.at[pl.ds(row, b.shape[0]), :], sem.at[0])
    copy.start()
    for at, part in zip(columns, (own, other)):
        out[:, at] = product(w[...], part[...], 1, 1).astype(LOW)
    copy.wait()


def project_back(where, weights, context, own, other, row):
    features, tokens = context.shape
    width = own.shape[1]
    return pl.pallas_call(
        partial(project_back_kernel, row),
        out_shape=(
            jax.ShapeDtypeStruct((features, tokens), LOW),
            pltpu.HBM(weights.shape, LOW),
        ),
        in_specs=[SMEM, ANY, VMEM, VMEM, VMEM],
        out_specs=(VMEM, ANY),
        scratch_shapes=[vmem(features, width), sems(4), vmem(features, width), sems(1)],
        compiler_params=megabytes(SCOPED),
        cost_estimate=work(4 * features * tokens * width),
    )(where[None], in_hbm(weights), context, own, other)


def last_grad_kernel(left, right, _, out, sums, tiles, tile_sems):
    leaving = Tiles(tiles, tile_sems)
    tile = tiles.shape[1]
    ones = jnp.ones((sums.shape[0], left.shape[1]), LOW)
    for at in range(0, left.shape[0], tile):
        here = pl.ds(at, tile)
        leaving.put(product(left[here, :], right[...], 1, 0).astype(LOW), out.at[here, :])
        sums[:, here] = product(ones, left[here, :], 1, 1)
    leaving.drain()


def last_grad(left, right, grads):
    rows, tokens = left.shape
    width = right.shape[1]
    tile = 512 if rows % 512 == 0 else rows // 3
    return pl.pallas_call(
        last_grad_kernel,
        out_shape=(pltpu.HBM(grads.shape, LOW), jax.ShapeDtypeStruct((8, rows), jnp.float32)),
        in_specs=[VMEM, VMEM, ANY],
        out_specs=(ANY, VMEM),
        scratch_shapes=[vmem(2, tile, width), sems(2)],
        compiler_params=megabytes(SCOPED),
        cost_estimate=work(2 * rows * tokens * width),
        input_output_aliases={2: 0},
    )(left, right, in_hbm(grads))


BIAS_OUTPUT, BIAS_OUTER, GAIN_ONE, SHIFT_ONE, GAIN_TWO, SHIFT_TWO = range(6)


def row_of(vectors, i):
    return vectors[pl.ds(i, 1), :]


def mean_of(value):
    return jnp.mean(value, axis=-1, keepdims=True)


def widened(here, *refs):
    return sum(ref[here, :].astype(jnp.float32) for ref in refs)


def norm_one_step(here, vectors, x, mine, got, middle, scaled, inverse):
    hidden = widened(here, x, mine, got) + row_of(vectors, BIAS_OUTPUT)
    center = hidden - mean_of(hidden)
    factor = lax.rsqrt(mean_of(center * center) + 1e-05)
    normal = center * factor
    middle[here, :] = (
        normal * row_of(vectors, GAIN_ONE) + row_of(vectors, SHIFT_ONE)
    ).astype(LOW)
    scaled[here, :] = normal.astype(LOW)
    inverse[here, :] = jnp.broadcast_to(factor, (factor.shape[0], 128))
    return ()


def back_through(upstream, normal, factor, gain):
    gained = upstream * gain
    return factor * (gained - mean_of(gained) - normal * mean_of(gained * normal))


def norm_two_step(here, vectors, middle, mine, got, upstream, layer, dz):
    outer = widened(here, middle, mine, got) + row_of(vectors, BIAS_OUTER)
    center = outer - mean_of(outer)
    factor = lax.rsqrt(mean_of(center * center) + 1e-05)
    normal = center * factor
    gain = row_of(vectors, GAIN_TWO)
    layer[here, :] = (normal * gain + row_of(vectors, SHIFT_TWO)).astype(LOW)
    dy = widened(here, upstream)
    result = back_through(dy, normal, factor, gain)
    dz[here, :] = result.astype(LOW)
    return (result, dy * normal, dy)


def norm_back_step(here, vectors, dz, mine, got, scaled, inverse, dhidden):
    dy = widened(here, dz, mine, got)
    normal = widened(here, scaled)
    factor = inverse[here, :][:, :1]
    result = back_through(dy, normal, factor, row_of(vectors, GAIN_ONE))
    dhidden[here, :] = result.astype(LOW)
    return (result, dy * normal, dy)


def layer_kernel(
    x, mine, got, upstream, vectors, bias, w_own, w_other,
    layer, dhidden, sums, inner, g_own, g_other,
    x_in, mine_in, got_in, up_in, in_sems, act, slope, mid, normal, inverse, dz, acc, out,
    out_sems, one, one_sems, two, two_sems, tile_one, tile_one_sems, tile_two, tile_two_sems,
):
    rows = x.shape[0]
    half, tile = w_own.shape[0] // 2, one.shape[1]
    ones = [c for w in (w_own, w_other) for c in row_chunks(w, 0, half, tile)]
    twos = [c for w in (w_own, w_other) for c in row_chunks(w, half, half, tile)]
    arriving = [
        Rows(source, target, in_sems.at[i])
        for i, (source, target) in enumerate(
            ((x, x_in), (mine, mine_in), (got, got_in), (upstream, up_in))
        )
    ]
    for copies in arriving[:3]:
        copies.start()
    first, second = Stream(ones + ones, one, one_sems), Stream(twos + twos, two, two_sems)
    arriving[3].start()
    step = arriving[0].chunk
    places = [pl.ds(at, step) for at in range(0, rows, step)]

    for n, here in enumerate(places):
        for copies in arriving[:3]:
            copies.upto(n * step + step)
        norm_one_step(here, vectors, x_in, mine_in, got_in, mid, normal, inverse)

    before = product(mid[...], first.next()[...], 1, 1) + bias[:, pl.ds(0, tile)]
    for n in range(len(ones)):
        columns = pl.ds(n * tile, tile)
        down_weight = second.next()
        if n + 1 < len(ones):
            up_weight = first.next()
            after = product(mid[...], up_weight[...], 1, 1) + bias[:, pl.ds((n + 1) * tile, tile)]
        value, derivative = gelu_pair(before)
        before = after
        value = value.astype(LOW)
        act[:, columns] = value
        slope[:, columns] = derivative.astype(LOW)
        part = product(value, down_weight[...], 1, 0)
        if n:
            acc[...] += part
        else:
            acc[...] = part

    arriving[3].whole()
    leaving, totals = [], []
    for n, here in enumerate(places):
        outer = acc[here, :] + widened(here, mid) + row_of(vectors, BIAS_OUTER)
        center = outer - mean_of(outer)
        factor = lax.rsqrt(mean_of(center * center) + 1e-05)
        scaled = center * factor
        gain = row_of(vectors, GAIN_TWO)
        out[here, :] = (scaled * gain + row_of(vectors, SHIFT_TWO)).astype(LOW)
        leaving.append(pltpu.make_async_copy(out.at[here], layer.at[here], out_sems.at[n]))
        leaving[-1].start()
        dy = widened(here, up_in)
        result = back_through(dy, scaled, factor, gain)
        acc[here, :] = result
        dz[here, :] = result.astype(LOW)
        totals.append([jnp.sum(v, axis=0, keepdims=True) for v in (result, dy * scaled, dy)])

    grads_one, grads_two = Tiles(tile_one, tile_one_sems), Tiles(tile_two, tile_two_sems)
    for n in range(len(ones)):
        columns = pl.ds(n * tile, tile)
        target, begin = (g_own, n * tile) if n * tile < half else (g_other, n * tile - half)
        value = product(act[:, columns], dz[...], 0, 0)
        grads_two.put(value.astype(LOW), target.at[pl.ds(half + begin, tile), :])
        grad = product(dz[...], second.next()[...], 1, 1) * slope[:, columns].astype(jnp.float32)
        inner[:, columns] = jnp.broadcast_to(
            jnp.sum(grad, axis=0, keepdims=True), (inner.shape[0], tile)
        )
        slope[:, columns] = grad.astype(LOW)
        value = product(slope[:, columns], mid[...], 0, 0)
        grads_one.put(value.astype(LOW), target.at[pl.ds(begin, tile), :])
        acc[...] += product(slope[:, columns], first.next()[...], 1, 0)

    for here in places:
        dy = acc[here, :]
        scaled = widened(here, normal)
        factor = inverse[here, :][:, :1]
        result = back_through(dy, scaled, factor, row_of(vectors, GAIN_ONE))
        dhidden[here, :] = result.astype(LOW)
        totals.append([jnp.sum(v, axis=0, keepdims=True) for v in (result, dy * scaled, dy)])
    count = len(places)
    lines = [sum(t[i] for t in part) for part in (totals[:count], totals[count:]) for i in range(3)]
    sums[...] = jnp.concatenate(lines + [jnp.zeros_like(lines[0])] * 2, axis=0)
    grads_one.drain()
    grads_two.drain()
    for copy in leaving:
        copy.wait()


def layer_part(x, mine, got, upstream, vectors, bias, w_own, w_other):
    rows, width = x.shape
    hidden = bias.shape[1]
    tile = 512
    low = jax.ShapeDtypeStruct((rows, width), LOW)
    grad = pltpu.HBM(w_own.shape, LOW)
    dma = pltpu.SemaphoreType.DMA
    return pl.pallas_call(
        layer_kernel,
        out_shape=(
            low,
            low,
            jax.ShapeDtypeStruct((8, width), jnp.float32),
            jax.ShapeDtypeStruct((8, hidden), jnp.float32),
            grad,
            grad,
        ),
        in_specs=[ANY] * 4 + [VMEM] * 2 + [ANY] * 2,
        out_specs=(ANY, VMEM, VMEM, VMEM, ANY, ANY),
        scratch_shapes=[vmem(rows, width) for _ in range(4)]
        + [
            dma((4, 4)),
            vmem(rows, hidden),
            vmem(rows, hidden),
            vmem(rows, width),
            vmem(rows, width),
            vmem(rows, 128, dtype=jnp.float32),
            vmem(rows, width),
            vmem(rows, width, dtype=jnp.float32),
            vmem(rows, width),
            sems(4),
            vmem(3, tile, width),
            sems(3),
            vmem(3, tile, width),
            sems(3),
            vmem(2, tile, width),
            sems(2),
            vmem(2, tile, width),
            sems(2),
        ],
        compiler_params=megabytes(46),
        cost_estimate=work(12 * rows * hidden * width, 2**25, rows * hidden),
    )(*[in_hbm(v) for v in (x, mine, got, upstream)], vectors, bias, in_hbm(w_own), in_hbm(w_other))


def rows_kernel(step, count, with_sums, vectors, *refs):
    inputs, outs = refs[:count], refs[count:]
    if with_sums:
        sums, outs = outs[-1], outs[:-1]
    rows = inputs[0].shape[0]
    tile = min(rows, 128)
    totals = 0
    for at in range(0, rows, tile):
        values = step(pl.ds(at, tile), vectors, *inputs, *outs)
        if with_sums:
            parts = [jnp.sum(value, axis=0, keepdims=True) for value in values]
            totals = totals + jnp.concatenate(parts + [jnp.zeros_like(parts[0])] * 5, axis=0)
    if with_sums:
        sums[...] = totals


def by_rows(step, inputs, vectors, outs, with_sums):
    rows, width = inputs[0].shape
    shapes = [jax.ShapeDtypeStruct((rows, n), dtype) for n, dtype in outs]
    if with_sums:
        shapes.append(jax.ShapeDtypeStruct((8, width), jnp.float32))
    return pl.pallas_call(
        partial(rows_kernel, step, len(inputs), with_sums),
        out_shape=tuple(shapes),
        in_specs=[VMEM] * (1 + len(inputs)),
        out_specs=(VMEM,) * len(shapes),
        compiler_params=megabytes(12),
        cost_estimate=work(40 * rows * width, 2**23, rows),
    )(vectors, *inputs)


def shampoo_kernel(scale, grad, left_root, right_root, left, right, weight, *outs):
    new_left, new_right, new_weight = outs
    for i in range(grad.shape[0]):
        g = grad[i].astype(LOW)
        new_left[i] = 0.5 * left[i] + (0.5 * scale) * product(g, g, 0, 0)
        new_right[i] = 0.5 * right[i] + (0.5 * scale) * product(g, g, 1, 1)
        step = product(g, left_root[i].astype(LOW), 1, 1)
        step = product(right_root[i].astype(LOW), step.astype(LOW), 0, 0)
        here = weight[i]
        size = jnp.sqrt(jnp.mean(here * here, keepdims=True) + 1e-06)
        norm = jnp.sqrt(jnp.mean(step * step, keepdims=True) + 1e-06)
        new_weight[i] = here - (0.3 * size / norm) * step


def shampoo(scale, grad, left_root, right_root, left, right, weight):
    owned = grad.shape[0]
    tile = 8 if owned % 8 == 0 else owned

    def spec(value):
        return pl.BlockSpec((tile,) + value.shape[1:], lambda i: (i, 0, 0))

    inputs = (grad, left_root, right_root, left, right, weight)
    return pl.pallas_call(
        partial(shampoo_kernel, scale),
        out_shape=tuple(
            jax.ShapeDtypeStruct(v.shape, jnp.float32) for v in (left, right, weight)
        ),
        grid=(owned // tile,),
        in_specs=[spec(v) for v in inputs],
        out_specs=tuple(spec(v) for v in (left, right, weight)),
        compiler_params=pltpu.CompilerParams(vmem_limit_bytes=12 * 2**20),
    )(*inputs)


class Fabric:
    def __init__(self, sizes, row_ways):
        self.batch, self.model = sizes
        self.ways = row_ways
        self.panels = self.model // row_ways
        self.wide = row_ways == 2 and self.panels == 2 and self.batch % 2 == 0
        self.row_groups = [
            list(range(i, i + row_ways)) for i in range(0, self.model, row_ways)
        ]
        self.same_groups = [list(range(t, self.model, row_ways)) for t in range(row_ways)]

    def send(self, value, move):
        pairs = []
        for d in range(self.batch):
            for m in range(self.model):
                e, n = move(d, m)
                pairs.append((d * self.model + m, (e % self.batch) * self.model + n))
        return lax.ppermute(value, BOTH, pairs)

    def to_core(self, value):
        return self.send(value, lambda d, m: (d, m ^ 1))

    def to_x(self, value):
        return self.send(value, lambda d, m: (d, m ^ 2))

    def to_y(self, value):
        return self.send(value, lambda d, m: (d ^ 1, m))

    def to_z(self, value):
        return self.send(value, lambda d, m: (d + 2, m))

    def row_gather(self, own):
        if self.wide:
            return self.join(self.share(own), 0)
        return lax.all_gather(own, "mp", axis=0, tiled=True, axis_index_groups=self.row_groups)

    def share(self, own):
        if self.wide:
            return [own, self.to_core(own)]
        return [self.row_gather(own)]

    def gather_back(self, parts):
        if self.wide:
            return parts[0].astype(LOW), self.to_core(parts[1].astype(LOW))
        mine = lax.psum_scatter(
            parts[0].astype(LOW),
            "mp",
            scatter_dimension=0,
            tiled=True,
            axis_index_groups=self.row_groups,
        )
        return mine, jnp.zeros(mine.shape, LOW)

    def cut(self, value, axis):
        if not self.wide:
            return [value]
        size = value.shape[axis] // 2
        core = lax.rem(lax.axis_index("mp"), 2)
        return [
            lax.dynamic_slice_in_dim(value, at * size, size, axis) for at in (core, 1 - core)
        ]

    def join(self, parts, axis):
        if not self.wide:
            return parts[0]
        own, other = parts
        first = lax.rem(lax.axis_index("mp"), 2) == 0
        return jnp.concatenate(
            [jnp.where(first, own, other), jnp.where(first, other, own)], axis=axis
        )

    def row_sum(self, value):
        if self.wide:
            return value + self.to_core(value)
        return lax.psum(value, "mp", axis_index_groups=self.row_groups)


def shards(
    sizes,
    x_in,
    out_grad,
    item_lengths,
    weight_store,
    owner_perm,
    left_roots,
    right_roots,
    left_stats,
    right_stats,
    head_vectors,
    head_first,
    head_second,
    shared_vectors,
    shared_first,
    shared_second,
):
    batch_ways, model_ways = sizes
    shard_rows, model_width = x_in.shape
    fabric = Fabric(sizes, SLOTS // shard_rows)
    ways, panels, wide = fabric.ways, fabric.panels, fabric.wide
    dp_at, mp_at = lax.axis_index("dp"), lax.axis_index("mp")
    row_at, place_at = lax.div(mp_at, ways), lax.rem(mp_at, ways)

    owned, row_block, col_block = weight_store.shape[1:]
    head_part, shared_part = head_vectors.shape[1], shared_vectors.shape[0]
    head_count, shared_count = head_part * batch_ways, shared_part * batch_ways * model_ways
    block_count = owner_perm.shape[1]
    row_groups = model_width // row_block
    head_width = model_width // model_ways
    ffn_total = shared_count - 6 * model_width
    ffn_width = ffn_total // model_ways
    heads64, ffn64 = head_width // DH, ffn_width // DH
    hidden_rows = panels * (4 * head_width + 2 * ffn_width)
    q_rows, f_rows = panels * head_width, panels * ffn_width
    panel_shape = (hidden_rows, model_width)
    panel_shapes = ((4 * q_rows, model_width), (2 * f_rows, model_width))
    half_a = (owned // 2) * DH + EXTRA
    blocks_a, blocks_b = owned // 2, owned - owned // 2

    def two_parts(value):
        high = lax.reduce_precision(value, 8, 7)
        return jnp.concatenate([high.astype(LOW), (value - high).astype(LOW)])

    blocks_low = jnp.swapaxes(weight_store[0], 1, 2).astype(LOW).reshape(owned * DH, 128)
    vectors = jnp.concatenate([two_parts(head_vectors[0]), two_parts(shared_vectors)])
    vectors = jnp.pad(vectors, (0, EXTRA * 128 - vectors.shape[0])).reshape(EXTRA, 128)
    own = jnp.concatenate(
        [blocks_low[: blocks_a * DH], vectors, blocks_low[blocks_a * DH :]], axis=0
    )

    layout = (heads64, ffn64, row_groups)
    perm = owner_perm.reshape(batch_ways, owned)
    if wide:
        perm_other = fabric.to_x(perm)
    else:
        perm_all = lax.all_gather(perm, "mp", axis=0, axis_index_groups=fabric.same_groups)
        panel_ids = jnp.arange(panels, dtype=jnp.int32)[:, None, None]
        places = places_of(perm_all, panel_ids, panels, *layout)

    if wide:
        rings = batch_ways // 2
        z_at, y_at = lax.div(dp_at, 2), lax.rem(dp_at, 2)
        table, table_back = tables(
            jnp.stack([z_at, y_at, row_at]), perm, perm_other, rings, layout
        )
        low_half, high_half = (0, 0, blocks_a), (half_a, blocks_a, blocks_b)
        at_extra = blocks_a * DH

        def piece(entry, *halves):
            return [(row, entry, first, count) for row, first, count in halves]

        def near_of(k):
            return [
                (value, piece(4 * k + i, low_half, high_half), at_extra)
                for i, value in enumerate((ring, by_x, by_y))
            ]

        def far_of(k):
            return [
                (far_a[k], piece(4 * k + 3, low_half), at_extra),
                (far_b[k], piece(4 * k + 3, (0, blocks_a, blocks_b)), None),
            ]

        placed, near, far_a, far_b = None, [], [], []
        ring = own
        for k in range(rings):
            if k:
                deps = [table] if k == 1 else [far_a[k - 2], far_b[k - 2]]
                ring = gate(after, deps + ([placed[2]] if placed else []))
            after = fabric.to_z(ring) if k + 1 < rings else None
            by_x, by_y = fabric.to_x(ring), fabric.to_y(ring)
            if k:
                low, high = halves(*last, half_a, [ring])
                far_a.append(fabric.to_x(low))
                far_b.append(fabric.to_y(high))
                parts = near + (far_of(k - 2) if k > 1 else [])
                placed = place(table, *zip(*parts), panel_shapes, placed, [low])
            near, last = near_of(k), (by_y, by_x)
        low, high = halves(*last, half_a, [far_a[-1], far_b[-1]])
        far_a.append(fabric.to_x(low))
        far_b.append(fabric.to_y(high))
        placed = place(table, *zip(*(near + far_of(rings - 2))), panel_shapes, placed, [low])
        w_near, w_ffn, extras = place(table, *zip(*far_of(rings - 1)), panel_shapes, placed)
        extras = extras.astype(jnp.float32)
    else:
        gathered = lax.all_gather(own, "mp", axis=0, axis_index_groups=fabric.same_groups)
        gathered = lax.all_gather(gathered, "dp", axis=0)
        entries = batch_ways * panels
        table = places.transpose(1, 0, 2).reshape(entries, owned)
        index = jnp.arange(entries, dtype=jnp.int32)[:, None]
        table = jnp.concatenate([table, jnp.broadcast_to(index, (entries, 16))], axis=1)
        extras = gathered[:, :, blocks_a * DH : half_a].astype(jnp.float32)
        stride = own.shape[0]
        flat = gathered.reshape(-1, 128)
        pieces = []
        for i in range(batch_ways * panels):
            pieces += [(i * stride, i, 0, blocks_a), (i * stride + half_a, i, blocks_a, blocks_b)]
        w_near, w_ffn, _ = place(table, [flat], [pieces], [None], panel_shapes)
        weights = jnp.concatenate([w_near, w_ffn], axis=0)

    extras = extras.reshape(batch_ways, panels, EXTRA * 128)
    head_all = extras[:, :, :head_part] + extras[:, :, head_part : 2 * head_part]
    begin = 2 * head_part
    shared_all = (
        extras[:, :, begin : begin + shared_part]
        + extras[:, :, begin + shared_part : begin + 2 * shared_part]
    )
    head_all = head_all.transpose(1, 0, 2).reshape(panels, head_count)
    if wide:
        shared_other = fabric.to_core(shared_all)
        first = place_at == 0
        shared = jnp.stack(
            [
                jnp.where(first, shared_all, shared_other),
                jnp.where(first, shared_other, shared_all),
            ],
            axis=2,
        )
    else:
        shared = lax.all_gather(
            shared_all, "mp", axis=0, axis_index_groups=fabric.row_groups
        ).transpose(1, 2, 0, 3)
    shared = shared.reshape(shared_count)

    bias_query = head_all[:, :head_width].reshape(q_rows)
    bias_value = head_all[:, head_width:].reshape(q_rows)
    bias_qkv = jnp.concatenate([bias_query, jnp.zeros((q_rows,), jnp.float32), bias_value])
    vectors = jnp.pad(shared[: 6 * model_width].reshape(6, model_width), ((0, 2), (0, 0)))
    bias_inner = shared[6 * model_width :].reshape(panels, ways, ffn_width)
    bias_local = lax.dynamic_index_in_dim(bias_inner, place_at, 1, keepdims=False).reshape(f_rows)
    if wide:
        bias_other = lax.dynamic_index_in_dim(bias_inner, 1 - place_at, 1, keepdims=False)
        bias_both = jnp.concatenate([bias_local, bias_other.reshape(f_rows)])

    lengths = lax.dynamic_index_in_dim(item_lengths, row_at, 0, keepdims=False)
    starts = jnp.cumsum(lengths) - lengths

    x_row = fabric.row_gather(x_in)
    bias_qkv = jnp.broadcast_to(bias_qkv[None], (8, 3 * q_rows))
    qkv = project_in(w_near, x_row, bias_qkv).reshape(3, q_rows, SLOTS)
    context, log_total = attend(starts, lengths, qkv)
    if wide:
        w_ffn = gate(w_ffn, [x_row])
        w_ffn_other = fabric.to_core(w_ffn)
        mine, got = fabric.gather_back(project(place_at, context, w_near, 3 * q_rows))
        layer_value, hidden_grad, sums, inner_sums, grad_ffn, grad_ffn_other = layer_part(
            x_in, mine, got, out_grad, vectors, bias_both[None], w_ffn, w_ffn_other
        )
        hidden_parts = fabric.share(hidden_grad)
        grad_ffn_got = fabric.to_core(gate(grad_ffn_other, [hidden_parts[1]]))
        dcontext, grad_near = project_back(
            place_at, w_near, context, *hidden_parts, 3 * q_rows
        )
        inner = [
            part.reshape(panels, ffn_width) for part in (inner_sums[0, :f_rows], inner_sums[0, f_rows:])
        ]
        inner_all = jnp.where(
            place_at == 0, jnp.stack(inner, axis=1), jnp.stack(inner[::-1], axis=1)
        )
    else:
        w_out, w_qkv = w_near[3 * q_rows :], w_near[: 3 * q_rows]
        mine, got = fabric.gather_back([product(context, w_out, 0, 0)])
        low = (model_width, LOW)
        middle, middle_scaled, middle_inverse = by_rows(
            norm_one_step, (x_in, mine, got), vectors, (low, low, (128, jnp.float32)), False
        )
        middle_parts = fabric.share(middle)
        activated, slopes, results = ffn(middle_parts, weights, 4 * q_rows, bias_local[None])
        mine, got = fabric.gather_back(results)
        layer_value, resid_grad, sums_two = by_rows(
            norm_two_step, (middle, mine, got, out_grad), vectors, (low, low), True
        )
        resid_parts = fabric.share(resid_grad)
        before_grads, results, inner_sums = ffn_back(resid_parts, weights, 4 * q_rows, slopes)
        mine, got = fabric.gather_back(results)
        hidden_grad, sums_one = by_rows(
            norm_back_step,
            (resid_grad, mine, got, middle_scaled, middle_inverse),
            vectors,
            (low,),
            True,
        )
        grads = ffn_grad(
            activated, resid_parts, before_grads, middle_parts, panel_shape, 4 * q_rows
        )
        hidden_parts = fabric.share(hidden_grad)
        dcontext = product(w_out, hidden_parts[0], 1, 1).astype(LOW)
        part = product(context, hidden_parts[0], 1, 0).astype(LOW)
        grad_near = lax.dynamic_update_slice_in_dim(grads, part, 3 * q_rows, 0)
        sums = jnp.concatenate([sums_two[:3], sums_one[:3]], axis=0)
        inner_all = lax.dynamic_update_slice(
            jnp.zeros((panels, ways, ffn_width), jnp.float32),
            inner_sums[0].reshape(panels, 1, ffn_width),
            (0, place_at, 0),
        )
    qkv_grad = attend_back(starts, lengths, qkv, context, dcontext, log_total)
    qkv_grad = qkv_grad.reshape(3 * q_rows, SLOTS)
    grad_near, column_sums = last_grad(qkv_grad, x_row, grad_near)
    if wide:
        mine, got = fabric.gather_back(project(place_at, qkv_grad, w_near, 0))
    else:
        mine, got = fabric.gather_back([product(qkv_grad, w_qkv, 0, 0)])
    input_grad = sum(v.astype(jnp.float32) for v in (hidden_grad, mine, got))
    column_sums = column_sums[0]

    head_grad = jnp.concatenate(
        [
            column_sums[:q_rows].reshape(panels, head_width),
            column_sums[2 * q_rows :].reshape(panels, head_width),
        ],
        axis=1,
    )
    shared_grad = jnp.concatenate(
        [sums[i] for i in (3, 0, 4, 5, 1, 2)] + [inner_all.reshape(ffn_total)]
    )
    if wide:
        shared_grad = gate(shared_grad, [qkv_grad])
    shared_grad = fabric.row_sum(shared_grad)
    shared_grad = shared_grad.reshape(batch_ways, panels, ways, shared_part)
    shared_grad = lax.dynamic_index_in_dim(shared_grad, place_at, 2, keepdims=False)
    head_grad = head_grad.reshape(panels, batch_ways, head_part).transpose(1, 0, 2)
    extra_grad = jnp.concatenate([head_grad, shared_grad], axis=2).astype(LOW)
    extra_grad = jnp.pad(
        extra_grad, ((0, 0), (0, 0), (0, EXTRA * 128 - head_part - shared_part))
    ).reshape(batch_ways * panels, EXTRA, 128)

    if wide:
        half_b = blocks_b * DH

        def low_of(k, entries):
            parts = []
            for i, entry in enumerate(entries):
                parts.append((i * half_a, 4 * k + entry, 0, blocks_a))
                parts.append((i * half_a + blocks_a * DH, 4 * k + entry, 0, 0))
            return parts

        def high_of(k, entries):
            return [
                (i * half_b, 4 * k + entry, blocks_a, blocks_b) for i, entry in enumerate(entries)
            ]

        sent, kept, far, order = {}, {}, {}, []

        def gather(pieces):
            result = fetch(table_back, (grad_near, grad_ffn, grad_ffn_got), extra_grad, pieces, order)
            order[:] = [result[0]]
            return result

        def send(k):
            send_x, send_y = gather([low_of(k, (1, 3)), high_of(k, (2, 3))])
            sent[k] = fabric.to_x(send_x), fabric.to_y(send_y)

        def keep(k):
            kept[k] = gather([low_of(k, (0, 2)), high_of(k, (0, 1))])

        def pass_on(k):
            sum_a, sum_b = turn(kept[k][0], sent[k][0], kept[k][1], sent[k][1], order)
            far[k] = fabric.to_y(sum_a), fabric.to_x(sum_b)
            order[:] = [sum_a]

        def finish(k, running):
            half = [(kept[k][i], sent[k][i], far[k][i]) for i in range(2)]
            result = total(*half, running, k == 0, order)
            if k == 0:
                return result
            order[:] = [result]
            return fabric.to_z(result)

        last = rings - 1
        for k in (last, last - 1):
            send(k)
        for k in (last, last - 1):
            keep(k)
        for k in (last, last - 1):
            pass_on(k)
        if last > 1:
            send(last - 2)
            keep(last - 2)
        running = finish(last, None)
        for k in range(last - 2, -1, -1):
            pass_on(k)
            if k:
                send(k - 1)
                keep(k - 1)
            running = finish(k + 1, running)
        running = finish(0, running)
        block_grads, vector_grads = running
    else:
        pieces = []
        for i in range(batch_ways * panels):
            base = i * own.shape[0]
            pieces += [
                (base, i, 0, blocks_a),
                (base + blocks_a * DH, i, 0, 0),
                (base + half_a, i, blocks_a, blocks_b),
            ]
        chunks = fetch_all(table, grad_near, extra_grad, pieces)
        chunks = chunks.reshape(batch_ways, panels, own.shape[0], 128)
        chunks = lax.psum_scatter(chunks, "dp", scatter_dimension=0, tiled=False)
        reduced = lax.psum_scatter(
            chunks,
            "mp",
            scatter_dimension=0,
            tiled=False,
            axis_index_groups=fabric.same_groups,
        ).astype(jnp.float32)

        block_grads = jnp.concatenate([reduced[: blocks_a * DH], reduced[half_a:]], axis=0)
        vector_grads = reduced[blocks_a * DH : half_a]

    block_grads = block_grads.reshape(owned, DH, 128)
    vector_grads = vector_grads.reshape(EXTRA * 128)
    head_grad_mine = vector_grads[:head_part]
    shared_grad_mine = vector_grads[head_part : head_part + shared_part]

    token_total = shard_rows * model_ways * batch_ways
    new_left, new_right, new_weights = shampoo(
        1.0 / token_total,
        block_grads,
        left_roots[0],
        right_roots[0],
        left_stats[0],
        right_stats[0],
        jnp.swapaxes(weight_store[0], 1, 2),
    )
    head_one, head_two, head_new = adam_update(
        head_vectors[0], head_first[0], head_second[0], head_grad_mine
    )
    shared_one, shared_two, shared_new = adam_update(
        shared_vectors, shared_first, shared_second, shared_grad_mine
    )
    return (
        layer_value,
        input_grad,
        jnp.swapaxes(block_grads, 1, 2)[None],
        new_left[None],
        new_right[None],
        jnp.swapaxes(new_weights, 1, 2)[None],
        head_one[None],
        head_two[None],
        head_new[None],
        shared_one,
        shared_two,
        shared_new,
    )


def solution(mesh):
    rows, blocks, vector, head = P(BOTH, None), P("mp", "dp", None, None), P(BOTH), P("mp", "dp")
    return jax.shard_map(
        partial(shards, (mesh.shape["dp"], mesh.shape["mp"])),
        mesh=mesh,
        in_specs=(rows, rows, P("dp", None), blocks, P("mp", None))
        + (blocks,) * 4
        + (head,) * 3
        + (vector,) * 3,
        out_specs=(rows, rows) + (blocks,) * 4 + (head,) * 3 + (vector,) * 3,
        check_vma=False,
    )
```

```python
from functools import partial

import jax
import jax.numpy as jnp
from jax import lax
from jax.experimental import pallas as pl
from jax.experimental.pallas import tpu as pltpu
from jax.sharding import PartitionSpec as P

DH = 64
SLOTS = 1024
STEP = 10
SHORT = 128
LONG = 512
EXTRA = 16
SCOPED = 14
LOW = jnp.bfloat16
BOTH = ("dp", "mp")
ANY = pl.BlockSpec(memory_space=pl.ANY)
VMEM = pl.BlockSpec(memory_space=pltpu.VMEM)
SMEM = pl.BlockSpec(memory_space=pltpu.SMEM)
FREE = pl.CostEstimate(flops=0, bytes_accessed=0, transcendentals=0)
MOVE = pl.CostEstimate(flops=0, bytes_accessed=2**24, transcendentals=0)


def sems(n):
    return pltpu.SemaphoreType.DMA((n,))


def in_hbm(value):
    return pltpu.with_memory_space_constraint(value, pltpu.HBM)


def product(left, right, left_dim, right_dim):
    return lax.dot_general(
        left, right, (((left_dim,), (right_dim,)), ((), ())), preferred_element_type=jnp.float32
    )


def adam_update(current, moment_one, moment_two, gradient):
    first_new = 0.9 * moment_one + 0.1 * gradient
    second_new = 0.999 * moment_two + 0.001 * gradient * gradient
    stepped = first_new / (1.0 - 0.9**STEP) / (jnp.sqrt(second_new / (1.0 - 0.999**STEP)) + 1e-08)
    return (first_new, second_new, current - 0.3 * stepped)


def gelu_pair(before):
    below = 0.5 + 0.5 * lax.erf(before * 0.5**0.5)
    slope = below + before * jnp.exp(before * before * -0.5) * 0.3989422804014327
    return before * below, slope


def attend_kernel(start_ref, length_ref, qkv_ref, ctx_ref, lse_ref):
    def item(begin, size):
        here = pl.ds(begin, size)
        for g in range(lse_ref.shape[0]):
            head = pl.ds(g * DH, DH)
            scores = product(qkv_ref[1, head, here], qkv_ref[0, head, here], 0, 0)
            top = jnp.max(scores, axis=0, keepdims=True)
            expo = jnp.exp(scores - top)
            total = jnp.sum(expo, axis=0, keepdims=True)
            ctx = product(qkv_ref[2, head, here], expo.astype(LOW), 1, 0) / total
            ctx_ref[head, here] = ctx.astype(LOW)
            lse_ref[g, :, here] = top + jnp.log(total)

    each_item(start_ref, length_ref, item)


def each_item(start_ref, length_ref, item):
    @pl.loop(0, start_ref.shape[0])
    def _(i):
        begin = pl.multiple_of(start_ref[i], SHORT)

        @pl.when(length_ref[i] == LONG)
        def _():
            item(begin, LONG)

        @pl.when(length_ref[i] == SHORT)
        def _():
            item(begin, SHORT)


def attend_back_kernel(
    start_ref, length_ref, qkv_ref, ctx_ref, dctx_ref, lse_ref, out_ref
):
    def item(begin, size):
        here = pl.ds(begin, size)
        for g in range(lse_ref.shape[0]):
            head = pl.ds(g * DH, DH)
            queries, keys, values = (qkv_ref[i, head, here] for i in range(3))
            dctx = dctx_ref[head, here]
            probs = jnp.exp(product(keys, queries, 0, 0) - lse_ref[g, :, here])
            dprobs = product(values, dctx, 0, 0)
            delta = jnp.sum(
                dctx.astype(jnp.float32) * ctx_ref[head, here].astype(jnp.float32),
                axis=0,
                keepdims=True,
            )
            dscores = (probs * (dprobs - delta)).astype(LOW)
            out_ref[0, head, here] = (product(keys, dscores, 1, 0) * DH**-0.5).astype(LOW)
            out_ref[1, head, here] = product(queries, dscores, 1, 1).astype(LOW)
            out_ref[2, head, here] = product(dctx, probs.astype(LOW), 1, 1).astype(LOW)

    each_item(start_ref, length_ref, item)


def attend(starts, lengths, qkv):
    heads = qkv.shape[1] // DH
    group = min(heads, 2)
    return pl.pallas_call(
        attend_kernel,
        out_shape=(
            jax.ShapeDtypeStruct(qkv.shape[1:], LOW),
            jax.ShapeDtypeStruct((heads, 1, SLOTS), jnp.float32),
        ),
        grid_spec=pltpu.PrefetchScalarGridSpec(
            num_scalar_prefetch=2,
            grid=(heads // group,),
            in_specs=[pl.BlockSpec((3, group * DH, SLOTS), lambda h, *_: (0, h, 0))],
            out_specs=(
                pl.BlockSpec((group * DH, SLOTS), lambda h, *_: (h, 0)),
                pl.BlockSpec((group, 1, SLOTS), lambda h, *_: (h, 0, 0)),
            ),
        ),
        compiler_params=pltpu.CompilerParams(vmem_limit_bytes=12 * 2**20),
        cost_estimate=pl.CostEstimate(
            flops=heads * SLOTS * LONG * 1024, bytes_accessed=2**22, transcendentals=heads * 2**19
        ),
    )(starts, lengths, qkv)


def attend_back(starts, lengths, qkv, ctx, dctx, lse):
    heads = qkv.shape[1] // DH
    group = min(heads, 2)
    one = pl.BlockSpec((group * DH, SLOTS), lambda h, *_: (h, 0))
    three = pl.BlockSpec((3, group * DH, SLOTS), lambda h, *_: (0, h, 0))
    return pl.pallas_call(
        attend_back_kernel,
        out_shape=jax.ShapeDtypeStruct(qkv.shape, LOW),
        grid_spec=pltpu.PrefetchScalarGridSpec(
            num_scalar_prefetch=2,
            grid=(heads // group,),
            in_specs=[three, one, one, pl.BlockSpec((group, 1, SLOTS), lambda h, *_: (h, 0, 0))],
            out_specs=three,
        ),
        compiler_params=pltpu.CompilerParams(vmem_limit_bytes=14 * 2**20),
        cost_estimate=pl.CostEstimate(
            flops=heads * SLOTS * LONG * 2560, bytes_accessed=2**23, transcendentals=heads * 2**19
        ),
    )(starts, lengths, qkv, ctx, dctx, lse)


def tile_at(ref, place, groups):
    row = pl.multiple_of(lax.div(place, groups) * DH, DH)
    col = pl.multiple_of(lax.rem(place, groups) * 128, 128)
    return ref.at[pl.ds(row, DH), pl.ds(col, 128)]


def place_kernel(pieces, extra_rows, count, more, table_ref, *refs):
    sources, refs = refs[:count], refs[count + more :]
    near_ref, ffn_ref, extra_ref = refs[:3]
    buffers, sems = refs[3:-1], refs[-1]
    arriving = [
        pltpu.make_async_copy(source, buffer, sems.at[2 * count + i])
        for i, (source, buffer) in enumerate(zip(sources, buffers))
    ]
    for copy in arriving:
        copy.start()
    groups = near_ref.shape[1] // 128
    bound = near_ref.shape[0] // DH * groups
    owned = table_ref.shape[1] - 16
    for i, (source, parts) in enumerate(zip(buffers, pieces)):
        arriving[i].wait()
        for row, entry, first, blocks in parts:

            @pl.loop(0, blocks)
            def _(j):
                at = table_ref[entry, first + j]
                block = source.at[pl.ds(pl.multiple_of(row + j * DH, 16), DH), :]

                @pl.when(at < bound)
                def _():
                    target = tile_at(near_ref, at, groups)
                    pltpu.make_async_copy(block, target, sems.at[i]).start()

                @pl.when(at >= bound)
                def _():
                    target = tile_at(ffn_ref, at - bound, groups)
                    pltpu.make_async_copy(block, target, sems.at[i]).start()

        if extra_rows[i] is not None:
            pltpu.make_async_copy(
                source.at[pl.ds(extra_rows[i], EXTRA), :],
                extra_ref.at[table_ref[parts[0][1], owned]],
                sems.at[count + i],
            ).start()

    for i, parts in enumerate(pieces):
        total = sum(part[3] for part in parts) * DH
        if total <= ffn_ref.shape[0]:
            landed = [ffn_ref.at[pl.ds(0, total), pl.ds(0, 128)]]
        else:
            landed = [near_ref, ffn_ref]
        for ref in landed:
            pltpu.make_async_copy(ref, ref, sems.at[i]).wait()
        if extra_rows[i] is not None:
            pltpu.make_async_copy(extra_ref.at[0], extra_ref.at[0], sems.at[count + i]).wait()


def place(table, sources, pieces, extra_rows, shapes, previous=None, deps=()):
    chained = previous is not None
    more = [in_hbm(v) for v in previous] if chained else []
    count = len(sources)
    return pl.pallas_call(
        partial(place_kernel, pieces, extra_rows, count, len(more) + len(deps)),
        out_shape=tuple(pltpu.HBM(shape, LOW) for shape in shapes)
        + (pltpu.HBM((table.shape[0], EXTRA, 128), LOW),),
        grid_spec=pltpu.PrefetchScalarGridSpec(
            num_scalar_prefetch=1,
            grid=(),
            in_specs=[ANY] * (count + len(more) + len(deps)),
            out_specs=(ANY,) * 3,
            scratch_shapes=[pltpu.VMEM(v.shape, LOW) for v in sources] + [sems(3 * count)],
        ),
        cost_estimate=FREE,
        compiler_params=pltpu.CompilerParams(vmem_limit_bytes=12 * 2**20),
        input_output_aliases={1 + count + i: i for i in range(3)} if chained else {},
    )(table, *[in_hbm(v) for v in sources], *more, *deps)


def gate_kernel(*refs):
    pass


def gate(value, deps):
    return pl.pallas_call(
        gate_kernel,
        out_shape=jax.ShapeDtypeStruct(value.shape, value.dtype),
        in_specs=[ANY] * (1 + len(deps)),
        out_specs=ANY,
        cost_estimate=FREE,
        input_output_aliases={0: 0},
    )(value, *deps)


def halves_kernel(low, high, *refs):
    out_low, out_high = refs[-2:]
    out_low[...] = low[pl.ds(0, out_low.shape[0])]
    out_high[...] = high[pl.ds(low.shape[0] - out_high.shape[0], out_high.shape[0])]


def halves(low, high, rows, deps=()):
    rest = high.shape[0] - rows
    return pl.pallas_call(
        halves_kernel,
        out_shape=tuple(jax.ShapeDtypeStruct((n, 128), LOW) for n in (rows, rest)),
        in_specs=[VMEM] * 2 + [ANY] * len(deps),
        out_specs=(VMEM,) * 2,
        cost_estimate=FREE,
        compiler_params=pltpu.CompilerParams(vmem_limit_bytes=12 * 2**20),
    )(low, high, *deps)


def fetch_kernel(pieces, deps, table_ref, near_ref, ffn_ref, other_ref, zero_ref, extra_ref, *refs):
    count = len(pieces)
    outs, others, sems = refs[deps : deps + count], refs[deps + count : -1], refs[-1]
    groups = near_ref.shape[1] // 128
    bound = near_ref.shape[0] // DH * groups
    owned = table_ref.shape[1] - 16
    for i, parts in enumerate(pieces):
        for row, entry, first, blocks in parts:
            if blocks == 0:
                pltpu.make_async_copy(
                    extra_ref.at[table_ref[entry, owned]],
                    outs[i].at[pl.ds(row, EXTRA), :],
                    sems.at[i],
                ).start()
                continue

            @pl.loop(0, blocks)
            def _(j):
                at = table_ref[entry, first + j]
                here = pl.ds(pl.multiple_of(row + j * DH, 16), DH)

                def take(source, other):
                    pltpu.make_async_copy(source, outs[i].at[here, :], sems.at[i]).start()
                    pltpu.make_async_copy(
                        other, others[i].at[here, :], sems.at[count + i]
                    ).start()

                @pl.when(at < bound)
                def _():
                    take(tile_at(near_ref, at, groups), zero_ref)

                @pl.when(at >= bound)
                def _():
                    take(
                        tile_at(ffn_ref, at - bound, groups),
                        tile_at(other_ref, at - bound, groups),
                    )

    for i, parts in enumerate(pieces):
        pltpu.make_async_copy(outs[i], outs[i], sems.at[i]).wait()
        rows = sum(part[3] for part in parts) * DH
        landed = others[i].at[pl.ds(0, rows), :]
        pltpu.make_async_copy(landed, landed, sems.at[count + i]).wait()
        for row, _, _, blocks in parts:
            if blocks:
                here = pl.ds(row, blocks * DH)
                value = outs[i][here].astype(jnp.float32) + others[i][here].astype(jnp.float32)
                outs[i][here] = value.astype(LOW)


def fetch(table, grads, extra, pieces, deps=()):
    rows = [sum(part[3] * DH or EXTRA for part in parts) for parts in pieces]
    zero = jnp.zeros((DH, 128), LOW)
    return pl.pallas_call(
        partial(fetch_kernel, pieces, len(deps)),
        out_shape=tuple(jax.ShapeDtypeStruct((n, 128), LOW) for n in rows),
        grid_spec=pltpu.PrefetchScalarGridSpec(
            num_scalar_prefetch=1,
            grid=(),
            in_specs=[ANY] * (5 + len(deps)),
            out_specs=(VMEM,) * len(pieces),
            scratch_shapes=[pltpu.VMEM((n, 128), LOW) for n in rows]
            + [pltpu.SemaphoreType.DMA((2 * len(pieces),))],
        ),
        cost_estimate=FREE,
        compiler_params=pltpu.CompilerParams(vmem_limit_bytes=12 * 2**20),
    )(table, *[in_hbm(g) for g in grads], zero, extra, *deps)


def fetch_all_kernel(pieces, table_ref, grad_ref, extra_ref, out, sem):
    groups = grad_ref.shape[1] // 128
    owned = table_ref.shape[1] - 16
    for row, entry, first, blocks in pieces:
        if blocks == 0:
            pltpu.make_async_copy(
                extra_ref.at[table_ref[entry, owned]], out.at[pl.ds(row, EXTRA), :], sem.at[0]
            ).start()
            continue

        @pl.loop(0, blocks)
        def _(j):
            pltpu.make_async_copy(
                tile_at(grad_ref, table_ref[entry, first + j], groups),
                out.at[pl.ds(pl.multiple_of(row + j * DH, 16), DH), :],
                sem.at[0],
            ).start()

    pltpu.make_async_copy(out, out, sem.at[0]).wait()


def fetch_all(table, grad, extra, pieces):
    rows = sum(part[3] * DH or EXTRA for part in pieces)
    return pl.pallas_call(
        partial(fetch_all_kernel, pieces),
        out_shape=jax.ShapeDtypeStruct((rows, 128), LOW),
        grid_spec=pltpu.PrefetchScalarGridSpec(
            num_scalar_prefetch=1,
            grid=(),
            in_specs=[ANY] * 2,
            out_specs=VMEM,
            scratch_shapes=[pltpu.SemaphoreType.DMA((1,))],
        ),
        compiler_params=pltpu.CompilerParams(vmem_limit_bytes=16 * 2**20),
    )(table, in_hbm(grad), extra)


def turn_kernel(deps, keep_a, got_a, keep_b, got_b, *refs):
    for keep, got, out in zip((keep_a, keep_b), (got_a, got_b), refs[deps:]):
        there = pl.ds(out.shape[0], out.shape[0])
        out[...] = (keep[there].astype(jnp.float32) + got[there].astype(jnp.float32)).astype(LOW)


def turn(keep_a, got_a, keep_b, got_b, deps=()):
    return pl.pallas_call(
        partial(turn_kernel, len(deps)),
        out_shape=tuple(
            jax.ShapeDtypeStruct((keep.shape[0] // 2, 128), LOW) for keep in (keep_a, keep_b)
        ),
        in_specs=[VMEM] * 4 + [ANY] * len(deps),
        out_specs=(VMEM,) * 2,
        cost_estimate=FREE,
        compiler_params=pltpu.CompilerParams(vmem_limit_bytes=12 * 2**20),
    )(keep_a, got_a, keep_b, got_b, *deps)


def total_rows(half, running, start, row, rows):
    here = pl.ds(row, rows)
    result = sum(ref[here].astype(jnp.float32) for ref in half)
    if running is not None:
        result = result + running[pl.ds(start + row, rows)].astype(jnp.float32)
    return result


def total_kernel(chained, deps, *refs):
    running = refs[6] if chained else None
    out = refs[6 + chained + deps]
    start = 0
    for half in (refs[:3], refs[3:6]):
        size = half[2].shape[0]
        result = total_rows(half, running, start, 0, size)
        out[pl.ds(start, size)] = result.astype(out.dtype)
        start += size


def total(half_a, half_b, running, deps=()):
    chain = [] if running is None else [running]
    return pl.pallas_call(
        partial(total_kernel, len(chain), len(deps)),
        out_shape=jax.ShapeDtypeStruct((half_a[2].shape[0] + half_b[2].shape[0], 128), LOW),
        in_specs=[VMEM] * (6 + len(chain)) + [ANY] * len(deps),
        out_specs=VMEM,
        cost_estimate=FREE,
        compiler_params=pltpu.CompilerParams(vmem_limit_bytes=12 * 2**20),
    )(*half_a, *half_b, *chain, *deps)


def divided(value, by):
    shift = by.bit_length() - 1
    assert by == 1 << shift
    return lax.shift_right_logical(value, jnp.full_like(value, shift)), value & (by - 1)


def places_of(perm, panel, panels, heads64, ffn64, row_groups):
    col, row = divided(perm, row_groups)
    in_ffn = jnp.maximum(col - 4 * heads64, 0)
    kind, at = divided(col, heads64)
    ffn_kind, ffn_at = divided(in_ffn, ffn64)
    at_head = (kind * panels + panel) * heads64 + at
    at_ffn = 4 * heads64 * panels + (ffn_kind * panels + panel) * ffn64 + ffn_at
    return jnp.where(col < 4 * heads64, at_head, at_ffn) * row_groups + row


def tables_kernel(rings, sizes, at_ref, own_ref, other_ref, come_ref, go_ref):
    z_at, y_at, x_at = at_ref[0], at_ref[1], at_ref[2]
    owned = own_ref.shape[1]
    for sign, out in ((-1, come_ref), (1, go_ref)):
        for k in range(rings):
            z = lax.rem(z_at + sign * k + rings, rings)
            for y in range(2):
                dp = z * 2 + (y_at ^ y)
                for x, perm in enumerate((own_ref, other_ref)):
                    panel = x_at ^ x
                    entry = 4 * k + 2 * y + x
                    out[pl.ds(entry, 1), :] = jnp.full((1, out.shape[1]), dp * 2 + panel, jnp.int32)
                    out[pl.ds(entry, 1), pl.ds(0, owned)] = places_of(
                        perm[pl.ds(dp, 1), :], panel, 2, *sizes
                    )


def tables(at, own, other, rings, sizes):
    shape = jax.ShapeDtypeStruct((rings * 4, own.shape[1] + 16), jnp.int32)
    return pl.pallas_call(
        partial(tables_kernel, rings, sizes),
        out_shape=(shape, shape),
        in_specs=[SMEM, VMEM, VMEM],
        out_specs=(VMEM, VMEM),
        cost_estimate=FREE,
    )(at, own, other)


class Rows:
    def __init__(self, source, target, sems, first=0):
        rows = min(source.shape[0], target.shape[0])
        self.chunk = rows // sems.shape[0]
        self.copies = []
        for i in range(sems.shape[0]):
            here = pl.ds(i * self.chunk, self.chunk)
            there = pl.ds(first + i * self.chunk, self.chunk)
            self.copies.append(pltpu.make_async_copy(source.at[there], target.at[here], sems.at[i]))
        self.done = 0

    def start(self):
        for copy in self.copies:
            copy.start()
        return self

    def upto(self, rows):
        while self.done * self.chunk < rows and self.done < len(self.copies):
            self.copies[self.done].wait()
            self.done += 1

    def whole(self):
        self.upto(self.chunk * len(self.copies))


class Stream:
    def __init__(self, chunks, buffer, sems):
        slots = buffer.shape[0]
        self.buffer = buffer
        self.copies = [
            pltpu.make_async_copy(chunk, buffer.at[i % slots], sems.at[i % slots])
            for i, chunk in enumerate(chunks)
        ]
        self.used = 0
        for copy in self.copies[:slots]:
            copy.start()

    def next(self):
        slots = self.buffer.shape[0]
        ahead = self.used - 1 + slots
        if self.used and ahead < len(self.copies):
            self.copies[ahead].start()
        self.copies[self.used].wait()
        self.used += 1
        return self.buffer.at[(self.used - 1) % slots]


def row_chunks(weight, row, rows, size):
    return [weight.at[pl.ds(row + at, size), :] for at in range(0, rows, size)]


def column_chunks(weight, row, rows, size):
    return [weight.at[pl.ds(row, rows), pl.ds(at, size)] for at in range(0, weight.shape[1], size)]


class Tiles:
    def __init__(self, buffer, sems):
        self.buffer, self.sems, self.under_way = buffer, sems, []

    def put(self, value, target):
        slot = len(self.under_way) % 2
        if len(self.under_way) >= 2:
            self.under_way[-2].wait()
        self.buffer[slot] = value
        copy = pltpu.make_async_copy(self.buffer.at[slot], target, self.sems.at[slot])
        copy.start()
        self.under_way.append(copy)

    def drain(self):
        for copy in self.under_way[-2:]:
            copy.wait()


def vmem(*shape, dtype=LOW):
    return pltpu.VMEM(shape, dtype)


def megabytes(n):
    return pltpu.CompilerParams(vmem_limit_bytes=n * 2**20)


def work(flops, moved=2**22, transcendentals=0):
    return pl.CostEstimate(flops=flops, bytes_accessed=moved, transcendentals=transcendentals)


def project_in_kernel(q_rows, weight, x, bias, out, w, w_sems):
    rows, tile = out.shape[0], w.shape[1]
    chunks = Stream(row_chunks(weight, 0, rows, tile), w, w_sems)
    for at in range(0, rows, tile):
        here = pl.ds(at, tile)
        value = product(chunks.next()[...], x[...], 1, 1) + jnp.transpose(bias[:, here])[:, :1]
        out[here, :] = (value * (DH**-0.5 if at < q_rows else 1.0)).astype(LOW)


def project_in(weights, x, bias):
    rows, width = bias.shape[1], weights.shape[1]
    return pl.pallas_call(
        partial(project_in_kernel, rows // 3),
        out_shape=jax.ShapeDtypeStruct((rows, x.shape[0]), LOW),
        in_specs=[ANY, VMEM, VMEM],
        out_specs=VMEM,
        scratch_shapes=[vmem(3, min(rows // 3, 256), width), sems(3)],
        compiler_params=megabytes(12),
        cost_estimate=work(2 * rows * x.shape[0] * x.shape[1]),
    )(in_hbm(weights), x, bias)


def project_kernel(row, deps, where_ref, context, weight, *refs):
    mine, theirs, w, w_sems, tiles, tile_sems = refs[deps:]
    loader = Rows(weight, w, w_sems, row).start()
    loader.whole()
    half = mine.shape[0]
    leaving = Tiles(tiles, tile_sems)
    for i, out in ((1, theirs), (0, mine)):
        at = pl.multiple_of((where_ref[0] ^ i) * half, half)
        leaving.put(product(context[:, pl.ds(at, half)], w[...], 0, 0).astype(LOW), out)
    leaving.drain()


def project(where, context, weights, row, deps=(), cost=None):
    features, tokens = context.shape
    width = weights.shape[1]
    out = pltpu.HBM((tokens // 2, width), LOW)
    return pl.pallas_call(
        partial(project_kernel, row, len(deps)),
        out_shape=(out, out),
        in_specs=[SMEM, VMEM, ANY] + [ANY] * len(deps),
        out_specs=(ANY, ANY),
        scratch_shapes=[
            vmem(features, width),
            sems(4),
            vmem(2, tokens // 2, width),
            sems(2),
        ],
        compiler_params=megabytes(14),
        cost_estimate=cost or work(2 * features * tokens * width),
    )(where[None], context, in_hbm(weights), *deps)


def ffn_kernel(parts, row, *refs):
    inputs, (weight, bias), refs = refs[:parts], refs[parts : parts + 2], refs[parts + 2 :]
    values, slopes, outs = refs[:parts], refs[parts : 2 * parts], refs[2 * parts : 3 * parts]
    first, first_sems, second, second_sems = refs[3 * parts :]
    hidden, tile = bias.shape[1], first.shape[1]
    chunks = Stream(row_chunks(weight, row, hidden, tile), first, first_sems)
    columns = Stream(
        column_chunks(weight, row + hidden, hidden, second.shape[2]), second, second_sems
    )
    for at in range(0, hidden, tile):
        here = pl.ds(at, tile)
        w = chunks.next()
        for i, x in enumerate(inputs):
            before = product(x[...], w[...], 1, 1) + bias[:, here]
            result, derivative = gelu_pair(before)
            values[i][:, here] = result.astype(LOW)
            slopes[i][:, here] = derivative.astype(LOW)
    finish_ffn(columns, values, outs)


def finish_ffn(columns, values, outs):
    tile = columns.buffer.shape[2]
    for at in range(0, outs[0].shape[1], tile):
        w = columns.next()
        for value, out in zip(values, outs):
            out[:, pl.ds(at, tile)] = product(value[...], w[...], 1, 0).astype(LOW)


def ffn_shapes(parts, hidden, width):
    tokens = parts[0].shape[0]
    low = [jax.ShapeDtypeStruct((tokens, hidden), LOW)] * len(parts)
    outs = [jax.ShapeDtypeStruct((tokens, width), LOW)] * len(parts)
    scratch = [vmem(2, min(hidden, 512), width), sems(2), vmem(2, hidden, 256), sems(2)]
    return low, outs, scratch


def ffn(parts, weights, row, bias):
    hidden, width, n = bias.shape[1], weights.shape[1], len(parts)
    low, outs, scratch = ffn_shapes(parts, hidden, width)
    result = pl.pallas_call(
        partial(ffn_kernel, n, row),
        out_shape=tuple(low + low + outs),
        in_specs=[VMEM] * n + [ANY, VMEM],
        out_specs=(VMEM,) * (3 * n),
        scratch_shapes=scratch,
        compiler_params=megabytes(SCOPED),
        cost_estimate=work(4 * SLOTS * hidden * width, 2**24, SLOTS * hidden),
    )(*parts, in_hbm(weights), bias)
    return result[:n], result[n : 2 * n], result[2 * n :]


def ffn_back_kernel(parts, row, *refs):
    inputs, weight, slopes = refs[:parts], refs[parts], refs[parts + 1 : 2 * parts + 1]
    refs = refs[2 * parts + 1 :]
    grads, outs, sums = refs[:parts], refs[parts : 2 * parts], refs[2 * parts]
    first, first_sems, second, second_sems = refs[2 * parts + 1 :]
    hidden, tile = sums.shape[1], first.shape[1]
    chunks = Stream(row_chunks(weight, row + hidden, hidden, tile), first, first_sems)
    columns = Stream(column_chunks(weight, row, hidden, second.shape[2]), second, second_sems)
    for at in range(0, hidden, tile):
        here = pl.ds(at, tile)
        w = chunks.next()
        total = 0.0
        for x, slope, grad in zip(inputs, slopes, grads):
            result = product(x[...], w[...], 1, 1) * slope[:, here].astype(jnp.float32)
            grad[:, here] = result.astype(LOW)
            total = total + jnp.sum(result, axis=0, keepdims=True)
        sums[:, here] = jnp.broadcast_to(total, (sums.shape[0], tile))
    finish_ffn(columns, grads, outs)


def ffn_back(parts, weights, row, slopes):
    hidden, width, n = slopes[0].shape[1], weights.shape[1], len(parts)
    low, outs, scratch = ffn_shapes(parts, hidden, width)
    result = pl.pallas_call(
        partial(ffn_back_kernel, n, row),
        out_shape=tuple(low + outs) + (jax.ShapeDtypeStruct((8, hidden), jnp.float32),),
        in_specs=[VMEM] * n + [ANY] + [VMEM] * n,
        out_specs=(VMEM,) * (2 * n + 1),
        scratch_shapes=scratch,
        compiler_params=megabytes(SCOPED),
        cost_estimate=work(4 * SLOTS * hidden * width, 2**24),
    )(*parts, in_hbm(weights), *slopes)
    return result[:n], result[n : 2 * n], result[-1]


def ffn_grad_kernel(parts, row, *refs):
    values, upper, grads, lower = (refs[i * parts : (i + 1) * parts] for i in range(4))
    out, tiles, tile_sems = refs[4 * parts :]
    leaving = Tiles(tiles, tile_sems)
    hidden, tile = values[0].shape[1], tiles.shape[1]
    for lefts, rights, begin in ((values, upper, row + hidden), (grads, lower, row)):
        for at in range(0, hidden, tile):
            here = pl.ds(at, tile)
            value = sum(product(a[:, here], b[...], 0, 0) for a, b in zip(lefts, rights))
            leaving.put(value.astype(LOW), out.at[pl.ds(begin + at, tile), :])
    leaving.drain()


def ffn_grad(values, upper, grads, lower, shape, row):
    n, hidden, width = len(values), values[0].shape[1], shape[1]
    return pl.pallas_call(
        partial(ffn_grad_kernel, n, row),
        out_shape=pltpu.HBM(shape, LOW),
        in_specs=[VMEM] * (4 * n),
        out_specs=ANY,
        scratch_shapes=[vmem(2, min(hidden, 512), width), sems(2)],
        compiler_params=megabytes(SCOPED),
        cost_estimate=work(4 * SLOTS * hidden * width, 2**24),
    )(*values, *upper, *grads, *lower)


def project_back_kernel(
    row, where_ref, weight, context, own, other, out, grad, w, w_sems, h, h_sems, c, c_sems, b, sem
):
    loader = Rows(weight, w, w_sems, row).start()
    hidden = [Rows(part, h.at[i], h_sems.at[i]).start() for i, part in enumerate((own, other))]
    context_rows = Rows(context, c, c_sems).start()
    half = own.shape[0]
    columns = [pl.ds(pl.multiple_of((where_ref[0] ^ i) * half, half), half) for i in range(2)]
    loader.whole()
    for i in range(2):
        hidden[i].whole()
        out[:, columns[i]] = product(w[...], h[i], 1, 1).astype(LOW)
    context_rows.whole()
    b[...] = sum(product(c[:, columns[i]], h[i], 1, 0) for i in range(2)).astype(LOW)
    copy = pltpu.make_async_copy(b, grad.at[pl.ds(row, b.shape[0]), :], sem.at[0])
    copy.start()
    copy.wait()


def project_back(where, weights, context, own, other, row):
    features, tokens = context.shape
    width = own.shape[1]
    return pl.pallas_call(
        partial(project_back_kernel, row),
        out_shape=(
            jax.ShapeDtypeStruct((features, tokens), LOW),
            pltpu.HBM(weights.shape, LOW),
        ),
        in_specs=[SMEM] + [ANY] * 4,
        out_specs=(VMEM, ANY),
        scratch_shapes=[
            vmem(features, width),
            sems(2),
            vmem(2, tokens // 2, width),
            pltpu.SemaphoreType.DMA((2, 2)),
            vmem(features, tokens),
            sems(2),
            vmem(features, width),
            sems(1),
        ],
        compiler_params=megabytes(SCOPED),
        cost_estimate=work(4 * features * tokens * width),
    )(where[None], *[in_hbm(v) for v in (weights, context, own, other)])


def last_grad_kernel(left, right, _, out, sums, tiles, tile_sems):
    leaving = Tiles(tiles, tile_sems)
    tile = tiles.shape[1]
    ones = jnp.ones((sums.shape[0], left.shape[1]), LOW)
    for at in range(0, left.shape[0], tile):
        here = pl.ds(at, tile)
        leaving.put(product(left[here, :], right[...], 1, 0).astype(LOW), out.at[here, :])
        sums[:, here] = product(ones, left[here, :], 1, 1)
    leaving.drain()


def last_grad(left, right, grads):
    rows, tokens = left.shape
    width = right.shape[1]
    tile = 512 if rows % 512 == 0 else rows // 3
    return pl.pallas_call(
        last_grad_kernel,
        out_shape=(pltpu.HBM(grads.shape, LOW), jax.ShapeDtypeStruct((8, rows), jnp.float32)),
        in_specs=[VMEM, VMEM, ANY],
        out_specs=(ANY, VMEM),
        scratch_shapes=[vmem(2, tile, width), sems(2)],
        compiler_params=megabytes(SCOPED),
        cost_estimate=work(2 * rows * tokens * width),
        input_output_aliases={2: 0},
    )(left, right, in_hbm(grads))


BIAS_OUTPUT, BIAS_OUTER, GAIN_ONE, SHIFT_ONE, GAIN_TWO, SHIFT_TWO = range(6)


def row_of(vectors, i):
    return vectors[pl.ds(i, 1), :]


def mean_of(value):
    return jnp.mean(value, axis=-1, keepdims=True)


def widened(here, *refs):
    return sum(ref[here, :].astype(jnp.float32) for ref in refs)


def norm_one_step(here, vectors, x, mine, got, middle, scaled, inverse):
    hidden = widened(here, x, mine, got) + row_of(vectors, BIAS_OUTPUT)
    center = hidden - mean_of(hidden)
    factor = lax.rsqrt(mean_of(center * center) + 1e-05)
    normal = center * factor
    middle[here, :] = (
        normal * row_of(vectors, GAIN_ONE) + row_of(vectors, SHIFT_ONE)
    ).astype(LOW)
    scaled[here, :] = normal.astype(LOW)
    inverse[here, :] = jnp.broadcast_to(factor, (factor.shape[0], 128))
    return ()


def back_through(upstream, normal, factor, gain):
    gained = upstream * gain
    return factor * (gained - mean_of(gained) - normal * mean_of(gained * normal))


def norm_two_step(here, vectors, middle, mine, got, upstream, layer, dz):
    outer = widened(here, middle, mine, got) + row_of(vectors, BIAS_OUTER)
    center = outer - mean_of(outer)
    factor = lax.rsqrt(mean_of(center * center) + 1e-05)
    normal = center * factor
    gain = row_of(vectors, GAIN_TWO)
    layer[here, :] = (normal * gain + row_of(vectors, SHIFT_TWO)).astype(LOW)
    dy = widened(here, upstream)
    result = back_through(dy, normal, factor, gain)
    dz[here, :] = result.astype(LOW)
    return (result, dy * normal, dy)


def norm_back_step(here, vectors, dz, mine, got, scaled, inverse, dhidden):
    dy = widened(here, dz, mine, got)
    normal = widened(here, scaled)
    factor = inverse[here, :][:, :1]
    result = back_through(dy, normal, factor, row_of(vectors, GAIN_ONE))
    dhidden[here, :] = result.astype(LOW)
    return (result, dy * normal, dy)


def layer_kernel(
    x, mine, got, upstream, vectors, bias, w_own, w_other,
    layer, dhidden, sums, inner, g_own, g_other,
    x_in, mine_in, got_in, up_in, in_sems, act, slope, mid, normal, inverse, dz, acc, out,
    out_sems, one, one_sems, two, two_sems, tile_one, tile_one_sems, tile_two, tile_two_sems,
):
    rows = x.shape[0]
    half, tile = w_own.shape[0] // 2, one.shape[1]
    ones = [c for w in (w_own, w_other) for c in row_chunks(w, 0, half, tile)]
    twos = [c for w in (w_own, w_other) for c in row_chunks(w, half, half, tile)]
    arriving = [
        Rows(source, target, in_sems.at[i])
        for i, (source, target) in enumerate(
            ((x, x_in), (mine, mine_in), (got, got_in), (upstream, up_in))
        )
    ]
    for copies in arriving[:3]:
        copies.start()
    first, second = Stream(ones + ones, one, one_sems), Stream(twos + twos, two, two_sems)
    arriving[3].start()
    step = arriving[0].chunk
    places = [pl.ds(at, step) for at in range(0, rows, step)]

    for n, here in enumerate(places):
        for copies in arriving[:3]:
            copies.upto(n * step + step)
        norm_one_step(here, vectors, x_in, mine_in, got_in, mid, normal, inverse)

    before = product(mid[...], first.next()[...], 1, 1) + bias[:, pl.ds(0, tile)]
    for n in range(len(ones)):
        columns = pl.ds(n * tile, tile)
        down_weight = second.next()
        if n + 1 < len(ones):
            up_weight = first.next()
            after = product(mid[...], up_weight[...], 1, 1) + bias[:, pl.ds((n + 1) * tile, tile)]
        value, derivative = gelu_pair(before)
        before = after
        value = value.astype(LOW)
        act[:, columns] = value
        slope[:, columns] = derivative.astype(LOW)
        part = product(value, down_weight[...], 1, 0)
        if n:
            acc[...] += part
        else:
            acc[...] = part

    arriving[3].whole()
    leaving, totals = [], []
    for n, here in enumerate(places):
        outer = acc[here, :] + widened(here, mid) + row_of(vectors, BIAS_OUTER)
        center = outer - mean_of(outer)
        factor = lax.rsqrt(mean_of(center * center) + 1e-05)
        scaled = center * factor
        gain = row_of(vectors, GAIN_TWO)
        out[here, :] = (scaled * gain + row_of(vectors, SHIFT_TWO)).astype(LOW)
        leaving.append(pltpu.make_async_copy(out.at[here], layer.at[here], out_sems.at[n]))
        leaving[-1].start()
        dy = widened(here, up_in)
        result = back_through(dy, scaled, factor, gain)
        acc[here, :] = result
        dz[here, :] = result.astype(LOW)
        totals.append([jnp.sum(v, axis=0, keepdims=True) for v in (result, dy * scaled, dy)])

    grads_one, grads_two = Tiles(tile_one, tile_one_sems), Tiles(tile_two, tile_two_sems)
    for n in range(len(ones)):
        columns = pl.ds(n * tile, tile)
        target, begin = (g_own, n * tile) if n * tile < half else (g_other, n * tile - half)
        value = product(act[:, columns], dz[...], 0, 0)
        grads_two.put(value.astype(LOW), target.at[pl.ds(half + begin, tile), :])
        grad = product(dz[...], second.next()[...], 1, 1) * slope[:, columns].astype(jnp.float32)
        inner[:, columns] = jnp.broadcast_to(
            jnp.sum(grad, axis=0, keepdims=True), (inner.shape[0], tile)
        )
        slope[:, columns] = grad.astype(LOW)
        value = product(slope[:, columns], mid[...], 0, 0)
        grads_one.put(value.astype(LOW), target.at[pl.ds(begin, tile), :])
        acc[...] += product(slope[:, columns], first.next()[...], 1, 0)

    for n, here in enumerate(places):
        dy = acc[here, :]
        scaled = widened(here, normal)
        factor = inverse[here, :][:, :1]
        result = back_through(dy, scaled, factor, row_of(vectors, GAIN_ONE))
        got_in[here, :] = result.astype(LOW)
        leaving.append(pltpu.make_async_copy(got_in.at[here], dhidden.at[here], in_sems.at[2, n]))
        leaving[-1].start()
        totals.append([jnp.sum(v, axis=0, keepdims=True) for v in (result, dy * scaled, dy)])
    count = len(places)
    lines = [sum(t[i] for t in part) for part in (totals[:count], totals[count:]) for i in range(3)]
    sums[...] = jnp.concatenate(lines + [jnp.zeros_like(lines[0])] * 2, axis=0)
    grads_one.drain()
    grads_two.drain()
    for copy in leaving:
        copy.wait()


def layer_part(x, mine, got, upstream, vectors, bias, w_own, w_other):
    rows, width = x.shape
    hidden = bias.shape[1]
    tile = 512
    low = jax.ShapeDtypeStruct((rows, width), LOW)
    grad = pltpu.HBM(w_own.shape, LOW)
    dma = pltpu.SemaphoreType.DMA
    return pl.pallas_call(
        layer_kernel,
        out_shape=(
            low,
            pltpu.HBM((rows, width), LOW),
            jax.ShapeDtypeStruct((8, width), jnp.float32),
            jax.ShapeDtypeStruct((8, hidden), jnp.float32),
            grad,
            grad,
        ),
        in_specs=[ANY] * 4 + [VMEM] * 2 + [ANY] * 2,
        out_specs=(ANY, ANY, VMEM, VMEM, ANY, ANY),
        scratch_shapes=[vmem(rows, width) for _ in range(4)]
        + [
            dma((4, 4)),
            vmem(rows, hidden),
            vmem(rows, hidden),
            vmem(rows, width),
            vmem(rows, width),
            vmem(rows, 128, dtype=jnp.float32),
            vmem(rows, width),
            vmem(rows, width, dtype=jnp.float32),
            vmem(rows, width),
            sems(4),
            vmem(3, tile, width),
            sems(3),
            vmem(3, tile, width),
            sems(3),
            vmem(2, tile, width),
            sems(2),
            vmem(2, tile, width),
            sems(2),
        ],
        compiler_params=megabytes(46),
        cost_estimate=work(12 * rows * hidden * width, 2**25, rows * hidden),
    )(*[in_hbm(v) for v in (x, mine, got, upstream)], vectors, bias, in_hbm(w_own), in_hbm(w_other))


def rows_kernel(step, count, with_sums, vectors, *refs):
    inputs, outs = refs[:count], refs[count:]
    if with_sums:
        sums, outs = outs[-1], outs[:-1]
    rows = inputs[0].shape[0]
    tile = min(rows, 128)
    totals = 0
    for at in range(0, rows, tile):
        values = step(pl.ds(at, tile), vectors, *inputs, *outs)
        if with_sums:
            parts = [jnp.sum(value, axis=0, keepdims=True) for value in values]
            totals = totals + jnp.concatenate(parts + [jnp.zeros_like(parts[0])] * 5, axis=0)
    if with_sums:
        sums[...] = totals


def by_rows(step, inputs, vectors, outs, with_sums):
    rows, width = inputs[0].shape
    shapes = [jax.ShapeDtypeStruct((rows, n), dtype) for n, dtype in outs]
    if with_sums:
        shapes.append(jax.ShapeDtypeStruct((8, width), jnp.float32))
    return pl.pallas_call(
        partial(rows_kernel, step, len(inputs), with_sums),
        out_shape=tuple(shapes),
        in_specs=[VMEM] * (1 + len(inputs)),
        out_specs=(VMEM,) * len(shapes),
        compiler_params=megabytes(12),
        cost_estimate=work(40 * rows * width, 2**23, rows),
    )(vectors, *inputs)


def shampoo_blocks(scale, grad, left_root, right_root, left, right, weight, outs):
    new_left, new_right, new_weight = outs
    for i in range(grad.shape[0]):
        g = grad[i].astype(LOW)
        new_left[i] = 0.5 * left[i] + (0.5 * scale) * product(g, g, 0, 0)
        new_right[i] = 0.5 * right[i] + (0.5 * scale) * product(g, g, 1, 1)
        step = product(g, left_root[i].astype(LOW), 1, 1)
        step = product(right_root[i].astype(LOW), step.astype(LOW), 0, 0)
        here = weight[i]
        size = jnp.sqrt(jnp.mean(here * here, keepdims=True) + 1e-06)
        norm = jnp.sqrt(jnp.mean(step * step, keepdims=True) + 1e-06)
        new_weight[i] = here - (0.3 * size / norm) * step


def shampoo_kernel(scale, *refs):
    grad, inputs, outs = refs[0], refs[1:6], refs[6:]
    shampoo_blocks(scale, grad, *inputs, outs)


def last_kernel(scale, *refs):
    halves, running, inputs = (refs[:3], refs[3:6]), refs[6], refs[7:12]
    grad, extra, outs = refs[12], refs[13], refs[14:]
    blocks = grad.shape[0]
    at = pl.program_id(0)
    rows_a = halves[0][2].shape[0] - EXTRA
    steps_a = rows_a // (blocks * DH)

    def take(half, start, step):
        row = pl.multiple_of(step * blocks * DH, blocks * DH)
        value = total_rows(half, running, start, row, blocks * DH)
        grad[...] = value.reshape(blocks, DH, 128)

    @pl.when(at < steps_a)
    def _():
        take(halves[0], 0, at)

    @pl.when(at >= steps_a)
    def _():
        take(halves[1], rows_a + EXTRA, at - steps_a)

    extra[...] = total_rows(halves[0], running, 0, rows_a, EXTRA)
    shampoo_blocks(scale, grad, *inputs, outs)


def shampoo_specs(tile, values):
    return [pl.BlockSpec((tile,) + v.shape[1:], lambda i: (i, 0, 0)) for v in values]


def shampoo(scale, grad, *state):
    owned = grad.shape[0]
    tile = 8 if owned % 8 == 0 else owned
    return pl.pallas_call(
        partial(shampoo_kernel, scale),
        out_shape=tuple(jax.ShapeDtypeStruct(v.shape, jnp.float32) for v in state[2:]),
        grid=(owned // tile,),
        in_specs=shampoo_specs(tile, (grad, *state)),
        out_specs=tuple(shampoo_specs(tile, state[2:])),
        compiler_params=megabytes(16),
    )(grad, *state)


def last_step(scale, half_a, half_b, running, *state):
    owned = state[0].shape[0]
    tile = 8
    grad = jax.ShapeDtypeStruct((owned, DH, 128), jnp.float32)
    return pl.pallas_call(
        partial(last_kernel, scale),
        out_shape=(grad, jax.ShapeDtypeStruct((EXTRA, 128), jnp.float32))
        + tuple(jax.ShapeDtypeStruct(v.shape, jnp.float32) for v in state[2:]),
        grid=(owned // tile,),
        in_specs=[
            pl.BlockSpec(v.shape, lambda i: (0, 0)) for v in (*half_a, *half_b, running)
        ]
        + shampoo_specs(tile, state),
        out_specs=(
            *shampoo_specs(tile, (grad,)),
            pl.BlockSpec((EXTRA, 128), lambda i: (0, 0)),
            *shampoo_specs(tile, state[2:]),
        ),
        compiler_params=megabytes(32),
    )(*half_a, *half_b, running, *state)


class Fabric:
    def __init__(self, sizes, row_ways):
        self.batch, self.model = sizes
        self.ways = row_ways
        self.panels = self.model // row_ways
        self.wide = row_ways == 2 and self.panels == 2 and self.batch % 2 == 0
        self.row_groups = [
            list(range(i, i + row_ways)) for i in range(0, self.model, row_ways)
        ]
        self.same_groups = [list(range(t, self.model, row_ways)) for t in range(row_ways)]

    def send(self, value, move):
        pairs = []
        for d in range(self.batch):
            for m in range(self.model):
                e, n = move(d, m)
                pairs.append((d * self.model + m, (e % self.batch) * self.model + n))
        return lax.ppermute(value, BOTH, pairs)

    def to_core(self, value):
        return self.send(value, lambda d, m: (d, m ^ 1))

    def to_x(self, value):
        return self.send(value, lambda d, m: (d, m ^ 2))

    def to_y(self, value):
        return self.send(value, lambda d, m: (d ^ 1, m))

    def to_z(self, value):
        return self.send(value, lambda d, m: (d + 2, m))

    def row_gather(self, own):
        if self.wide:
            return self.join(self.share(own), 0)
        return lax.all_gather(own, "mp", axis=0, tiled=True, axis_index_groups=self.row_groups)

    def share(self, own):
        if self.wide:
            return [own, self.to_core(own)]
        return [self.row_gather(own)]

    def gather_back(self, parts):
        if self.wide:
            return parts[0].astype(LOW), self.to_core(parts[1].astype(LOW))
        mine = lax.psum_scatter(
            parts[0].astype(LOW),
            "mp",
            scatter_dimension=0,
            tiled=True,
            axis_index_groups=self.row_groups,
        )
        return mine, jnp.zeros(mine.shape, LOW)

    def cut(self, value, axis):
        if not self.wide:
            return [value]
        size = value.shape[axis] // 2
        core = lax.rem(lax.axis_index("mp"), 2)
        return [
            lax.dynamic_slice_in_dim(value, at * size, size, axis) for at in (core, 1 - core)
        ]

    def join(self, parts, axis):
        if not self.wide:
            return parts[0]
        own, other = parts
        first = lax.rem(lax.axis_index("mp"), 2) == 0
        return jnp.concatenate(
            [jnp.where(first, own, other), jnp.where(first, other, own)], axis=axis
        )

    def row_sum(self, value):
        if self.wide:
            return value + self.to_core(value)
        return lax.psum(value, "mp", axis_index_groups=self.row_groups)


def shards(
    sizes,
    x_in,
    out_grad,
    item_lengths,
    weight_store,
    owner_perm,
    left_roots,
    right_roots,
    left_stats,
    right_stats,
    head_vectors,
    head_first,
    head_second,
    shared_vectors,
    shared_first,
    shared_second,
):
    batch_ways, model_ways = sizes
    shard_rows, model_width = x_in.shape
    fabric = Fabric(sizes, SLOTS // shard_rows)
    ways, panels, wide = fabric.ways, fabric.panels, fabric.wide
    dp_at, mp_at = lax.axis_index("dp"), lax.axis_index("mp")
    row_at, place_at = lax.div(mp_at, ways), lax.rem(mp_at, ways)

    owned, row_block, col_block = weight_store.shape[1:]
    head_part, shared_part = head_vectors.shape[1], shared_vectors.shape[0]
    head_count, shared_count = head_part * batch_ways, shared_part * batch_ways * model_ways
    block_count = owner_perm.shape[1]
    row_groups = model_width // row_block
    head_width = model_width // model_ways
    ffn_total = shared_count - 6 * model_width
    ffn_width = ffn_total // model_ways
    heads64, ffn64 = head_width // DH, ffn_width // DH
    hidden_rows = panels * (4 * head_width + 2 * ffn_width)
    q_rows, f_rows = panels * head_width, panels * ffn_width
    panel_shape = (hidden_rows, model_width)
    panel_shapes = ((4 * q_rows, model_width), (2 * f_rows, model_width))
    half_a = (owned // 2) * DH + EXTRA
    blocks_a, blocks_b = owned // 2, owned - owned // 2

    def two_parts(value):
        high = lax.reduce_precision(value, 8, 7)
        return jnp.concatenate([high.astype(LOW), (value - high).astype(LOW)])

    blocks_low = jnp.swapaxes(weight_store[0], 1, 2).astype(LOW).reshape(owned * DH, 128)
    vectors = jnp.concatenate([two_parts(head_vectors[0]), two_parts(shared_vectors)])
    vectors = jnp.pad(vectors, (0, EXTRA * 128 - vectors.shape[0])).reshape(EXTRA, 128)
    own = jnp.concatenate(
        [blocks_low[: blocks_a * DH], vectors, blocks_low[blocks_a * DH :]], axis=0
    )

    layout = (heads64, ffn64, row_groups)
    perm = owner_perm.reshape(batch_ways, owned)
    if wide:
        perm_other = fabric.to_x(perm)
    else:
        perm_all = lax.all_gather(perm, "mp", axis=0, axis_index_groups=fabric.same_groups)
        panel_ids = jnp.arange(panels, dtype=jnp.int32)[:, None, None]
        places = places_of(perm_all, panel_ids, panels, *layout)

    if wide:
        rings = batch_ways // 2
        z_at, y_at = lax.div(dp_at, 2), lax.rem(dp_at, 2)
        table, table_back = tables(
            jnp.stack([z_at, y_at, row_at]), perm, perm_other, rings, layout
        )
        low_half, high_half = (0, 0, blocks_a), (half_a, blocks_a, blocks_b)
        at_extra = blocks_a * DH

        def piece(entry, *halves):
            return [(row, entry, first, count) for row, first, count in halves]

        def near_of(k):
            return [
                (value, piece(4 * k + i, low_half, high_half), at_extra)
                for i, value in enumerate((ring, by_x, by_y))
            ]

        def far_of(k):
            return [
                (far_a[k], piece(4 * k + 3, low_half), at_extra),
                (far_b[k], piece(4 * k + 3, (0, blocks_a, blocks_b)), None),
            ]

        near, far_a, far_b = [], [], []
        ring = own
        for k in range(rings):
            if k:
                deps = [table] if k == 1 else [far_a[k - 2], far_b[k - 2]]
                ring = gate(after, [by_x, by_y] + deps)
            after = fabric.to_z(ring) if k + 1 < rings else None
            by_x, by_y = fabric.to_x(ring), fabric.to_y(ring)
            near.append(near_of(k))
            if k:
                low, high = halves(*last, half_a, [ring])
                far_a.append(fabric.to_x(low))
                far_b.append(fabric.to_y(high))
            last = (by_y, by_x)
        placed = None
        for k in range(rings - 1):
            parts = near[k] + (far_of(k - 1) if k else [])
            placed = place(table, *zip(*parts), panel_shapes, placed, [low])
        low, high = halves(*last, half_a, [far_a[-1], far_b[-1], placed[2]])
        far_a.append(fabric.to_x(low))
        far_b.append(fabric.to_y(high))
        placed = place(
            table, *zip(*(near[-1] + far_of(rings - 2))), panel_shapes, placed, [low]
        )
        w_near, w_ffn, extras = place(table, *zip(*far_of(rings - 1)), panel_shapes, placed)
        extras = extras.astype(jnp.float32)
    else:
        gathered = lax.all_gather(own, "mp", axis=0, axis_index_groups=fabric.same_groups)
        gathered = lax.all_gather(gathered, "dp", axis=0)
        entries = batch_ways * panels
        table = places.transpose(1, 0, 2).reshape(entries, owned)
        index = jnp.arange(entries, dtype=jnp.int32)[:, None]
        table = jnp.concatenate([table, jnp.broadcast_to(index, (entries, 16))], axis=1)
        extras = gathered[:, :, blocks_a * DH : half_a].astype(jnp.float32)
        stride = own.shape[0]
        flat = gathered.reshape(-1, 128)
        pieces = []
        for i in range(batch_ways * panels):
            pieces += [(i * stride, i, 0, blocks_a), (i * stride + half_a, i, blocks_a, blocks_b)]
        w_near, w_ffn, _ = place(table, [flat], [pieces], [None], panel_shapes)
        weights = jnp.concatenate([w_near, w_ffn], axis=0)

    extras = extras.reshape(batch_ways, panels, EXTRA * 128)
    head_all = extras[:, :, :head_part] + extras[:, :, head_part : 2 * head_part]
    begin = 2 * head_part
    shared_all = (
        extras[:, :, begin : begin + shared_part]
        + extras[:, :, begin + shared_part : begin + 2 * shared_part]
    )
    head_all = head_all.transpose(1, 0, 2).reshape(panels, head_count)
    if wide:
        shared_other = fabric.to_core(shared_all)
        first = place_at == 0
        shared = jnp.stack(
            [
                jnp.where(first, shared_all, shared_other),
                jnp.where(first, shared_other, shared_all),
            ],
            axis=2,
        )
    else:
        shared = lax.all_gather(
            shared_all, "mp", axis=0, axis_index_groups=fabric.row_groups
        ).transpose(1, 2, 0, 3)
    shared = shared.reshape(shared_count)

    bias_query = head_all[:, :head_width].reshape(q_rows)
    bias_value = head_all[:, head_width:].reshape(q_rows)
    bias_qkv = jnp.concatenate([bias_query, jnp.zeros((q_rows,), jnp.float32), bias_value])
    vectors = jnp.pad(shared[: 6 * model_width].reshape(6, model_width), ((0, 2), (0, 0)))
    bias_inner = shared[6 * model_width :].reshape(panels, ways, ffn_width)
    bias_local = lax.dynamic_index_in_dim(bias_inner, place_at, 1, keepdims=False).reshape(f_rows)
    if wide:
        bias_other = lax.dynamic_index_in_dim(bias_inner, 1 - place_at, 1, keepdims=False)
        bias_both = jnp.concatenate([bias_local, bias_other.reshape(f_rows)])

    lengths = lax.dynamic_index_in_dim(item_lengths, row_at, 0, keepdims=False)
    starts = jnp.cumsum(lengths) - lengths

    x_row = fabric.row_gather(x_in)
    bias_qkv = jnp.broadcast_to(bias_qkv[None], (8, 3 * q_rows))
    qkv = project_in(w_near, x_row, bias_qkv).reshape(3, q_rows, SLOTS)
    context, log_total = attend(starts, lengths, qkv)
    if wide:
        w_ffn = gate(w_ffn, [x_row])
        w_ffn_other = fabric.to_core(w_ffn)
        mine, got = fabric.gather_back(project(place_at, context, w_near, 3 * q_rows))
        layer_value, hidden_grad, sums, inner_sums, grad_ffn, grad_ffn_other = layer_part(
            x_in, mine, got, out_grad, vectors, bias_both[None], w_ffn, w_ffn_other
        )
        hidden_parts = fabric.share(hidden_grad)
        grad_ffn_got = fabric.to_core(gate(grad_ffn_other, [hidden_parts[1]]))
        dcontext, grad_near = project_back(
            place_at, w_near, context, *hidden_parts, 3 * q_rows
        )
        inner = [
            part.reshape(panels, ffn_width) for part in (inner_sums[0, :f_rows], inner_sums[0, f_rows:])
        ]
        inner_all = jnp.where(
            place_at == 0, jnp.stack(inner, axis=1), jnp.stack(inner[::-1], axis=1)
        )
    else:
        w_out, w_qkv = w_near[3 * q_rows :], w_near[: 3 * q_rows]
        mine, got = fabric.gather_back([product(context, w_out, 0, 0)])
        low = (model_width, LOW)
        middle, middle_scaled, middle_inverse = by_rows(
            norm_one_step, (x_in, mine, got), vectors, (low, low, (128, jnp.float32)), False
        )
        middle_parts = fabric.share(middle)
        activated, slopes, results = ffn(middle_parts, weights, 4 * q_rows, bias_local[None])
        mine, got = fabric.gather_back(results)
        layer_value, resid_grad, sums_two = by_rows(
            norm_two_step, (middle, mine, got, out_grad), vectors, (low, low), True
        )
        resid_parts = fabric.share(resid_grad)
        before_grads, results, inner_sums = ffn_back(resid_parts, weights, 4 * q_rows, slopes)
        mine, got = fabric.gather_back(results)
        hidden_grad, sums_one = by_rows(
            norm_back_step,
            (resid_grad, mine, got, middle_scaled, middle_inverse),
            vectors,
            (low,),
            True,
        )
        grads = ffn_grad(
            activated, resid_parts, before_grads, middle_parts, panel_shape, 4 * q_rows
        )
        hidden_parts = fabric.share(hidden_grad)
        dcontext = product(w_out, hidden_parts[0], 1, 1).astype(LOW)
        part = product(context, hidden_parts[0], 1, 0).astype(LOW)
        grad_near = lax.dynamic_update_slice_in_dim(grads, part, 3 * q_rows, 0)
        sums = jnp.concatenate([sums_two[:3], sums_one[:3]], axis=0)
        inner_all = lax.dynamic_update_slice(
            jnp.zeros((panels, ways, ffn_width), jnp.float32),
            inner_sums[0].reshape(panels, 1, ffn_width),
            (0, place_at, 0),
        )
    qkv_grad = attend_back(starts, lengths, qkv, context, dcontext, log_total)
    qkv_grad = qkv_grad.reshape(3 * q_rows, SLOTS)
    grad_near, column_sums = last_grad(qkv_grad, x_row, grad_near)
    column_sums = column_sums[0]
    if wide:
        mine, theirs = project(place_at, qkv_grad, w_near, 0)

    head_grad = jnp.concatenate(
        [
            column_sums[:q_rows].reshape(panels, head_width),
            column_sums[2 * q_rows :].reshape(panels, head_width),
        ],
        axis=1,
    )
    shared_grad = jnp.concatenate(
        [sums[i] for i in (3, 0, 4, 5, 1, 2)] + [inner_all.reshape(ffn_total)]
    )
    if wide:
        shared_grad = gate(shared_grad, [qkv_grad])
    shared_grad = fabric.row_sum(shared_grad)
    shared_grad = shared_grad.reshape(batch_ways, panels, ways, shared_part)
    shared_grad = lax.dynamic_index_in_dim(shared_grad, place_at, 2, keepdims=False)
    head_grad = head_grad.reshape(panels, batch_ways, head_part).transpose(1, 0, 2)
    extra_grad = jnp.concatenate([head_grad, shared_grad], axis=2).astype(LOW)
    extra_grad = jnp.pad(
        extra_grad, ((0, 0), (0, 0), (0, EXTRA * 128 - head_part - shared_part))
    ).reshape(batch_ways * panels, EXTRA, 128)

    if wide:
        half_b = blocks_b * DH

        def low_of(k, entries):
            parts = []
            for i, entry in enumerate(entries):
                parts.append((i * half_a, 4 * k + entry, 0, blocks_a))
                parts.append((i * half_a + blocks_a * DH, 4 * k + entry, 0, 0))
            return parts

        def high_of(k, entries):
            return [
                (i * half_b, 4 * k + entry, blocks_a, blocks_b) for i, entry in enumerate(entries)
            ]

        sent, kept, far, order = {}, {}, {}, []

        def gather(pieces):
            result = fetch(table_back, (grad_near, grad_ffn, grad_ffn_got), extra_grad, pieces, order)
            order[:] = [result[0]]
            return result

        def send(k, after=()):
            send_x, send_y = gather([low_of(k, (1, 3)), high_of(k, (2, 3))])
            if after:
                send_x, send_y = gate(send_x, after), gate(send_y, after)
            sent[k] = fabric.to_x(send_x), fabric.to_y(send_y)

        def keep(k):
            kept[k] = gather([low_of(k, (0, 2)), high_of(k, (0, 1))])

        def pass_on(k):
            sum_a, sum_b = turn(kept[k][0], sent[k][0], kept[k][1], sent[k][1], order)
            far[k] = fabric.to_y(sum_a), fabric.to_x(sum_b)
            order[:] = [sum_a]

        def finish(k, running):
            half = [(kept[k][i], sent[k][i], far[k][i]) for i in range(2)]
            result = total(*half, running, order)
            order[:] = [result]
            return fabric.to_z(result)

        last = rings - 1
        for k in (last, last - 1):
            send(k)
        for k in (last, last - 1):
            keep(k)
        pass_on(last)
        pass_on(last - 1)
        if last > 1:
            send(last - 2)
            keep(last - 2)
        running = finish(last, None)
        for k in range(last - 2, -1, -1):
            pass_on(k)
            if k:
                send(k - 1)
                keep(k - 1)
            running = finish(k + 1, running)
        final = [(kept[0][i], sent[0][i], far[0][i]) for i in range(2)]
    else:
        pieces = []
        for i in range(batch_ways * panels):
            base = i * own.shape[0]
            pieces += [
                (base, i, 0, blocks_a),
                (base + blocks_a * DH, i, 0, 0),
                (base + half_a, i, blocks_a, blocks_b),
            ]
        chunks = fetch_all(table, grad_near, extra_grad, pieces)
        chunks = chunks.reshape(batch_ways, panels, own.shape[0], 128)
        chunks = lax.psum_scatter(chunks, "dp", scatter_dimension=0, tiled=False)
        reduced = lax.psum_scatter(
            chunks,
            "mp",
            scatter_dimension=0,
            tiled=False,
            axis_index_groups=fabric.same_groups,
        ).astype(jnp.float32)

        block_grads = jnp.concatenate([reduced[: blocks_a * DH], reduced[half_a:]], axis=0)
        vector_grads = reduced[blocks_a * DH : half_a]

    scale = 1.0 / (shard_rows * model_ways * batch_ways)
    state = (
        left_roots[0],
        right_roots[0],
        left_stats[0],
        right_stats[0],
        jnp.swapaxes(weight_store[0], 1, 2),
    )
    if wide:
        block_grads, vector_grads, *renewed = last_step(scale, *final, running, *state)
        mine, got = fabric.gather_back((mine, theirs))
    else:
        block_grads = block_grads.reshape(owned, DH, 128)
        renewed = shampoo(scale, block_grads, *state)
        mine, got = fabric.gather_back([product(qkv_grad, w_qkv, 0, 0)])
    new_left, new_right, new_weights = renewed
    input_grad = sum(v.astype(jnp.float32) for v in (hidden_grad, mine, got))
    vector_grads = vector_grads.reshape(EXTRA * 128)
    head_grad_mine = vector_grads[:head_part]
    shared_grad_mine = vector_grads[head_part : head_part + shared_part]

    head_one, head_two, head_new = adam_update(
        head_vectors[0], head_first[0], head_second[0], head_grad_mine
    )
    shared_one, shared_two, shared_new = adam_update(
        shared_vectors, shared_first, shared_second, shared_grad_mine
    )
    return (
        layer_value,
        input_grad,
        jnp.swapaxes(block_grads, 1, 2)[None],
        new_left[None],
        new_right[None],
        jnp.swapaxes(new_weights, 1, 2)[None],
        head_one[None],
        head_two[None],
        head_new[None],
        shared_one,
        shared_two,
        shared_new,
    )


def solution(mesh):
    rows, blocks, vector, head = P(BOTH, None), P("mp", "dp", None, None), P(BOTH), P("mp", "dp")
    return jax.shard_map(
        partial(shards, (mesh.shape["dp"], mesh.shape["mp"])),
        mesh=mesh,
        in_specs=(rows, rows, P("dp", None), blocks, P("mp", None))
        + (blocks,) * 4
        + (head,) * 3
        + (vector,) * 3,
        out_specs=(rows, rows) + (blocks,) * 4 + (head,) * 3 + (vector,) * 3,
        check_vma=False,
    )
```

```python
from functools import partial

import jax
import jax.numpy as jnp
from jax import lax
from jax.experimental import pallas as pl
from jax.experimental.pallas import tpu as pltpu
from jax.sharding import PartitionSpec as P

DH = 64
SLOTS = 1024
STEP = 10
SHORT = 128
LONG = 512
EXTRA = 16
SCOPED = 14
FINE = 32
WIDE = 1024
WHOLE = 2048
LOW = jnp.bfloat16
BOTH = ("dp", "mp")
ANY = pl.BlockSpec(memory_space=pl.ANY)
VMEM = pl.BlockSpec(memory_space=pltpu.VMEM)
SMEM = pl.BlockSpec(memory_space=pltpu.SMEM)
FREE = pl.CostEstimate(flops=0, bytes_accessed=0, transcendentals=0)
MOVE = pl.CostEstimate(flops=0, bytes_accessed=2**24, transcendentals=0)


def sems(n):
    return pltpu.SemaphoreType.DMA((n,))


def in_hbm(value):
    return pltpu.with_memory_space_constraint(value, pltpu.HBM)


def product(left, right, left_dim, right_dim):
    return lax.dot_general(
        left, right, (((left_dim,), (right_dim,)), ((), ())), preferred_element_type=jnp.float32
    )


def adam_update(current, moment_one, moment_two, gradient):
    first_new = 0.9 * moment_one + 0.1 * gradient
    second_new = 0.999 * moment_two + 0.001 * gradient * gradient
    stepped = first_new / (1.0 - 0.9**STEP) / (jnp.sqrt(second_new / (1.0 - 0.999**STEP)) + 1e-08)
    return (first_new, second_new, current - 0.3 * stepped)


def gelu_pair(before):
    below = 0.5 + 0.5 * lax.erf(before * 0.5**0.5)
    slope = below + before * jnp.exp(before * before * -0.5) * 0.3989422804014327
    return before * below, slope


def attend_kernel(start_ref, length_ref, qkv_ref, ctx_ref, lse_ref):
    def item(begin, size):
        here = pl.ds(begin, size)
        for g in range(lse_ref.shape[0]):
            head = pl.ds(g * DH, DH)
            scores = product(qkv_ref[1, head, here], qkv_ref[0, head, here], 0, 0)
            top = jnp.max(scores, axis=0, keepdims=True)
            expo = jnp.exp(scores - top)
            total = jnp.sum(expo, axis=0, keepdims=True)
            ctx = product(qkv_ref[2, head, here], expo.astype(LOW), 1, 0) / total
            ctx_ref[head, here] = ctx.astype(LOW)
            lse_ref[g, :, here] = top + jnp.log(total)

    each_item(start_ref, length_ref, item)


def each_item(start_ref, length_ref, item):
    @pl.loop(0, start_ref.shape[0])
    def _(i):
        begin = pl.multiple_of(start_ref[i], SHORT)

        @pl.when(length_ref[i] == LONG)
        def _():
            item(begin, LONG)

        @pl.when(length_ref[i] == SHORT)
        def _():
            item(begin, SHORT)


def attend_back_kernel(
    start_ref, length_ref, qkv_ref, ctx_ref, dctx_ref, lse_ref, out_ref
):
    def item(begin, size):
        here = pl.ds(begin, size)
        for g in range(lse_ref.shape[0]):
            head = pl.ds(g * DH, DH)
            queries, keys, values = (qkv_ref[i, head, here] for i in range(3))
            dctx = dctx_ref[head, here]
            probs = jnp.exp(product(keys, queries, 0, 0) - lse_ref[g, :, here])
            dprobs = product(values, dctx, 0, 0)
            delta = jnp.sum(
                dctx.astype(jnp.float32) * ctx_ref[head, here].astype(jnp.float32),
                axis=0,
                keepdims=True,
            )
            dscores = (probs * (dprobs - delta)).astype(LOW)
            out_ref[0, head, here] = (product(keys, dscores, 1, 0) * DH**-0.5).astype(LOW)
            out_ref[1, head, here] = product(queries, dscores, 1, 1).astype(LOW)
            out_ref[2, head, here] = product(dctx, probs.astype(LOW), 1, 1).astype(LOW)

    each_item(start_ref, length_ref, item)


def attend(starts, lengths, qkv):
    heads = qkv.shape[1] // DH
    group = min(heads, 2)
    return pl.pallas_call(
        attend_kernel,
        out_shape=(
            jax.ShapeDtypeStruct(qkv.shape[1:], LOW),
            jax.ShapeDtypeStruct((heads, 1, SLOTS), jnp.float32),
        ),
        grid_spec=pltpu.PrefetchScalarGridSpec(
            num_scalar_prefetch=2,
            grid=(heads // group,),
            in_specs=[pl.BlockSpec((3, group * DH, SLOTS), lambda h, *_: (0, h, 0))],
            out_specs=(
                pl.BlockSpec((group * DH, SLOTS), lambda h, *_: (h, 0)),
                pl.BlockSpec((group, 1, SLOTS), lambda h, *_: (h, 0, 0)),
            ),
        ),
        compiler_params=pltpu.CompilerParams(vmem_limit_bytes=12 * 2**20),
        cost_estimate=pl.CostEstimate(
            flops=heads * SLOTS * LONG * 1024, bytes_accessed=2**22, transcendentals=heads * 2**19
        ),
    )(starts, lengths, qkv)


def attend_back(starts, lengths, qkv, ctx, dctx, lse):
    heads = qkv.shape[1] // DH
    group = min(heads, 2)
    one = pl.BlockSpec((group * DH, SLOTS), lambda h, *_: (h, 0))
    three = pl.BlockSpec((3, group * DH, SLOTS), lambda h, *_: (0, h, 0))
    return pl.pallas_call(
        attend_back_kernel,
        out_shape=jax.ShapeDtypeStruct(qkv.shape, LOW),
        grid_spec=pltpu.PrefetchScalarGridSpec(
            num_scalar_prefetch=2,
            grid=(heads // group,),
            in_specs=[three, one, one, pl.BlockSpec((group, 1, SLOTS), lambda h, *_: (h, 0, 0))],
            out_specs=three,
        ),
        compiler_params=pltpu.CompilerParams(vmem_limit_bytes=14 * 2**20),
        cost_estimate=pl.CostEstimate(
            flops=heads * SLOTS * LONG * 2560, bytes_accessed=2**23, transcendentals=heads * 2**19
        ),
    )(starts, lengths, qkv, ctx, dctx, lse)


def tile_at(ref, place, groups):
    shift = groups.bit_length() - 1
    row = pl.multiple_of(lax.shift_right_logical(place, shift) * DH, DH)
    col = pl.multiple_of((place & (groups - 1)) * 128, 128)
    return ref.at[pl.ds(row, DH), pl.ds(col, 128)]


def place_kernel(pieces, extra_rows, count, more, table_ref, *refs):
    sources, refs = refs[:count], refs[count + more :]
    near_ref, ffn_ref, extra_ref = refs[:3]
    buffers, sems = refs[3:-1], refs[-1]
    arriving = [
        pltpu.make_async_copy(source, buffer, sems.at[2 * count + i])
        for i, (source, buffer) in enumerate(zip(sources, buffers))
    ]
    for copy in arriving:
        copy.start()
    groups = near_ref.shape[1] // 128
    bound = near_ref.shape[0] // DH * groups
    owned = table_ref.shape[1] - 16
    for i, (source, parts) in enumerate(zip(buffers, pieces)):
        arriving[i].wait()
        for row, entry, first, blocks in parts:

            @pl.loop(0, blocks, unroll=min(blocks, 8))
            def _(j):
                at = table_ref[entry, first + j]
                block = source.at[pl.ds(pl.multiple_of(row + j * DH, 16), DH), :]

                @pl.when(at < bound)
                def _():
                    target = tile_at(near_ref, at, groups)
                    pltpu.make_async_copy(block, target, sems.at[i]).start()

                @pl.when(at >= bound)
                def _():
                    target = tile_at(ffn_ref, at - bound, groups)
                    pltpu.make_async_copy(block, target, sems.at[i]).start()

        if extra_rows[i] is not None:
            pltpu.make_async_copy(
                source.at[pl.ds(extra_rows[i], EXTRA), :],
                extra_ref.at[table_ref[parts[0][1], owned]],
                sems.at[count + i],
            ).start()

    for i, parts in enumerate(pieces):
        total = sum(part[3] for part in parts) * DH
        if total <= ffn_ref.shape[0]:
            landed = [ffn_ref.at[pl.ds(0, total), pl.ds(0, 128)]]
        else:
            landed = [near_ref, ffn_ref]
        for ref in landed:
            pltpu.make_async_copy(ref, ref, sems.at[i]).wait()
        if extra_rows[i] is not None:
            pltpu.make_async_copy(extra_ref.at[0], extra_ref.at[0], sems.at[count + i]).wait()


def place(table, sources, pieces, extra_rows, shapes, previous=None, deps=()):
    chained = previous is not None
    more = [in_hbm(v) for v in previous] if chained else []
    count = len(sources)
    return pl.pallas_call(
        partial(place_kernel, pieces, extra_rows, count, len(more) + len(deps)),
        out_shape=tuple(pltpu.HBM(shape, LOW) for shape in shapes)
        + (pltpu.HBM((table.shape[0], EXTRA, 128), LOW),),
        grid_spec=pltpu.PrefetchScalarGridSpec(
            num_scalar_prefetch=1,
            grid=(),
            in_specs=[ANY] * (count + len(more) + len(deps)),
            out_specs=(ANY,) * 3,
            scratch_shapes=[pltpu.VMEM(v.shape, LOW) for v in sources] + [sems(3 * count)],
        ),
        cost_estimate=FREE,
        compiler_params=pltpu.CompilerParams(vmem_limit_bytes=12 * 2**20),
        input_output_aliases={1 + count + i: i for i in range(3)} if chained else {},
    )(table, *[v if v.shape[0] < WHOLE else in_hbm(v) for v in sources], *more, *deps)


def gate_kernel(*refs):
    pass


def gate(value, deps, space=None):
    shape = jax.ShapeDtypeStruct(value.shape, value.dtype)
    return pl.pallas_call(
        gate_kernel,
        out_shape=space(value.shape, value.dtype) if space else shape,
        in_specs=[ANY] * (1 + len(deps)),
        out_specs=ANY,
        cost_estimate=FREE,
        input_output_aliases={0: 0},
    )(pltpu.with_memory_space_constraint(value, space) if space else value, *deps)


def halves_kernel(low, high, *refs):
    out_low, out_high = refs[-2:]
    out_low[...] = low[pl.ds(0, out_low.shape[0])]
    out_high[...] = high[pl.ds(low.shape[0] - out_high.shape[0], out_high.shape[0])]


def halves(low, high, rows, deps=()):
    rest = high.shape[0] - rows
    return pl.pallas_call(
        halves_kernel,
        out_shape=tuple(jax.ShapeDtypeStruct((n, 128), LOW) for n in (rows, rest)),
        in_specs=[VMEM] * 2 + [ANY] * len(deps),
        out_specs=(VMEM,) * 2,
        cost_estimate=FREE,
        compiler_params=pltpu.CompilerParams(vmem_limit_bytes=12 * 2**20),
    )(low, high, *deps)


def fetch_kernel(pieces, deps, table_ref, near_ref, ffn_ref, other_ref, zero_ref, extra_ref, *refs):
    count = len(pieces)
    outs, others, sems = refs[deps : deps + count], refs[deps + count : -1], refs[-1]
    groups = near_ref.shape[1] // 128
    bound = near_ref.shape[0] // DH * groups
    owned = table_ref.shape[1] - 16
    for i, parts in enumerate(pieces):
        for row, entry, first, blocks in parts:
            if blocks == 0:
                pltpu.make_async_copy(
                    extra_ref.at[table_ref[entry, owned]],
                    outs[i].at[pl.ds(row, EXTRA), :],
                    sems.at[i],
                ).start()
                continue

            @pl.loop(0, blocks, unroll=min(blocks, 8))
            def _(j):
                at = table_ref[entry, first + j]
                here = pl.ds(pl.multiple_of(row + j * DH, 16), DH)

                def take(source, other):
                    pltpu.make_async_copy(source, outs[i].at[here, :], sems.at[i]).start()
                    pltpu.make_async_copy(
                        other, others[i].at[here, :], sems.at[count + i]
                    ).start()

                @pl.when(at < bound)
                def _():
                    take(tile_at(near_ref, at, groups), zero_ref)

                @pl.when(at >= bound)
                def _():
                    take(
                        tile_at(ffn_ref, at - bound, groups),
                        tile_at(other_ref, at - bound, groups),
                    )

    for i, parts in enumerate(pieces):
        pltpu.make_async_copy(outs[i], outs[i], sems.at[i]).wait()
        rows = sum(part[3] for part in parts) * DH
        landed = others[i].at[pl.ds(0, rows), :]
        pltpu.make_async_copy(landed, landed, sems.at[count + i]).wait()
        for row, _, _, blocks in parts:
            if blocks:
                here = pl.ds(row, blocks * DH)
                value = outs[i][here].astype(jnp.float32) + others[i][here].astype(jnp.float32)
                outs[i][here] = value.astype(LOW)


def fetch(table, grads, extra, pieces, deps=()):
    rows = [sum(part[3] * DH or EXTRA for part in parts) for parts in pieces]
    zero = jnp.zeros((DH, 128), LOW)
    return pl.pallas_call(
        partial(fetch_kernel, pieces, len(deps)),
        out_shape=tuple(jax.ShapeDtypeStruct((n, 128), LOW) for n in rows),
        grid_spec=pltpu.PrefetchScalarGridSpec(
            num_scalar_prefetch=1,
            grid=(),
            in_specs=[ANY] * (5 + len(deps)),
            out_specs=(VMEM,) * len(pieces),
            scratch_shapes=[pltpu.VMEM((n, 128), LOW) for n in rows]
            + [pltpu.SemaphoreType.DMA((2 * len(pieces),))],
        ),
        cost_estimate=FREE,
        compiler_params=pltpu.CompilerParams(vmem_limit_bytes=12 * 2**20),
    )(table, *[in_hbm(g) for g in grads], zero, extra, *deps)


def fetch_all_kernel(pieces, table_ref, grad_ref, extra_ref, out, sem):
    groups = grad_ref.shape[1] // 128
    owned = table_ref.shape[1] - 16
    for row, entry, first, blocks in pieces:
        if blocks == 0:
            pltpu.make_async_copy(
                extra_ref.at[table_ref[entry, owned]], out.at[pl.ds(row, EXTRA), :], sem.at[0]
            ).start()
            continue

        @pl.loop(0, blocks)
        def _(j):
            pltpu.make_async_copy(
                tile_at(grad_ref, table_ref[entry, first + j], groups),
                out.at[pl.ds(pl.multiple_of(row + j * DH, 16), DH), :],
                sem.at[0],
            ).start()

    pltpu.make_async_copy(out, out, sem.at[0]).wait()


def fetch_all(table, grad, extra, pieces):
    rows = sum(part[3] * DH or EXTRA for part in pieces)
    return pl.pallas_call(
        partial(fetch_all_kernel, pieces),
        out_shape=jax.ShapeDtypeStruct((rows, 128), LOW),
        grid_spec=pltpu.PrefetchScalarGridSpec(
            num_scalar_prefetch=1,
            grid=(),
            in_specs=[ANY] * 2,
            out_specs=VMEM,
            scratch_shapes=[pltpu.SemaphoreType.DMA((1,))],
        ),
        compiler_params=pltpu.CompilerParams(vmem_limit_bytes=16 * 2**20),
    )(table, in_hbm(grad), extra)


def turn_kernel(deps, keep_a, got_a, keep_b, got_b, *refs):
    for keep, got, out in zip((keep_a, keep_b), (got_a, got_b), refs[deps:]):
        there = pl.ds(out.shape[0], out.shape[0])
        out[...] = (keep[there].astype(jnp.float32) + got[there].astype(jnp.float32)).astype(LOW)


def turn(keep_a, got_a, keep_b, got_b, deps=()):
    return pl.pallas_call(
        partial(turn_kernel, len(deps)),
        out_shape=tuple(
            jax.ShapeDtypeStruct((keep.shape[0] // 2, 128), LOW) for keep in (keep_a, keep_b)
        ),
        in_specs=[VMEM] * 4 + [ANY] * len(deps),
        out_specs=(VMEM,) * 2,
        cost_estimate=FREE,
        compiler_params=pltpu.CompilerParams(vmem_limit_bytes=12 * 2**20),
    )(keep_a, got_a, keep_b, got_b, *deps)


def total_rows(half, running, start, row, rows):
    here = pl.ds(row, rows)
    result = sum(ref[here].astype(jnp.float32) for ref in half)
    if running is not None:
        result = result + running[pl.ds(start + row, rows)].astype(jnp.float32)
    return result


def total_kernel(chained, deps, *refs):
    running = refs[6] if chained else None
    out = refs[6 + chained + deps]
    start = 0
    for half in (refs[:3], refs[3:6]):
        size = half[2].shape[0]
        result = total_rows(half, running, start, 0, size)
        out[pl.ds(start, size)] = result.astype(out.dtype)
        start += size


def total(half_a, half_b, running, deps=()):
    chain = [] if running is None else [running]
    return pl.pallas_call(
        partial(total_kernel, len(chain), len(deps)),
        out_shape=jax.ShapeDtypeStruct((half_a[2].shape[0] + half_b[2].shape[0], 128), LOW),
        in_specs=[VMEM] * (6 + len(chain)) + [ANY] * len(deps),
        out_specs=VMEM,
        cost_estimate=FREE,
        compiler_params=pltpu.CompilerParams(vmem_limit_bytes=12 * 2**20),
    )(*half_a, *half_b, *chain, *deps)


def divided(value, by):
    shift = by.bit_length() - 1
    assert by == 1 << shift
    return lax.shift_right_logical(value, jnp.full_like(value, shift)), value & (by - 1)


def places_of(perm, panel, panels, heads64, ffn64, row_groups):
    col, row = divided(perm, row_groups)
    in_ffn = jnp.maximum(col - 4 * heads64, 0)
    kind, at = divided(col, heads64)
    ffn_kind, ffn_at = divided(in_ffn, ffn64)
    at_head = (kind * panels + panel) * heads64 + at
    at_ffn = 4 * heads64 * panels + (ffn_kind * panels + panel) * ffn64 + ffn_at
    return jnp.where(col < 4 * heads64, at_head, at_ffn) * row_groups + row


def tables_kernel(rings, sizes, at_ref, own_ref, other_ref, come_ref, go_ref):
    z_at, y_at, x_at = at_ref[0], at_ref[1], at_ref[2]
    owned = own_ref.shape[1]
    for sign, out in ((-1, come_ref), (1, go_ref)):
        for k in range(rings):
            z = lax.rem(z_at + sign * k + rings, rings)
            for y in range(2):
                dp = z * 2 + (y_at ^ y)
                for x, perm in enumerate((own_ref, other_ref)):
                    panel = x_at ^ x
                    entry = 4 * k + 2 * y + x
                    out[pl.ds(entry, 1), :] = jnp.full((1, out.shape[1]), dp * 2 + panel, jnp.int32)
                    out[pl.ds(entry, 1), pl.ds(0, owned)] = places_of(
                        perm[pl.ds(dp, 1), :], panel, 2, *sizes
                    )


def tables(at, own, other, rings, sizes):
    shape = jax.ShapeDtypeStruct((rings * 4, own.shape[1] + 16), jnp.int32)
    return pl.pallas_call(
        partial(tables_kernel, rings, sizes),
        out_shape=(shape, shape),
        in_specs=[SMEM, VMEM, VMEM],
        out_specs=(VMEM, VMEM),
        cost_estimate=FREE,
    )(at, own, other)


class Rows:
    def __init__(self, source, target, sems, first=0):
        rows = min(source.shape[0], target.shape[0])
        self.chunk = rows // sems.shape[0]
        self.copies = []
        for i in range(sems.shape[0]):
            here = pl.ds(i * self.chunk, self.chunk)
            there = pl.ds(first + i * self.chunk, self.chunk)
            self.copies.append(pltpu.make_async_copy(source.at[there], target.at[here], sems.at[i]))
        self.done = 0

    def start(self):
        for copy in self.copies:
            copy.start()
        return self

    def upto(self, rows):
        while self.done * self.chunk < rows and self.done < len(self.copies):
            self.copies[self.done].wait()
            self.done += 1

    def whole(self):
        self.upto(self.chunk * len(self.copies))


class Stream:
    def __init__(self, chunks, buffer, sems):
        slots = buffer.shape[0]
        self.buffer = buffer
        self.copies = [
            pltpu.make_async_copy(chunk, buffer.at[i % slots], sems.at[i % slots])
            for i, chunk in enumerate(chunks)
        ]
        self.used = 0
        for copy in self.copies[:slots]:
            copy.start()

    def next(self):
        slots = self.buffer.shape[0]
        ahead = self.used - 1 + slots
        if self.used and ahead < len(self.copies):
            self.copies[ahead].start()
        self.copies[self.used].wait()
        self.used += 1
        return self.buffer.at[(self.used - 1) % slots]


def row_chunks(weight, row, rows, size):
    return [weight.at[pl.ds(row + at, size), :] for at in range(0, rows, size)]


def column_chunks(weight, row, rows, size):
    return [weight.at[pl.ds(row, rows), pl.ds(at, size)] for at in range(0, weight.shape[1], size)]


class Tiles:
    def __init__(self, buffer, sems):
        self.buffer, self.sems, self.under_way = buffer, sems, []

    def put(self, value, target):
        slots = self.buffer.shape[0]
        slot = len(self.under_way) % slots
        if len(self.under_way) >= slots:
            self.under_way[-slots].wait()
        self.buffer[slot] = value
        copy = pltpu.make_async_copy(self.buffer.at[slot], target, self.sems.at[slot])
        copy.start()
        self.under_way.append(copy)

    def drain(self):
        for copy in self.under_way[-self.buffer.shape[0] :]:
            copy.wait()


def vmem(*shape, dtype=LOW):
    return pltpu.VMEM(shape, dtype)


def megabytes(n):
    return pltpu.CompilerParams(vmem_limit_bytes=n * 2**20)


def work(flops, moved=2**22, transcendentals=0):
    return pl.CostEstimate(flops=flops, bytes_accessed=moved, transcendentals=transcendentals)


def project_in_kernel(q_rows, weight, x, bias, out, w, w_sems):
    rows, tile = out.shape[0], w.shape[1]
    chunks = Stream(row_chunks(weight, 0, rows, tile), w, w_sems)
    for at in range(0, rows, tile):
        here = pl.ds(at, tile)
        value = product(chunks.next()[...], x[...], 1, 1) + jnp.transpose(bias[:, here])[:, :1]
        out[here, :] = (value * (DH**-0.5 if at < q_rows else 1.0)).astype(LOW)


def project_in(weights, x, bias):
    rows, width = bias.shape[1], weights.shape[1]
    return pl.pallas_call(
        partial(project_in_kernel, rows // 3),
        out_shape=jax.ShapeDtypeStruct((rows, x.shape[0]), LOW),
        in_specs=[ANY, VMEM, VMEM],
        out_specs=VMEM,
        scratch_shapes=[vmem(3, min(rows // 3, 512), width), sems(3)],
        compiler_params=megabytes(12),
        cost_estimate=work(2 * rows * x.shape[0] * x.shape[1]),
    )(in_hbm(weights), x, bias)


def project_kernel(row, deps, where_ref, context, weight, *refs):
    mine, theirs, w, w_sems, tiles, tile_sems = refs[deps:]
    loader = Rows(weight, w, w_sems, row).start()
    loader.whole()
    half = mine.shape[0]
    leaving = Tiles(tiles, tile_sems)
    for i, out in ((1, theirs), (0, mine)):
        at = pl.multiple_of((where_ref[0] ^ i) * half, half)
        leaving.put(product(context[:, pl.ds(at, half)], w[...], 0, 0).astype(LOW), out)
    leaving.drain()


def project(where, context, weights, row, deps=(), cost=None):
    features, tokens = context.shape
    width = weights.shape[1]
    out = pltpu.HBM((tokens // 2, width), LOW)
    return pl.pallas_call(
        partial(project_kernel, row, len(deps)),
        out_shape=(out, out),
        in_specs=[SMEM, VMEM, ANY] + [ANY] * len(deps),
        out_specs=(ANY, ANY),
        scratch_shapes=[
            vmem(features, width),
            sems(4),
            vmem(2, tokens // 2, width),
            sems(2),
        ],
        compiler_params=megabytes(14),
        cost_estimate=cost or work(2 * features * tokens * width),
    )(where[None], context, in_hbm(weights), *deps)


def ffn_kernel(parts, row, *refs):
    inputs, (weight, bias), refs = refs[:parts], refs[parts : parts + 2], refs[parts + 2 :]
    values, slopes, outs = refs[:parts], refs[parts : 2 * parts], refs[2 * parts : 3 * parts]
    first, first_sems, second, second_sems = refs[3 * parts :]
    hidden, tile = bias.shape[1], first.shape[1]
    chunks = Stream(row_chunks(weight, row, hidden, tile), first, first_sems)
    columns = Stream(
        column_chunks(weight, row + hidden, hidden, second.shape[2]), second, second_sems
    )
    for at in range(0, hidden, tile):
        here = pl.ds(at, tile)
        w = chunks.next()
        for i, x in enumerate(inputs):
            before = product(x[...], w[...], 1, 1) + bias[:, here]
            result, derivative = gelu_pair(before)
            values[i][:, here] = result.astype(LOW)
            slopes[i][:, here] = derivative.astype(LOW)
    finish_ffn(columns, values, outs)


def finish_ffn(columns, values, outs):
    tile = columns.buffer.shape[2]
    for at in range(0, outs[0].shape[1], tile):
        w = columns.next()
        for value, out in zip(values, outs):
            out[:, pl.ds(at, tile)] = product(value[...], w[...], 1, 0).astype(LOW)


def ffn_shapes(parts, hidden, width):
    tokens = parts[0].shape[0]
    low = [jax.ShapeDtypeStruct((tokens, hidden), LOW)] * len(parts)
    outs = [jax.ShapeDtypeStruct((tokens, width), LOW)] * len(parts)
    scratch = [vmem(2, min(hidden, 512), width), sems(2), vmem(2, hidden, 256), sems(2)]
    return low, outs, scratch


def ffn(parts, weights, row, bias):
    hidden, width, n = bias.shape[1], weights.shape[1], len(parts)
    low, outs, scratch = ffn_shapes(parts, hidden, width)
    result = pl.pallas_call(
        partial(ffn_kernel, n, row),
        out_shape=tuple(low + low + outs),
        in_specs=[VMEM] * n + [ANY, VMEM],
        out_specs=(VMEM,) * (3 * n),
        scratch_shapes=scratch,
        compiler_params=megabytes(SCOPED),
        cost_estimate=work(4 * SLOTS * hidden * width, 2**24, SLOTS * hidden),
    )(*parts, in_hbm(weights), bias)
    return result[:n], result[n : 2 * n], result[2 * n :]


def ffn_back_kernel(parts, row, *refs):
    inputs, weight, slopes = refs[:parts], refs[parts], refs[parts + 1 : 2 * parts + 1]
    refs = refs[2 * parts + 1 :]
    grads, outs, sums = refs[:parts], refs[parts : 2 * parts], refs[2 * parts]
    first, first_sems, second, second_sems = refs[2 * parts + 1 :]
    hidden, tile = sums.shape[1], first.shape[1]
    chunks = Stream(row_chunks(weight, row + hidden, hidden, tile), first, first_sems)
    columns = Stream(column_chunks(weight, row, hidden, second.shape[2]), second, second_sems)
    for at in range(0, hidden, tile):
        here = pl.ds(at, tile)
        w = chunks.next()
        total = 0.0
        for x, slope, grad in zip(inputs, slopes, grads):
            result = product(x[...], w[...], 1, 1) * slope[:, here].astype(jnp.float32)
            grad[:, here] = result.astype(LOW)
            total = total + jnp.sum(result, axis=0, keepdims=True)
        sums[:, here] = jnp.broadcast_to(total, (sums.shape[0], tile))
    finish_ffn(columns, grads, outs)


def ffn_back(parts, weights, row, slopes):
    hidden, width, n = slopes[0].shape[1], weights.shape[1], len(parts)
    low, outs, scratch = ffn_shapes(parts, hidden, width)
    result = pl.pallas_call(
        partial(ffn_back_kernel, n, row),
        out_shape=tuple(low + outs) + (jax.ShapeDtypeStruct((8, hidden), jnp.float32),),
        in_specs=[VMEM] * n + [ANY] + [VMEM] * n,
        out_specs=(VMEM,) * (2 * n + 1),
        scratch_shapes=scratch,
        compiler_params=megabytes(SCOPED),
        cost_estimate=work(4 * SLOTS * hidden * width, 2**24),
    )(*parts, in_hbm(weights), *slopes)
    return result[:n], result[n : 2 * n], result[-1]


def ffn_grad_kernel(parts, row, *refs):
    values, upper, grads, lower = (refs[i * parts : (i + 1) * parts] for i in range(4))
    out, tiles, tile_sems = refs[4 * parts :]
    leaving = Tiles(tiles, tile_sems)
    hidden, tile = values[0].shape[1], tiles.shape[1]
    for lefts, rights, begin in ((values, upper, row + hidden), (grads, lower, row)):
        for at in range(0, hidden, tile):
            here = pl.ds(at, tile)
            value = sum(product(a[:, here], b[...], 0, 0) for a, b in zip(lefts, rights))
            leaving.put(value.astype(LOW), out.at[pl.ds(begin + at, tile), :])
    leaving.drain()


def ffn_grad(values, upper, grads, lower, shape, row):
    n, hidden, width = len(values), values[0].shape[1], shape[1]
    return pl.pallas_call(
        partial(ffn_grad_kernel, n, row),
        out_shape=pltpu.HBM(shape, LOW),
        in_specs=[VMEM] * (4 * n),
        out_specs=ANY,
        scratch_shapes=[vmem(2, min(hidden, 512), width), sems(2)],
        compiler_params=megabytes(SCOPED),
        cost_estimate=work(4 * SLOTS * hidden * width, 2**24),
    )(*values, *upper, *grads, *lower)


def project_back_kernel(
    row, deps, where_ref, weight, context, own, other, *refs
):
    out, grad, w, w_sems, h, h_sems, c, c_sems, b, sem = refs[deps:]
    loader = Rows(weight, w, w_sems, row).start()
    hidden = [Rows(part, h.at[i], h_sems.at[i]).start() for i, part in enumerate((own, other))]
    context_rows = Rows(context, c, c_sems).start()
    half = own.shape[0]
    columns = [pl.ds(pl.multiple_of((where_ref[0] ^ i) * half, half), half) for i in range(2)]
    loader.whole()
    for i in range(2):
        hidden[i].whole()
        out[:, columns[i]] = product(w[...], h[i], 1, 1).astype(LOW)
    context_rows.whole()
    b[...] = sum(product(c[:, columns[i]], h[i], 1, 0) for i in range(2)).astype(LOW)
    copy = pltpu.make_async_copy(b, grad.at[pl.ds(row, b.shape[0]), :], sem.at[0])
    copy.start()
    copy.wait()


def project_back(where, weights, context, own, other, row, deps=()):
    features, tokens = context.shape
    width = own.shape[1]
    return pl.pallas_call(
        partial(project_back_kernel, row, len(deps)),
        out_shape=(
            jax.ShapeDtypeStruct((features, tokens), LOW),
            pltpu.HBM(weights.shape, LOW),
        ),
        in_specs=[SMEM] + [ANY] * (4 + len(deps)),
        out_specs=(VMEM, ANY),
        scratch_shapes=[
            vmem(features, width),
            sems(2),
            vmem(2, tokens // 2, width),
            pltpu.SemaphoreType.DMA((2, 2)),
            vmem(features, tokens),
            sems(2),
            vmem(features, width),
            sems(1),
        ],
        compiler_params=megabytes(SCOPED),
        cost_estimate=work(4 * features * tokens * width),
    )(where[None], *[in_hbm(v) for v in (weights, context, own, other)], *deps)


def last_grad_kernel(left, right, _, out, sums, tiles, tile_sems):
    leaving = Tiles(tiles, tile_sems)
    tile = tiles.shape[1]
    for at in range(0, left.shape[0], tile):
        here = pl.ds(at, tile)
        leaving.put(product(left[here, :], right[...], 1, 0).astype(LOW), out.at[here, :])
    sums[...] = product(jnp.ones((sums.shape[0], left.shape[1]), LOW), left[...], 1, 1)
    leaving.drain()


def last_grad(left, right, grads):
    rows, tokens = left.shape
    width = right.shape[1]
    tile = rows // 2
    return pl.pallas_call(
        last_grad_kernel,
        out_shape=(pltpu.HBM(grads.shape, LOW), jax.ShapeDtypeStruct((8, rows), jnp.float32)),
        in_specs=[VMEM, VMEM, ANY],
        out_specs=(ANY, VMEM),
        scratch_shapes=[vmem(2, tile, width), sems(2)],
        compiler_params=megabytes(SCOPED),
        cost_estimate=work(2 * rows * tokens * width),
        input_output_aliases={2: 0},
    )(left, right, in_hbm(grads))


BIAS_OUTPUT, BIAS_OUTER, GAIN_ONE, SHIFT_ONE, GAIN_TWO, SHIFT_TWO = range(6)


def row_of(vectors, i):
    return vectors[pl.ds(i, 1), :]


def mean_of(value):
    return jnp.mean(value, axis=-1, keepdims=True)


def widened(here, *refs):
    return sum(ref[here, :].astype(jnp.float32) for ref in refs)


def norm_one_step(here, vectors, x, mine, got, middle, scaled, inverse):
    hidden = widened(here, x, mine, got) + row_of(vectors, BIAS_OUTPUT)
    center = hidden - mean_of(hidden)
    factor = lax.rsqrt(mean_of(center * center) + 1e-05)
    normal = center * factor
    middle[here, :] = (
        normal * row_of(vectors, GAIN_ONE) + row_of(vectors, SHIFT_ONE)
    ).astype(LOW)
    scaled[here, :] = normal.astype(LOW)
    inverse[here, :] = jnp.broadcast_to(factor, (factor.shape[0], 128))
    return ()


def back_through(upstream, normal, factor, gain):
    gained = upstream * gain
    return factor * (gained - mean_of(gained) - normal * mean_of(gained * normal))


def norm_two_step(here, vectors, middle, mine, got, upstream, layer, dz):
    outer = widened(here, middle, mine, got) + row_of(vectors, BIAS_OUTER)
    center = outer - mean_of(outer)
    factor = lax.rsqrt(mean_of(center * center) + 1e-05)
    normal = center * factor
    gain = row_of(vectors, GAIN_TWO)
    layer[here, :] = (normal * gain + row_of(vectors, SHIFT_TWO)).astype(LOW)
    dy = widened(here, upstream)
    result = back_through(dy, normal, factor, gain)
    dz[here, :] = result.astype(LOW)
    return (result, dy * normal, dy)


def norm_back_step(here, vectors, dz, mine, got, scaled, inverse, dhidden):
    dy = widened(here, dz, mine, got)
    normal = widened(here, scaled)
    factor = inverse[here, :][:, :1]
    result = back_through(dy, normal, factor, row_of(vectors, GAIN_ONE))
    dhidden[here, :] = result.astype(LOW)
    return (result, dy * normal, dy)


def eight_rows(value):
    return sum(value[i : i + 8] for i in range(0, value.shape[0], 8))


def layer_kernel(
    x, mine, got, upstream, vectors, bias, w_own, w_other,
    layer, dhidden, sums, inner, g_own, g_other,
    x_in, mine_in, got_in, up_in, in_sems, act, slope, mid, normal, inverse, dz, acc, out,
    out_sems, one, one_sems, two, two_sems, tile_one, tile_one_sems, tile_two, tile_two_sems,
):
    rows = x.shape[0]
    half, tile = w_own.shape[0] // 2, one.shape[1]
    ones = [c for w in (w_own, w_other) for c in row_chunks(w, 0, half, tile)]
    twos = [c for w in (w_own, w_other) for c in row_chunks(w, half, half, tile)]
    arriving = [
        Rows(source, target, in_sems.at[i])
        for i, (source, target) in enumerate(
            ((x, x_in), (mine, mine_in), (got, got_in), (upstream, up_in))
        )
    ]
    for copies in arriving[:3]:
        copies.start()
    first, second = Stream(ones + ones, one, one_sems), Stream(twos + twos, two, two_sems)
    arriving[3].start()
    step = arriving[0].chunk
    places = [pl.ds(at, step) for at in range(0, rows, step)]

    for at in range(0, rows, FINE):
        for copies in arriving[:3]:
            copies.upto(at + FINE)
        norm_one_step(pl.ds(at, FINE), vectors, x_in, mine_in, got_in, mid, normal, inverse)

    before = product(mid[...], first.next()[...], 1, 1) + bias[:, pl.ds(0, tile)]
    for n in range(len(ones)):
        columns = pl.ds(n * tile, tile)
        down_weight = second.next()
        if n + 1 < len(ones):
            up_weight = first.next()
            after = product(mid[...], up_weight[...], 1, 1) + bias[:, pl.ds((n + 1) * tile, tile)]
        value, derivative = gelu_pair(before)
        before = after
        value = value.astype(LOW)
        act[:, columns] = value
        slope[:, columns] = derivative.astype(LOW)
        part = product(value, down_weight[...], 1, 0)
        if n:
            acc[...] += part
        else:
            acc[...] = part

    arriving[3].whole()
    leaving, totals = [], []
    for at in range(0, rows, FINE):
        here = pl.ds(at, FINE)
        outer = acc[here, :] + widened(here, mid) + row_of(vectors, BIAS_OUTER)
        center = outer - mean_of(outer)
        factor = lax.rsqrt(mean_of(center * center) + 1e-05)
        scaled = center * factor
        gain = row_of(vectors, GAIN_TWO)
        out[here, :] = (scaled * gain + row_of(vectors, SHIFT_TWO)).astype(LOW)
        dy = widened(here, up_in)
        result = back_through(dy, scaled, factor, gain)
        acc[here, :] = result
        dz[here, :] = result.astype(LOW)
        totals.append([eight_rows(v) for v in (result, dy * scaled, dy)])
        if (at + FINE) % step == 0:
            n = at // step
            leaving.append(
                pltpu.make_async_copy(out.at[places[n]], layer.at[places[n]], out_sems.at[n])
            )
            leaving[-1].start()

    grads_one, grads_two = Tiles(tile_one, tile_one_sems), Tiles(tile_two, tile_two_sems)
    for n in range(len(ones)):
        columns = pl.ds(n * tile, tile)
        target, begin = (g_own, n * tile) if n * tile < half else (g_other, n * tile - half)
        value = product(act[:, columns], dz[...], 0, 0)
        grads_two.put(value.astype(LOW), target.at[pl.ds(half + begin, tile), :])
        grad = product(dz[...], second.next()[...], 1, 1) * slope[:, columns].astype(jnp.float32)
        inner[:, columns] = jnp.broadcast_to(
            jnp.sum(grad, axis=0, keepdims=True), (inner.shape[0], tile)
        )
        slope[:, columns] = grad.astype(LOW)
        value = product(slope[:, columns], mid[...], 0, 0)
        grads_one.put(value.astype(LOW), target.at[pl.ds(begin, tile), :])
        acc[...] += product(slope[:, columns], first.next()[...], 1, 0)

    for at in range(0, rows, FINE):
        here = pl.ds(at, FINE)
        dy = acc[here, :]
        scaled = widened(here, normal)
        factor = inverse[here, :][:, :1]
        result = back_through(dy, scaled, factor, row_of(vectors, GAIN_ONE))
        got_in[here, :] = result.astype(LOW)
        totals.append([eight_rows(v) for v in (result, dy * scaled, dy)])
        if (at + FINE) % step == 0:
            n = at // step
            leaving.append(
                pltpu.make_async_copy(got_in.at[places[n]], dhidden.at[places[n]], in_sems.at[2, n])
            )
            leaving[-1].start()
    count = rows // FINE
    lines = [
        jnp.sum(sum(t[i] for t in part), axis=0, keepdims=True)
        for part in (totals[:count], totals[count:])
        for i in range(3)
    ]
    sums[...] = jnp.concatenate(lines + [jnp.zeros_like(lines[0])] * 2, axis=0)
    grads_one.drain()
    grads_two.drain()
    for copy in leaving:
        copy.wait()


def layer_part(x, mine, got, upstream, vectors, bias, w_own, w_other):
    rows, width = x.shape
    hidden = bias.shape[1]
    tile = WIDE
    low = jax.ShapeDtypeStruct((rows, width), LOW)
    grad = pltpu.HBM(w_own.shape, LOW)
    dma = pltpu.SemaphoreType.DMA
    return pl.pallas_call(
        layer_kernel,
        out_shape=(
            low,
            pltpu.HBM((rows, width), LOW),
            jax.ShapeDtypeStruct((8, width), jnp.float32),
            jax.ShapeDtypeStruct((8, hidden), jnp.float32),
            grad,
            grad,
        ),
        in_specs=[ANY] * 4 + [VMEM] * 2 + [ANY] * 2,
        out_specs=(ANY, ANY, VMEM, VMEM, ANY, ANY),
        scratch_shapes=[vmem(rows, width) for _ in range(4)]
        + [
            dma((4, 4)),
            vmem(rows, hidden),
            vmem(rows, hidden),
            vmem(rows, width),
            vmem(rows, width),
            vmem(rows, 128, dtype=jnp.float32),
            vmem(rows, width),
            vmem(rows, width, dtype=jnp.float32),
            vmem(rows, width),
            sems(4),
            vmem(2, tile, width),
            sems(2),
            vmem(2, tile, width),
            sems(2),
            vmem(1, tile, width),
            sems(1),
            vmem(1, tile, width),
            sems(1),
        ],
        compiler_params=megabytes(50),
        cost_estimate=work(12 * rows * hidden * width, 2**25, rows * hidden),
    )(in_hbm(x), in_hbm(mine), got, in_hbm(upstream), vectors, bias, in_hbm(w_own), in_hbm(w_other))


def rows_kernel(step, count, with_sums, vectors, *refs):
    inputs, outs = refs[:count], refs[count:]
    if with_sums:
        sums, outs = outs[-1], outs[:-1]
    rows = inputs[0].shape[0]
    tile = min(rows, 128)
    totals = 0
    for at in range(0, rows, tile):
        values = step(pl.ds(at, tile), vectors, *inputs, *outs)
        if with_sums:
            parts = [jnp.sum(value, axis=0, keepdims=True) for value in values]
            totals = totals + jnp.concatenate(parts + [jnp.zeros_like(parts[0])] * 5, axis=0)
    if with_sums:
        sums[...] = totals


def by_rows(step, inputs, vectors, outs, with_sums):
    rows, width = inputs[0].shape
    shapes = [jax.ShapeDtypeStruct((rows, n), dtype) for n, dtype in outs]
    if with_sums:
        shapes.append(jax.ShapeDtypeStruct((8, width), jnp.float32))
    return pl.pallas_call(
        partial(rows_kernel, step, len(inputs), with_sums),
        out_shape=tuple(shapes),
        in_specs=[VMEM] * (1 + len(inputs)),
        out_specs=(VMEM,) * len(shapes),
        compiler_params=megabytes(12),
        cost_estimate=work(40 * rows * width, 2**23, rows),
    )(vectors, *inputs)


def shampoo_blocks(scale, grad, left_root, right_root, left, right, weight, outs):
    new_left, new_right, new_weight = outs
    for i in range(grad.shape[0]):
        g = grad[i].astype(LOW)
        new_left[i] = 0.5 * left[i] + (0.5 * scale) * product(g, g, 0, 0)
        new_right[i] = 0.5 * right[i] + (0.5 * scale) * product(g, g, 1, 1)
        step = product(g, left_root[i].astype(LOW), 1, 1)
        step = product(right_root[i].astype(LOW), step.astype(LOW), 0, 0)
        here = weight[i]
        size = jnp.sqrt(jnp.mean(here * here, keepdims=True) + 1e-06)
        norm = jnp.sqrt(jnp.mean(step * step, keepdims=True) + 1e-06)
        new_weight[i] = here - (0.3 * size / norm) * step


def shampoo_kernel(scale, *refs):
    grad, inputs, outs = refs[0], refs[1:6], refs[6:]
    shampoo_blocks(scale, grad, *inputs, outs)


def last_kernel(scale, *refs):
    halves, running, inputs = (refs[:3], refs[3:6]), refs[6], refs[7:12]
    grad, extra, outs = refs[12], refs[13], refs[14:]
    blocks = grad.shape[0]
    at = pl.program_id(0)
    rows_a = halves[0][2].shape[0] - EXTRA
    steps_a = rows_a // (blocks * DH)

    def take(half, start, step):
        row = pl.multiple_of(step * blocks * DH, blocks * DH)
        value = total_rows(half, running, start, row, blocks * DH)
        grad[...] = value.reshape(blocks, DH, 128)

    @pl.when(at < steps_a)
    def _():
        take(halves[0], 0, at)

    @pl.when(at >= steps_a)
    def _():
        take(halves[1], rows_a + EXTRA, at - steps_a)

    extra[...] = total_rows(halves[0], running, 0, rows_a, EXTRA)
    shampoo_blocks(scale, grad, *inputs, outs)


def shampoo_specs(tile, values):
    return [pl.BlockSpec((tile,) + v.shape[1:], lambda i: (i, 0, 0)) for v in values]


def shampoo(scale, grad, *state):
    owned = grad.shape[0]
    tile = 8 if owned % 8 == 0 else owned
    return pl.pallas_call(
        partial(shampoo_kernel, scale),
        out_shape=tuple(jax.ShapeDtypeStruct(v.shape, jnp.float32) for v in state[2:]),
        grid=(owned // tile,),
        in_specs=shampoo_specs(tile, (grad, *state)),
        out_specs=tuple(shampoo_specs(tile, state[2:])),
        compiler_params=megabytes(16),
    )(grad, *state)


def last_step(scale, half_a, half_b, running, *state):
    owned = state[0].shape[0]
    tile = 8
    grad = jax.ShapeDtypeStruct((owned, DH, 128), jnp.float32)
    return pl.pallas_call(
        partial(last_kernel, scale),
        out_shape=(grad, jax.ShapeDtypeStruct((EXTRA, 128), jnp.float32))
        + tuple(jax.ShapeDtypeStruct(v.shape, jnp.float32) for v in state[2:]),
        grid=(owned // tile,),
        in_specs=[
            pl.BlockSpec(v.shape, lambda i: (0, 0)) for v in (*half_a, *half_b, running)
        ]
        + shampoo_specs(tile, state),
        out_specs=(
            *shampoo_specs(tile, (grad,)),
            pl.BlockSpec((EXTRA, 128), lambda i: (0, 0)),
            *shampoo_specs(tile, state[2:]),
        ),
        compiler_params=megabytes(32),
    )(*half_a, *half_b, running, *state)


class Fabric:
    def __init__(self, sizes, row_ways):
        self.batch, self.model = sizes
        self.ways = row_ways
        self.panels = self.model // row_ways
        self.wide = row_ways == 2 and self.panels == 2 and self.batch % 2 == 0
        self.row_groups = [
            list(range(i, i + row_ways)) for i in range(0, self.model, row_ways)
        ]
        self.same_groups = [list(range(t, self.model, row_ways)) for t in range(row_ways)]

    def send(self, value, move):
        pairs = []
        for d in range(self.batch):
            for m in range(self.model):
                e, n = move(d, m)
                pairs.append((d * self.model + m, (e % self.batch) * self.model + n))
        return lax.ppermute(value, BOTH, pairs)

    def to_core(self, value):
        return self.send(value, lambda d, m: (d, m ^ 1))

    def to_x(self, value):
        return self.send(value, lambda d, m: (d, m ^ 2))

    def to_y(self, value):
        return self.send(value, lambda d, m: (d ^ 1, m))

    def to_z(self, value):
        return self.send(value, lambda d, m: (d + 2, m))

    def row_gather(self, own):
        if self.wide:
            return self.join(self.share(own), 0)
        return lax.all_gather(own, "mp", axis=0, tiled=True, axis_index_groups=self.row_groups)

    def share(self, own):
        if self.wide:
            return [own, self.to_core(own)]
        return [self.row_gather(own)]

    def gather_back(self, parts):
        if self.wide:
            return parts[0].astype(LOW), self.to_core(parts[1].astype(LOW))
        mine = lax.psum_scatter(
            parts[0].astype(LOW),
            "mp",
            scatter_dimension=0,
            tiled=True,
            axis_index_groups=self.row_groups,
        )
        return mine, jnp.zeros(mine.shape, LOW)

    def cut(self, value, axis):
        if not self.wide:
            return [value]
        size = value.shape[axis] // 2
        core = lax.rem(lax.axis_index("mp"), 2)
        return [
            lax.dynamic_slice_in_dim(value, at * size, size, axis) for at in (core, 1 - core)
        ]

    def join(self, parts, axis):
        if not self.wide:
            return parts[0]
        own, other = parts
        first = lax.rem(lax.axis_index("mp"), 2) == 0
        return jnp.concatenate(
            [jnp.where(first, own, other), jnp.where(first, other, own)], axis=axis
        )

    def row_sum(self, value):
        if self.wide:
            return value + self.to_core(value)
        return lax.psum(value, "mp", axis_index_groups=self.row_groups)


def shards(
    sizes,
    x_in,
    out_grad,
    item_lengths,
    weight_store,
    owner_perm,
    left_roots,
    right_roots,
    left_stats,
    right_stats,
    head_vectors,
    head_first,
    head_second,
    shared_vectors,
    shared_first,
    shared_second,
):
    batch_ways, model_ways = sizes
    shard_rows, model_width = x_in.shape
    fabric = Fabric(sizes, SLOTS // shard_rows)
    ways, panels, wide = fabric.ways, fabric.panels, fabric.wide
    dp_at, mp_at = lax.axis_index("dp"), lax.axis_index("mp")
    row_at, place_at = lax.div(mp_at, ways), lax.rem(mp_at, ways)

    owned, row_block, col_block = weight_store.shape[1:]
    head_part, shared_part = head_vectors.shape[1], shared_vectors.shape[0]
    head_count, shared_count = head_part * batch_ways, shared_part * batch_ways * model_ways
    block_count = owner_perm.shape[1]
    row_groups = model_width // row_block
    head_width = model_width // model_ways
    ffn_total = shared_count - 6 * model_width
    ffn_width = ffn_total // model_ways
    heads64, ffn64 = head_width // DH, ffn_width // DH
    hidden_rows = panels * (4 * head_width + 2 * ffn_width)
    q_rows, f_rows = panels * head_width, panels * ffn_width
    panel_shape = (hidden_rows, model_width)
    panel_shapes = ((4 * q_rows, model_width), (2 * f_rows, model_width))
    half_a = (owned // 2) * DH + EXTRA
    blocks_a, blocks_b = owned // 2, owned - owned // 2

    def two_parts(value):
        high = lax.reduce_precision(value, 8, 7)
        return jnp.concatenate([high.astype(LOW), (value - high).astype(LOW)])

    blocks_low = jnp.swapaxes(weight_store[0], 1, 2).astype(LOW).reshape(owned * DH, 128)
    vectors = jnp.concatenate([two_parts(head_vectors[0]), two_parts(shared_vectors)])
    vectors = jnp.pad(vectors, (0, EXTRA * 128 - vectors.shape[0])).reshape(EXTRA, 128)
    own = jnp.concatenate(
        [blocks_low[: blocks_a * DH], vectors, blocks_low[blocks_a * DH :]], axis=0
    )

    layout = (heads64, ffn64, row_groups)
    perm = owner_perm.reshape(batch_ways, owned)
    if wide:
        perm_other = fabric.to_x(perm)
    else:
        perm_all = lax.all_gather(perm, "mp", axis=0, axis_index_groups=fabric.same_groups)
        panel_ids = jnp.arange(panels, dtype=jnp.int32)[:, None, None]
        places = places_of(perm_all, panel_ids, panels, *layout)

    if wide:
        rings = batch_ways // 2
        z_at, y_at = lax.div(dp_at, 2), lax.rem(dp_at, 2)
        table, table_back = tables(
            jnp.stack([z_at, y_at, row_at]), perm, perm_other, rings, layout
        )
        low_half, high_half = (0, 0, blocks_a), (half_a, blocks_a, blocks_b)
        at_extra = blocks_a * DH

        def piece(entry, *halves):
            return [(row, entry, first, count) for row, first, count in halves]

        def near_of(k):
            return [
                (value, piece(4 * k + i, low_half, high_half), at_extra)
                for i, value in enumerate((ring, by_x, by_y))
            ]

        def far_of(k):
            return [
                (far_a[k], piece(4 * k + 3, low_half), at_extra),
                (far_b[k], piece(4 * k + 3, (0, blocks_a, blocks_b)), None),
            ]

        near, far_a, far_b = [], [], []
        ring = own
        for k in range(rings):
            if k:
                deps = [table] if k == 1 else [far_a[k - 2], far_b[k - 2]]
                ring = gate(after, [by_x, by_y] + deps, pltpu.VMEM)
            after = fabric.to_z(ring) if k + 1 < rings else None
            by_x, by_y = fabric.to_x(ring), fabric.to_y(ring)
            near.append(near_of(k))
            if k:
                low, high = halves(*last, half_a, [ring])
                far_a.append(fabric.to_x(low))
                far_b.append(fabric.to_y(high))
            last = (by_y, by_x)
        placed = None
        for k in range(rings - 1):
            parts = near[k] + (far_of(k - 1) if k else [])
            placed = place(table, *zip(*parts), panel_shapes, placed, [low])
        low, high = halves(*last, half_a, [far_a[-1], far_b[-1], placed[2]])
        far_a.append(fabric.to_x(low))
        far_b.append(fabric.to_y(high))
        placed = place(
            table, *zip(*(near[-1] + far_of(rings - 2))), panel_shapes, placed, [low]
        )
        w_near, w_ffn, extras = place(table, *zip(*far_of(rings - 1)), panel_shapes, placed)
        extras = extras.astype(jnp.float32)
    else:
        gathered = lax.all_gather(own, "mp", axis=0, axis_index_groups=fabric.same_groups)
        gathered = lax.all_gather(gathered, "dp", axis=0)
        entries = batch_ways * panels
        table = places.transpose(1, 0, 2).reshape(entries, owned)
        index = jnp.arange(entries, dtype=jnp.int32)[:, None]
        table = jnp.concatenate([table, jnp.broadcast_to(index, (entries, 16))], axis=1)
        extras = gathered[:, :, blocks_a * DH : half_a].astype(jnp.float32)
        stride = own.shape[0]
        flat = gathered.reshape(-1, 128)
        pieces = []
        for i in range(batch_ways * panels):
            pieces += [(i * stride, i, 0, blocks_a), (i * stride + half_a, i, blocks_a, blocks_b)]
        w_near, w_ffn, _ = place(table, [flat], [pieces], [None], panel_shapes)
        weights = jnp.concatenate([w_near, w_ffn], axis=0)

    extras = extras.reshape(batch_ways, panels, EXTRA * 128)
    head_all = extras[:, :, :head_part] + extras[:, :, head_part : 2 * head_part]
    begin = 2 * head_part
    shared_all = (
        extras[:, :, begin : begin + shared_part]
        + extras[:, :, begin + shared_part : begin + 2 * shared_part]
    )
    head_all = head_all.transpose(1, 0, 2).reshape(panels, head_count)
    if wide:
        shared_other = fabric.to_core(shared_all)
        first = place_at == 0
        shared = jnp.stack(
            [
                jnp.where(first, shared_all, shared_other),
                jnp.where(first, shared_other, shared_all),
            ],
            axis=2,
        )
    else:
        shared = lax.all_gather(
            shared_all, "mp", axis=0, axis_index_groups=fabric.row_groups
        ).transpose(1, 2, 0, 3)
    shared = shared.reshape(shared_count)

    bias_query = head_all[:, :head_width].reshape(q_rows)
    bias_value = head_all[:, head_width:].reshape(q_rows)
    bias_qkv = jnp.concatenate([bias_query, jnp.zeros((q_rows,), jnp.float32), bias_value])
    vectors = jnp.pad(shared[: 6 * model_width].reshape(6, model_width), ((0, 2), (0, 0)))
    bias_inner = shared[6 * model_width :].reshape(panels, ways, ffn_width)
    bias_local = lax.dynamic_index_in_dim(bias_inner, place_at, 1, keepdims=False).reshape(f_rows)
    if wide:
        bias_other = lax.dynamic_index_in_dim(bias_inner, 1 - place_at, 1, keepdims=False)
        bias_both = jnp.concatenate([bias_local, bias_other.reshape(f_rows)])

    lengths = lax.dynamic_index_in_dim(item_lengths, row_at, 0, keepdims=False)
    starts = jnp.cumsum(lengths) - lengths

    def shared_sums(sums, inner_all):
        lines = [sums[i] for i in (3, 0, 4, 5, 1, 2)] + [inner_all.reshape(ffn_total)]
        whole = fabric.row_sum(jnp.concatenate(lines))
        whole = whole.reshape(batch_ways, panels, ways, shared_part)
        return lax.dynamic_index_in_dim(whole, place_at, 2, keepdims=False)

    x_row = fabric.row_gather(x_in)
    bias_qkv = jnp.broadcast_to(bias_qkv[None], (8, 3 * q_rows))
    qkv = project_in(w_near, x_row, bias_qkv).reshape(3, q_rows, SLOTS)
    context, log_total = attend(starts, lengths, qkv)
    if wide:
        w_ffn = gate(w_ffn, [x_row])
        w_ffn_other = fabric.to_core(w_ffn)
        mine, got = fabric.gather_back(
            project(place_at, context, w_near, 3 * q_rows, [vectors, bias_both])
        )
        layer_value, hidden_grad, sums, inner_sums, grad_ffn, grad_ffn_other = layer_part(
            x_in, mine, got, out_grad, vectors, bias_both[None], w_ffn, w_ffn_other
        )
        hidden_parts = fabric.share(hidden_grad)
        inner = [
            part.reshape(panels, ffn_width) for part in (inner_sums[0, :f_rows], inner_sums[0, f_rows:])
        ]
        inner_all = jnp.where(
            place_at == 0, jnp.stack(inner, axis=1), jnp.stack(inner[::-1], axis=1)
        )
        shared_grad = shared_sums(sums, inner_all)
        grad_ffn_got = fabric.to_core(gate(grad_ffn_other, [hidden_parts[1], shared_grad]))
        dcontext, grad_near = project_back(
            place_at, w_near, context, *hidden_parts, 3 * q_rows, [shared_grad]
        )
    else:
        w_out, w_qkv = w_near[3 * q_rows :], w_near[: 3 * q_rows]
        mine, got = fabric.gather_back([product(context, w_out, 0, 0)])
        low = (model_width, LOW)
        middle, middle_scaled, middle_inverse = by_rows(
            norm_one_step, (x_in, mine, got), vectors, (low, low, (128, jnp.float32)), False
        )
        middle_parts = fabric.share(middle)
        activated, slopes, results = ffn(middle_parts, weights, 4 * q_rows, bias_local[None])
        mine, got = fabric.gather_back(results)
        layer_value, resid_grad, sums_two = by_rows(
            norm_two_step, (middle, mine, got, out_grad), vectors, (low, low), True
        )
        resid_parts = fabric.share(resid_grad)
        before_grads, results, inner_sums = ffn_back(resid_parts, weights, 4 * q_rows, slopes)
        mine, got = fabric.gather_back(results)
        hidden_grad, sums_one = by_rows(
            norm_back_step,
            (resid_grad, mine, got, middle_scaled, middle_inverse),
            vectors,
            (low,),
            True,
        )
        grads = ffn_grad(
            activated, resid_parts, before_grads, middle_parts, panel_shape, 4 * q_rows
        )
        hidden_parts = fabric.share(hidden_grad)
        dcontext = product(w_out, hidden_parts[0], 1, 1).astype(LOW)
        part = product(context, hidden_parts[0], 1, 0).astype(LOW)
        grad_near = lax.dynamic_update_slice_in_dim(grads, part, 3 * q_rows, 0)
        sums = jnp.concatenate([sums_two[:3], sums_one[:3]], axis=0)
        inner_all = lax.dynamic_update_slice(
            jnp.zeros((panels, ways, ffn_width), jnp.float32),
            inner_sums[0].reshape(panels, 1, ffn_width),
            (0, place_at, 0),
        )
        shared_grad = shared_sums(sums, inner_all)
    qkv_grad = attend_back(starts, lengths, qkv, context, dcontext, log_total)
    qkv_grad = qkv_grad.reshape(3 * q_rows, SLOTS)
    grad_near, column_sums = last_grad(qkv_grad, x_row, grad_near)
    column_sums = column_sums[0]
    if wide:
        mine, theirs = project(place_at, qkv_grad, w_near, 0)

    head_grad = jnp.concatenate(
        [
            column_sums[:q_rows].reshape(panels, head_width),
            column_sums[2 * q_rows :].reshape(panels, head_width),
        ],
        axis=1,
    )
    head_grad = head_grad.reshape(panels, batch_ways, head_part).transpose(1, 0, 2)
    extra_grad = jnp.concatenate([head_grad, shared_grad], axis=2).astype(LOW)
    extra_grad = jnp.pad(
        extra_grad, ((0, 0), (0, 0), (0, EXTRA * 128 - head_part - shared_part))
    ).reshape(batch_ways * panels, EXTRA, 128)

    if wide:
        half_b = blocks_b * DH

        def low_of(k, entries):
            parts = []
            for i, entry in enumerate(entries):
                parts.append((i * half_a, 4 * k + entry, 0, blocks_a))
                parts.append((i * half_a + blocks_a * DH, 4 * k + entry, 0, 0))
            return parts

        def high_of(k, entries):
            return [
                (i * half_b, 4 * k + entry, blocks_a, blocks_b) for i, entry in enumerate(entries)
            ]

        sent, kept, far, order = {}, {}, {}, []

        def gather(pieces):
            result = fetch(table_back, (grad_near, grad_ffn, grad_ffn_got), extra_grad, pieces, order)
            order[:] = [result[0]]
            return result

        def send(k, after=()):
            send_x, send_y = gather([low_of(k, (1, 3)), high_of(k, (2, 3))])
            if after:
                send_x, send_y = gate(send_x, after), gate(send_y, after)
            sent[k] = fabric.to_x(send_x), fabric.to_y(send_y)

        def keep(k):
            kept[k] = gather([low_of(k, (0, 2)), high_of(k, (0, 1))])

        def pass_on(k):
            sum_a, sum_b = turn(kept[k][0], sent[k][0], kept[k][1], sent[k][1], order)
            far[k] = fabric.to_y(sum_a), fabric.to_x(sum_b)
            order[:] = [sum_a]

        def finish(k, running):
            half = [(kept[k][i], sent[k][i], far[k][i]) for i in range(2)]
            result = total(*half, running, order)
            order[:] = [result]
            return fabric.to_z(result)

        last = rings - 1
        for k in (last, last - 1):
            send(k)
        for k in (last, last - 1):
            keep(k)
        pass_on(last)
        pass_on(last - 1)
        if last > 1:
            send(last - 2)
            keep(last - 2)
        running = finish(last, None)
        for k in range(last - 2, -1, -1):
            pass_on(k)
            if k:
                send(k - 1)
                keep(k - 1)
            running = finish(k + 1, running)
        final = [(kept[0][i], sent[0][i], far[0][i]) for i in range(2)]
    else:
        pieces = []
        for i in range(batch_ways * panels):
            base = i * own.shape[0]
            pieces += [
                (base, i, 0, blocks_a),
                (base + blocks_a * DH, i, 0, 0),
                (base + half_a, i, blocks_a, blocks_b),
            ]
        chunks = fetch_all(table, grad_near, extra_grad, pieces)
        chunks = chunks.reshape(batch_ways, panels, own.shape[0], 128)
        chunks = lax.psum_scatter(chunks, "dp", scatter_dimension=0, tiled=False)
        reduced = lax.psum_scatter(
            chunks,
            "mp",
            scatter_dimension=0,
            tiled=False,
            axis_index_groups=fabric.same_groups,
        ).astype(jnp.float32)

        block_grads = jnp.concatenate([reduced[: blocks_a * DH], reduced[half_a:]], axis=0)
        vector_grads = reduced[blocks_a * DH : half_a]

    scale = 1.0 / (shard_rows * model_ways * batch_ways)
    state = (
        left_roots[0],
        right_roots[0],
        left_stats[0],
        right_stats[0],
        jnp.swapaxes(weight_store[0], 1, 2),
    )
    if wide:
        block_grads, vector_grads, *renewed = last_step(scale, *final, running, *state)
        mine, got = fabric.gather_back((mine, theirs))
    else:
        block_grads = block_grads.reshape(owned, DH, 128)
        renewed = shampoo(scale, block_grads, *state)
        mine, got = fabric.gather_back([product(qkv_grad, w_qkv, 0, 0)])
    new_left, new_right, new_weights = renewed
    input_grad = sum(v.astype(jnp.float32) for v in (hidden_grad, mine, got))
    vector_grads = vector_grads.reshape(EXTRA * 128)
    head_grad_mine = vector_grads[:head_part]
    shared_grad_mine = vector_grads[head_part : head_part + shared_part]

    head_one, head_two, head_new = adam_update(
        head_vectors[0], head_first[0], head_second[0], head_grad_mine
    )
    shared_one, shared_two, shared_new = adam_update(
        shared_vectors, shared_first, shared_second, shared_grad_mine
    )
    return (
        layer_value,
        input_grad,
        jnp.swapaxes(block_grads, 1, 2)[None],
        new_left[None],
        new_right[None],
        jnp.swapaxes(new_weights, 1, 2)[None],
        head_one[None],
        head_two[None],
        head_new[None],
        shared_one,
        shared_two,
        shared_new,
    )


def solution(mesh):
    rows, blocks, vector, head = P(BOTH, None), P("mp", "dp", None, None), P(BOTH), P("mp", "dp")
    return jax.shard_map(
        partial(shards, (mesh.shape["dp"], mesh.shape["mp"])),
        mesh=mesh,
        in_specs=(rows, rows, P("dp", None), blocks, P("mp", None))
        + (blocks,) * 4
        + (head,) * 3
        + (vector,) * 3,
        out_specs=(rows, rows) + (blocks,) * 4 + (head,) * 3 + (vector,) * 3,
        check_vma=False,
    )
```

```python
from functools import partial

import jax
import jax.numpy as jnp
from jax import lax
from jax.experimental import pallas as pl
from jax.experimental.pallas import tpu as pltpu
from jax.sharding import PartitionSpec as P

DH = 64
SLOTS = 1024
STEP = 10
SHORT = 128
LONG = 512
EXTRA = 16
SCOPED = 14
FINE = 32
WIDE = 1024
WHOLE = 2048
LOW = jnp.bfloat16
BOTH = ("dp", "mp")
ANY = pl.BlockSpec(memory_space=pl.ANY)
VMEM = pl.BlockSpec(memory_space=pltpu.VMEM)
SMEM = pl.BlockSpec(memory_space=pltpu.SMEM)
FREE = pl.CostEstimate(flops=0, bytes_accessed=0, transcendentals=0)
TINY = pl.CostEstimate(flops=10**6, bytes_accessed=10**4, transcendentals=0)
MOVE = pl.CostEstimate(flops=0, bytes_accessed=2**24, transcendentals=0)


def sems(n):
    return pltpu.SemaphoreType.DMA((n,))


def in_hbm(value):
    return pltpu.with_memory_space_constraint(value, pltpu.HBM)


def product(left, right, left_dim, right_dim):
    return lax.dot_general(
        left, right, (((left_dim,), (right_dim,)), ((), ())), preferred_element_type=jnp.float32
    )


def adam_update(current, moment_one, moment_two, gradient):
    first_new = 0.9 * moment_one + 0.1 * gradient
    second_new = 0.999 * moment_two + 0.001 * gradient * gradient
    stepped = first_new / (1.0 - 0.9**STEP) / (jnp.sqrt(second_new / (1.0 - 0.999**STEP)) + 1e-08)
    return (first_new, second_new, current - 0.3 * stepped)


def gelu_pair(before):
    below = 0.5 + 0.5 * lax.erf(before * 0.5**0.5)
    slope = below + before * jnp.exp(before * before * -0.5) * 0.3989422804014327
    return before * below, slope


def attend_kernel(start_ref, length_ref, qkv_ref, ctx_ref, lse_ref):
    def item(begin, size):
        here = pl.ds(begin, size)
        for g in range(lse_ref.shape[0]):
            head = pl.ds(g * DH, DH)
            scores = product(qkv_ref[1, head, here], qkv_ref[0, head, here], 0, 0)
            top = jnp.max(scores, axis=0, keepdims=True)
            expo = jnp.exp(scores - top)
            total = jnp.sum(expo, axis=0, keepdims=True)
            ctx = product(qkv_ref[2, head, here], expo.astype(LOW), 1, 0) / total
            ctx_ref[head, here] = ctx.astype(LOW)
            lse_ref[g, :, here] = top + jnp.log(total)

    each_item(start_ref, length_ref, item)


def each_item(start_ref, length_ref, item):
    @pl.loop(0, start_ref.shape[0])
    def _(i):
        begin = pl.multiple_of(start_ref[i], SHORT)

        @pl.when(length_ref[i] == LONG)
        def _():
            item(begin, LONG)

        @pl.when(length_ref[i] == SHORT)
        def _():
            item(begin, SHORT)


def attend_back_kernel(
    start_ref, length_ref, qkv_ref, ctx_ref, dctx_ref, lse_ref, out_ref
):
    def item(begin, size):
        here = pl.ds(begin, size)
        for g in range(lse_ref.shape[0]):
            head = pl.ds(g * DH, DH)
            queries, keys, values = (qkv_ref[i, head, here] for i in range(3))
            dctx = dctx_ref[head, here]
            probs = jnp.exp(product(keys, queries, 0, 0) - lse_ref[g, :, here])
            dprobs = product(values, dctx, 0, 0)
            delta = jnp.sum(
                dctx.astype(jnp.float32) * ctx_ref[head, here].astype(jnp.float32),
                axis=0,
                keepdims=True,
            )
            dscores = (probs * (dprobs - delta)).astype(LOW)
            out_ref[0, head, here] = (product(keys, dscores, 1, 0) * DH**-0.5).astype(LOW)
            out_ref[1, head, here] = product(queries, dscores, 1, 1).astype(LOW)
            out_ref[2, head, here] = product(dctx, probs.astype(LOW), 1, 1).astype(LOW)

    each_item(start_ref, length_ref, item)


def attend(starts, lengths, qkv):
    heads = qkv.shape[1] // DH
    group = min(heads, 2)
    return pl.pallas_call(
        attend_kernel,
        out_shape=(
            jax.ShapeDtypeStruct(qkv.shape[1:], LOW),
            jax.ShapeDtypeStruct((heads, 1, SLOTS), jnp.float32),
        ),
        grid_spec=pltpu.PrefetchScalarGridSpec(
            num_scalar_prefetch=2,
            grid=(heads // group,),
            in_specs=[pl.BlockSpec((3, group * DH, SLOTS), lambda h, *_: (0, h, 0))],
            out_specs=(
                pl.BlockSpec((group * DH, SLOTS), lambda h, *_: (h, 0)),
                pl.BlockSpec((group, 1, SLOTS), lambda h, *_: (h, 0, 0)),
            ),
        ),
        compiler_params=pltpu.CompilerParams(vmem_limit_bytes=12 * 2**20),
        cost_estimate=pl.CostEstimate(
            flops=heads * SLOTS * LONG * 1024, bytes_accessed=2**22, transcendentals=heads * 2**19
        ),
    )(starts, lengths, qkv)


def attend_back(starts, lengths, qkv, ctx, dctx, lse):
    heads = qkv.shape[1] // DH
    group = min(heads, 2)
    one = pl.BlockSpec((group * DH, SLOTS), lambda h, *_: (h, 0))
    three = pl.BlockSpec((3, group * DH, SLOTS), lambda h, *_: (0, h, 0))
    return pl.pallas_call(
        attend_back_kernel,
        out_shape=jax.ShapeDtypeStruct(qkv.shape, LOW),
        grid_spec=pltpu.PrefetchScalarGridSpec(
            num_scalar_prefetch=2,
            grid=(heads // group,),
            in_specs=[three, one, one, pl.BlockSpec((group, 1, SLOTS), lambda h, *_: (h, 0, 0))],
            out_specs=three,
        ),
        compiler_params=pltpu.CompilerParams(vmem_limit_bytes=14 * 2**20),
        cost_estimate=pl.CostEstimate(
            flops=heads * SLOTS * LONG * 2560, bytes_accessed=2**23, transcendentals=heads * 2**19
        ),
    )(starts, lengths, qkv, ctx, dctx, lse)


def tile_at(ref, place, groups):
    shift = groups.bit_length() - 1
    row = pl.multiple_of(lax.shift_right_logical(place, shift) * DH, DH)
    col = pl.multiple_of((place & (groups - 1)) * 128, 128)
    return ref.at[pl.ds(row, DH), pl.ds(col, 128)]


def place_kernel(pieces, extra_rows, count, more, table_ref, *refs):
    sources, refs = refs[:count], refs[count + more :]
    near_ref, ffn_ref, extra_ref = refs[:3]
    buffers, sems = refs[3:-1], refs[-1]
    arriving = [
        pltpu.make_async_copy(source, buffer, sems.at[2 * count + i])
        for i, (source, buffer) in enumerate(zip(sources, buffers))
    ]
    for copy in arriving:
        copy.start()
    groups = near_ref.shape[1] // 128
    bound = near_ref.shape[0] // DH * groups
    owned = table_ref.shape[1] - 16
    for i, (source, parts) in enumerate(zip(buffers, pieces)):
        arriving[i].wait()
        for row, entry, first, blocks in parts:

            @pl.loop(0, blocks, unroll=min(blocks, 8))
            def _(j):
                at = table_ref[entry, first + j]
                block = source.at[pl.ds(pl.multiple_of(row + j * DH, 16), DH), :]

                @pl.when(at < bound)
                def _():
                    target = tile_at(near_ref, at, groups)
                    pltpu.make_async_copy(block, target, sems.at[i]).start()

                @pl.when(at >= bound)
                def _():
                    target = tile_at(ffn_ref, at - bound, groups)
                    pltpu.make_async_copy(block, target, sems.at[i]).start()

        if extra_rows[i] is not None:
            pltpu.make_async_copy(
                source.at[pl.ds(extra_rows[i], EXTRA), :],
                extra_ref.at[table_ref[parts[0][1], owned]],
                sems.at[count + i],
            ).start()

    for i, parts in enumerate(pieces):
        total = sum(part[3] for part in parts) * DH
        if total <= ffn_ref.shape[0]:
            landed = [ffn_ref.at[pl.ds(0, total), pl.ds(0, 128)]]
        else:
            landed = [near_ref, ffn_ref]
        for ref in landed:
            pltpu.make_async_copy(ref, ref, sems.at[i]).wait()
        if extra_rows[i] is not None:
            pltpu.make_async_copy(extra_ref.at[0], extra_ref.at[0], sems.at[count + i]).wait()


def place(table, sources, pieces, extra_rows, shapes, previous=None, deps=()):
    chained = previous is not None
    more = [in_hbm(v) for v in previous] if chained else []
    count = len(sources)
    return pl.pallas_call(
        partial(place_kernel, pieces, extra_rows, count, len(more) + len(deps)),
        out_shape=tuple(pltpu.HBM(shape, LOW) for shape in shapes)
        + (pltpu.HBM((table.shape[0], EXTRA, 128), LOW),),
        grid_spec=pltpu.PrefetchScalarGridSpec(
            num_scalar_prefetch=1,
            grid=(),
            in_specs=[ANY] * (count + len(more) + len(deps)),
            out_specs=(ANY,) * 3,
            scratch_shapes=[pltpu.VMEM(v.shape, LOW) for v in sources] + [sems(3 * count)],
        ),
        cost_estimate=FREE,
        compiler_params=pltpu.CompilerParams(vmem_limit_bytes=12 * 2**20),
        input_output_aliases={1 + count + i: i for i in range(3)} if chained else {},
    )(table, *[v if v.shape[0] < WHOLE else in_hbm(v) for v in sources], *more, *deps)


def gate_kernel(*refs):
    pass


def gate(value, deps, space=None):
    shape = jax.ShapeDtypeStruct(value.shape, value.dtype)
    return pl.pallas_call(
        gate_kernel,
        out_shape=space(value.shape, value.dtype) if space else shape,
        in_specs=[ANY] * (1 + len(deps)),
        out_specs=ANY,
        cost_estimate=FREE,
        input_output_aliases={0: 0},
    )(pltpu.with_memory_space_constraint(value, space) if space else value, *deps)


def halves_kernel(low, high, *refs):
    out_low, out_high = refs[-2:]
    out_low[...] = low[pl.ds(0, out_low.shape[0])]
    out_high[...] = high[pl.ds(low.shape[0] - out_high.shape[0], out_high.shape[0])]


def halves(low, high, rows, deps=()):
    rest = high.shape[0] - rows
    return pl.pallas_call(
        halves_kernel,
        out_shape=tuple(jax.ShapeDtypeStruct((n, 128), LOW) for n in (rows, rest)),
        in_specs=[VMEM] * 2 + [ANY] * len(deps),
        out_specs=(VMEM,) * 2,
        cost_estimate=FREE,
        compiler_params=pltpu.CompilerParams(vmem_limit_bytes=12 * 2**20),
    )(low, high, *deps)


def fetch_kernel(pieces, deps, table_ref, near_ref, ffn_ref, other_ref, zero_ref, extra_ref, *refs):
    count = len(pieces)
    outs, others, sems = refs[deps : deps + count], refs[deps + count : -1], refs[-1]
    groups = near_ref.shape[1] // 128
    bound = near_ref.shape[0] // DH * groups
    owned = table_ref.shape[1] - 16
    for i, parts in enumerate(pieces):
        for row, entry, first, blocks in parts:
            if blocks == 0:
                pltpu.make_async_copy(
                    extra_ref.at[table_ref[entry, owned]],
                    outs[i].at[pl.ds(row, EXTRA), :],
                    sems.at[i],
                ).start()
                continue

            @pl.loop(0, blocks, unroll=min(blocks, 8))
            def _(j):
                at = table_ref[entry, first + j]
                here = pl.ds(pl.multiple_of(row + j * DH, 16), DH)

                def take(source, other):
                    pltpu.make_async_copy(source, outs[i].at[here, :], sems.at[i]).start()
                    pltpu.make_async_copy(
                        other, others[i].at[here, :], sems.at[count + i]
                    ).start()

                @pl.when(at < bound)
                def _():
                    take(tile_at(near_ref, at, groups), zero_ref)

                @pl.when(at >= bound)
                def _():
                    take(
                        tile_at(ffn_ref, at - bound, groups),
                        tile_at(other_ref, at - bound, groups),
                    )

    for i, parts in enumerate(pieces):
        pltpu.make_async_copy(outs[i], outs[i], sems.at[i]).wait()
        rows = sum(part[3] for part in parts) * DH
        landed = others[i].at[pl.ds(0, rows), :]
        pltpu.make_async_copy(landed, landed, sems.at[count + i]).wait()
        for row, _, _, blocks in parts:
            if blocks:
                here = pl.ds(row, blocks * DH)
                value = outs[i][here].astype(jnp.float32) + others[i][here].astype(jnp.float32)
                outs[i][here] = value.astype(LOW)


def fetch(table, grads, extra, pieces, deps=()):
    rows = [sum(part[3] * DH or EXTRA for part in parts) for parts in pieces]
    zero = jnp.zeros((DH, 128), LOW)
    return pl.pallas_call(
        partial(fetch_kernel, pieces, len(deps)),
        out_shape=tuple(jax.ShapeDtypeStruct((n, 128), LOW) for n in rows),
        grid_spec=pltpu.PrefetchScalarGridSpec(
            num_scalar_prefetch=1,
            grid=(),
            in_specs=[ANY] * (5 + len(deps)),
            out_specs=(VMEM,) * len(pieces),
            scratch_shapes=[pltpu.VMEM((n, 128), LOW) for n in rows]
            + [pltpu.SemaphoreType.DMA((2 * len(pieces),))],
        ),
        cost_estimate=FREE,
        compiler_params=pltpu.CompilerParams(vmem_limit_bytes=12 * 2**20),
    )(table, *[in_hbm(g) for g in grads], zero, extra, *deps)


def fetch_all_kernel(pieces, table_ref, grad_ref, extra_ref, out, sem):
    groups = grad_ref.shape[1] // 128
    owned = table_ref.shape[1] - 16
    for row, entry, first, blocks in pieces:
        if blocks == 0:
            pltpu.make_async_copy(
                extra_ref.at[table_ref[entry, owned]], out.at[pl.ds(row, EXTRA), :], sem.at[0]
            ).start()
            continue

        @pl.loop(0, blocks)
        def _(j):
            pltpu.make_async_copy(
                tile_at(grad_ref, table_ref[entry, first + j], groups),
                out.at[pl.ds(pl.multiple_of(row + j * DH, 16), DH), :],
                sem.at[0],
            ).start()

    pltpu.make_async_copy(out, out, sem.at[0]).wait()


def fetch_all(table, grad, extra, pieces):
    rows = sum(part[3] * DH or EXTRA for part in pieces)
    return pl.pallas_call(
        partial(fetch_all_kernel, pieces),
        out_shape=jax.ShapeDtypeStruct((rows, 128), LOW),
        grid_spec=pltpu.PrefetchScalarGridSpec(
            num_scalar_prefetch=1,
            grid=(),
            in_specs=[ANY] * 2,
            out_specs=VMEM,
            scratch_shapes=[pltpu.SemaphoreType.DMA((1,))],
        ),
        compiler_params=pltpu.CompilerParams(vmem_limit_bytes=16 * 2**20),
    )(table, in_hbm(grad), extra)


def turn_kernel(deps, keep_a, got_a, keep_b, got_b, *refs):
    for keep, got, out in zip((keep_a, keep_b), (got_a, got_b), refs[deps:]):
        size = out.shape[0]
        parts = [ref[pl.ds(ref.shape[0] - size, size)] for ref in (keep, got)]
        out[...] = sum(part.astype(jnp.float32) for part in parts).astype(LOW)


def turn(keep_a, got_a, keep_b, got_b, deps=()):
    return pl.pallas_call(
        partial(turn_kernel, len(deps)),
        out_shape=tuple(
            jax.ShapeDtypeStruct((keep.shape[0] // 2, 128), LOW) for keep in (keep_a, keep_b)
        ),
        in_specs=[VMEM] * 4 + [ANY] * len(deps),
        out_specs=(VMEM,) * 2,
        cost_estimate=FREE,
        compiler_params=pltpu.CompilerParams(vmem_limit_bytes=12 * 2**20),
    )(keep_a, got_a, keep_b, got_b, *deps)


def merge_kernel(deps, first, second, more, one, two, three, *refs):
    total, *outs = refs[deps:]
    row = 0
    for ref, out in zip((first, second), outs):
        size = ref.shape[0]
        value = ref[...].astype(jnp.float32) + more[pl.ds(row, size)].astype(jnp.float32)
        out[...] = value.astype(LOW)
        row += size
    total[...] = sum(ref[...].astype(jnp.float32) for ref in (one, two, three)).astype(LOW)


def merge(first, second, more, parts, deps):
    return pl.pallas_call(
        partial(merge_kernel, len(deps)),
        out_shape=tuple(jax.ShapeDtypeStruct(v.shape, LOW) for v in (parts[0], first, second)),
        in_specs=[VMEM] * 6 + [ANY] * len(deps),
        out_specs=(VMEM,) * 3,
        cost_estimate=FREE,
        compiler_params=pltpu.CompilerParams(vmem_limit_bytes=12 * 2**20),
    )(first, second, more, *parts, *deps)


def total_rows(half, running, start, row, rows):
    here = pl.ds(row, rows)
    result = sum(ref[here].astype(jnp.float32) for ref in half)
    if running is not None:
        result = result + running[pl.ds(start + row, rows)].astype(jnp.float32)
    return result


def total_kernel(chained, deps, *refs):
    running = refs[6] if chained else None
    out = refs[6 + chained + deps]
    start = 0
    for half in (refs[:3], refs[3:6]):
        size = half[2].shape[0]
        result = total_rows(half, running, start, 0, size)
        out[pl.ds(start, size)] = result.astype(out.dtype)
        start += size


def total(half_a, half_b, running, deps=()):
    chain = [] if running is None else [running]
    return pl.pallas_call(
        partial(total_kernel, len(chain), len(deps)),
        out_shape=jax.ShapeDtypeStruct((half_a[2].shape[0] + half_b[2].shape[0], 128), LOW),
        in_specs=[VMEM] * (6 + len(chain)) + [ANY] * len(deps),
        out_specs=VMEM,
        cost_estimate=FREE,
        compiler_params=pltpu.CompilerParams(vmem_limit_bytes=12 * 2**20),
    )(*half_a, *half_b, *chain, *deps)


def divided(value, by):
    shift = by.bit_length() - 1
    assert by == 1 << shift
    return lax.shift_right_logical(value, jnp.full_like(value, shift)), value & (by - 1)


def places_of(perm, panel, panels, heads64, ffn64, row_groups):
    col, row = divided(perm, row_groups)
    in_ffn = jnp.maximum(col - 4 * heads64, 0)
    kind, at = divided(col, heads64)
    ffn_kind, ffn_at = divided(in_ffn, ffn64)
    at_head = (kind * panels + panel) * heads64 + at
    at_ffn = 4 * heads64 * panels + (ffn_kind * panels + panel) * ffn64 + ffn_at
    return jnp.where(col < 4 * heads64, at_head, at_ffn) * row_groups + row


def tables_kernel(rings, sizes, at_ref, own_ref, other_ref, come_ref, go_ref):
    z_at, y_at, x_at = at_ref[0], at_ref[1], at_ref[2]
    owned = own_ref.shape[1]
    for sign, out in ((-1, come_ref), (1, go_ref)):
        for k in range(rings):
            z = lax.rem(z_at + sign * k + rings, rings)
            for y in range(2):
                dp = z * 2 + (y_at ^ y)
                for x, perm in enumerate((own_ref, other_ref)):
                    panel = x_at ^ x
                    entry = 4 * k + 2 * y + x
                    out[pl.ds(entry, 1), :] = jnp.full((1, out.shape[1]), dp * 2 + panel, jnp.int32)
                    out[pl.ds(entry, 1), pl.ds(0, owned)] = places_of(
                        perm[pl.ds(dp, 1), :], panel, 2, *sizes
                    )


def tables(at, own, other, rings, sizes):
    shape = jax.ShapeDtypeStruct((rings * 4, own.shape[1] + 16), jnp.int32)
    return pl.pallas_call(
        partial(tables_kernel, rings, sizes),
        out_shape=(shape, shape),
        in_specs=[SMEM, VMEM, VMEM],
        out_specs=(VMEM, VMEM),
        cost_estimate=FREE,
    )(at, own, other)


class Rows:
    def __init__(self, source, target, sems, first=0):
        rows = min(source.shape[0], target.shape[0])
        self.chunk = rows // sems.shape[0]
        self.copies = []
        for i in range(sems.shape[0]):
            here = pl.ds(i * self.chunk, self.chunk)
            there = pl.ds(first + i * self.chunk, self.chunk)
            self.copies.append(pltpu.make_async_copy(source.at[there], target.at[here], sems.at[i]))
        self.done = 0

    def start(self):
        for copy in self.copies:
            copy.start()
        return self

    def upto(self, rows):
        while self.done * self.chunk < rows and self.done < len(self.copies):
            self.copies[self.done].wait()
            self.done += 1

    def whole(self):
        self.upto(self.chunk * len(self.copies))


class Stream:
    def __init__(self, chunks, buffer, sems):
        slots = buffer.shape[0]
        self.buffer = buffer
        self.copies = [
            pltpu.make_async_copy(chunk, buffer.at[i % slots], sems.at[i % slots])
            for i, chunk in enumerate(chunks)
        ]
        self.used = 0
        for copy in self.copies[:slots]:
            copy.start()

    def next(self):
        slots = self.buffer.shape[0]
        ahead = self.used - 1 + slots
        if self.used and ahead < len(self.copies):
            self.copies[ahead].start()
        self.copies[self.used].wait()
        self.used += 1
        return self.buffer.at[(self.used - 1) % slots]


def row_chunks(weight, row, rows, size):
    return [weight.at[pl.ds(row + at, size), :] for at in range(0, rows, size)]


def column_chunks(weight, row, rows, size):
    return [weight.at[pl.ds(row, rows), pl.ds(at, size)] for at in range(0, weight.shape[1], size)]


class Tiles:
    def __init__(self, buffer, sems):
        self.buffer, self.sems, self.under_way = buffer, sems, []

    def put(self, value, target):
        slots = self.buffer.shape[0]
        slot = len(self.under_way) % slots
        if len(self.under_way) >= slots:
            self.under_way[-slots].wait()
        self.buffer[slot] = value
        copy = pltpu.make_async_copy(self.buffer.at[slot], target, self.sems.at[slot])
        copy.start()
        self.under_way.append(copy)

    def drain(self):
        for copy in self.under_way[-self.buffer.shape[0] :]:
            copy.wait()


def vmem(*shape, dtype=LOW):
    return pltpu.VMEM(shape, dtype)


def megabytes(n):
    return pltpu.CompilerParams(vmem_limit_bytes=n * 2**20)


def work(flops, moved=2**22, transcendentals=0):
    return pl.CostEstimate(flops=flops, bytes_accessed=moved, transcendentals=transcendentals)


def project_in_kernel(q_rows, weight, x, bias, out, w, w_sems):
    rows, tile = out.shape[0], w.shape[1]
    chunks = Stream(row_chunks(weight, 0, rows, tile), w, w_sems)
    for at in range(0, rows, tile):
        here = pl.ds(at, tile)
        value = product(chunks.next()[...], x[...], 1, 1) + jnp.transpose(bias[:, here])[:, :1]
        out[here, :] = (value * (DH**-0.5 if at < q_rows else 1.0)).astype(LOW)


def project_in(weights, x, bias):
    rows, width = bias.shape[1], weights.shape[1]
    return pl.pallas_call(
        partial(project_in_kernel, rows // 3),
        out_shape=jax.ShapeDtypeStruct((rows, x.shape[0]), LOW),
        in_specs=[ANY, VMEM, VMEM],
        out_specs=VMEM,
        scratch_shapes=[vmem(3, min(rows // 3, 512), width), sems(3)],
        compiler_params=megabytes(12),
        cost_estimate=work(2 * rows * x.shape[0] * x.shape[1]),
    )(in_hbm(weights), x, bias)


def project_kernel(row, deps, where_ref, context, weight, *refs):
    mine, theirs, w, w_sems, tiles, tile_sems = refs[deps:]
    loader = Rows(weight, w, w_sems, row).start()
    loader.whole()
    half = mine.shape[0]
    leaving = Tiles(tiles, tile_sems)
    for i, out in ((1, theirs), (0, mine)):
        at = pl.multiple_of((where_ref[0] ^ i) * half, half)
        leaving.put(product(context[:, pl.ds(at, half)], w[...], 0, 0).astype(LOW), out)
    leaving.drain()


def project(where, context, weights, row, deps=(), cost=None):
    features, tokens = context.shape
    width = weights.shape[1]
    out = pltpu.HBM((tokens // 2, width), LOW)
    return pl.pallas_call(
        partial(project_kernel, row, len(deps)),
        out_shape=(out, out),
        in_specs=[SMEM, VMEM, ANY] + [ANY] * len(deps),
        out_specs=(ANY, ANY),
        scratch_shapes=[
            vmem(features, width),
            sems(4),
            vmem(2, tokens // 2, width),
            sems(2),
        ],
        compiler_params=megabytes(14),
        cost_estimate=cost or work(2 * features * tokens * width),
    )(where[None], context, in_hbm(weights), *deps)


def ffn_kernel(parts, row, *refs):
    inputs, (weight, bias), refs = refs[:parts], refs[parts : parts + 2], refs[parts + 2 :]
    values, slopes, outs = refs[:parts], refs[parts : 2 * parts], refs[2 * parts : 3 * parts]
    first, first_sems, second, second_sems = refs[3 * parts :]
    hidden, tile = bias.shape[1], first.shape[1]
    chunks = Stream(row_chunks(weight, row, hidden, tile), first, first_sems)
    columns = Stream(
        column_chunks(weight, row + hidden, hidden, second.shape[2]), second, second_sems
    )
    for at in range(0, hidden, tile):
        here = pl.ds(at, tile)
        w = chunks.next()
        for i, x in enumerate(inputs):
            before = product(x[...], w[...], 1, 1) + bias[:, here]
            result, derivative = gelu_pair(before)
            values[i][:, here] = result.astype(LOW)
            slopes[i][:, here] = derivative.astype(LOW)
    finish_ffn(columns, values, outs)


def finish_ffn(columns, values, outs):
    tile = columns.buffer.shape[2]
    for at in range(0, outs[0].shape[1], tile):
        w = columns.next()
        for value, out in zip(values, outs):
            out[:, pl.ds(at, tile)] = product(value[...], w[...], 1, 0).astype(LOW)


def ffn_shapes(parts, hidden, width):
    tokens = parts[0].shape[0]
    low = [jax.ShapeDtypeStruct((tokens, hidden), LOW)] * len(parts)
    outs = [jax.ShapeDtypeStruct((tokens, width), LOW)] * len(parts)
    scratch = [vmem(2, min(hidden, 512), width), sems(2), vmem(2, hidden, 256), sems(2)]
    return low, outs, scratch


def ffn(parts, weights, row, bias):
    hidden, width, n = bias.shape[1], weights.shape[1], len(parts)
    low, outs, scratch = ffn_shapes(parts, hidden, width)
    result = pl.pallas_call(
        partial(ffn_kernel, n, row),
        out_shape=tuple(low + low + outs),
        in_specs=[VMEM] * n + [ANY, VMEM],
        out_specs=(VMEM,) * (3 * n),
        scratch_shapes=scratch,
        compiler_params=megabytes(SCOPED),
        cost_estimate=work(4 * SLOTS * hidden * width, 2**24, SLOTS * hidden),
    )(*parts, in_hbm(weights), bias)
    return result[:n], result[n : 2 * n], result[2 * n :]


def ffn_back_kernel(parts, row, *refs):
    inputs, weight, slopes = refs[:parts], refs[parts], refs[parts + 1 : 2 * parts + 1]
    refs = refs[2 * parts + 1 :]
    grads, outs, sums = refs[:parts], refs[parts : 2 * parts], refs[2 * parts]
    first, first_sems, second, second_sems = refs[2 * parts + 1 :]
    hidden, tile = sums.shape[1], first.shape[1]
    chunks = Stream(row_chunks(weight, row + hidden, hidden, tile), first, first_sems)
    columns = Stream(column_chunks(weight, row, hidden, second.shape[2]), second, second_sems)
    for at in range(0, hidden, tile):
        here = pl.ds(at, tile)
        w = chunks.next()
        total = 0.0
        for x, slope, grad in zip(inputs, slopes, grads):
            result = product(x[...], w[...], 1, 1) * slope[:, here].astype(jnp.float32)
            grad[:, here] = result.astype(LOW)
            total = total + jnp.sum(result, axis=0, keepdims=True)
        sums[:, here] = jnp.broadcast_to(total, (sums.shape[0], tile))
    finish_ffn(columns, grads, outs)


def ffn_back(parts, weights, row, slopes):
    hidden, width, n = slopes[0].shape[1], weights.shape[1], len(parts)
    low, outs, scratch = ffn_shapes(parts, hidden, width)
    result = pl.pallas_call(
        partial(ffn_back_kernel, n, row),
        out_shape=tuple(low + outs) + (jax.ShapeDtypeStruct((8, hidden), jnp.float32),),
        in_specs=[VMEM] * n + [ANY] + [VMEM] * n,
        out_specs=(VMEM,) * (2 * n + 1),
        scratch_shapes=scratch,
        compiler_params=megabytes(SCOPED),
        cost_estimate=work(4 * SLOTS * hidden * width, 2**24),
    )(*parts, in_hbm(weights), *slopes)
    return result[:n], result[n : 2 * n], result[-1]


def ffn_grad_kernel(parts, row, *refs):
    values, upper, grads, lower = (refs[i * parts : (i + 1) * parts] for i in range(4))
    out, tiles, tile_sems = refs[4 * parts :]
    leaving = Tiles(tiles, tile_sems)
    hidden, tile = values[0].shape[1], tiles.shape[1]
    for lefts, rights, begin in ((values, upper, row + hidden), (grads, lower, row)):
        for at in range(0, hidden, tile):
            here = pl.ds(at, tile)
            value = sum(product(a[:, here], b[...], 0, 0) for a, b in zip(lefts, rights))
            leaving.put(value.astype(LOW), out.at[pl.ds(begin + at, tile), :])
    leaving.drain()


def ffn_grad(values, upper, grads, lower, shape, row):
    n, hidden, width = len(values), values[0].shape[1], shape[1]
    return pl.pallas_call(
        partial(ffn_grad_kernel, n, row),
        out_shape=pltpu.HBM(shape, LOW),
        in_specs=[VMEM] * (4 * n),
        out_specs=ANY,
        scratch_shapes=[vmem(2, min(hidden, 512), width), sems(2)],
        compiler_params=megabytes(SCOPED),
        cost_estimate=work(4 * SLOTS * hidden * width, 2**24),
    )(*values, *upper, *grads, *lower)


def project_back_kernel(
    row, deps, where_ref, weight, context, own, other, *refs
):
    out, grad, w, w_sems, h, h_sems, c, c_sems, b, sem = refs[deps:]
    loader = Rows(weight, w, w_sems, row).start()
    hidden = [Rows(part, h.at[i], h_sems.at[i]).start() for i, part in enumerate((own, other))]
    context_rows = Rows(context, c, c_sems).start()
    half = own.shape[0]
    columns = [pl.ds(pl.multiple_of((where_ref[0] ^ i) * half, half), half) for i in range(2)]
    loader.whole()
    for i in range(2):
        hidden[i].whole()
        out[:, columns[i]] = product(w[...], h[i], 1, 1).astype(LOW)
    context_rows.whole()
    b[...] = sum(product(c[:, columns[i]], h[i], 1, 0) for i in range(2)).astype(LOW)
    copy = pltpu.make_async_copy(b, grad.at[pl.ds(row, b.shape[0]), :], sem.at[0])
    copy.start()
    copy.wait()


def project_back(where, weights, context, own, other, row, deps=()):
    features, tokens = context.shape
    width = own.shape[1]
    return pl.pallas_call(
        partial(project_back_kernel, row, len(deps)),
        out_shape=(
            jax.ShapeDtypeStruct((features, tokens), LOW),
            pltpu.HBM(weights.shape, LOW),
        ),
        in_specs=[SMEM] + [ANY] * (4 + len(deps)),
        out_specs=(VMEM, ANY),
        scratch_shapes=[
            vmem(features, width),
            sems(2),
            vmem(2, tokens // 2, width),
            pltpu.SemaphoreType.DMA((2, 2)),
            vmem(features, tokens),
            sems(2),
            vmem(features, width),
            sems(1),
        ],
        compiler_params=megabytes(SCOPED),
        cost_estimate=work(4 * features * tokens * width),
    )(where[None], *[in_hbm(v) for v in (weights, context, own, other)], *deps)


def last_grad_kernel(left, right, _, out, sums, tiles, tile_sems):
    leaving = Tiles(tiles, tile_sems)
    tile = tiles.shape[1]
    for at in range(0, left.shape[0], tile):
        here = pl.ds(at, tile)
        leaving.put(product(left[here, :], right[...], 1, 0).astype(LOW), out.at[here, :])
    sums[...] = product(jnp.ones((sums.shape[0], left.shape[1]), LOW), left[...], 1, 1)
    leaving.drain()


def last_grad(left, right, grads):
    rows, tokens = left.shape
    width = right.shape[1]
    tile = rows // 2
    return pl.pallas_call(
        last_grad_kernel,
        out_shape=(pltpu.HBM(grads.shape, LOW), jax.ShapeDtypeStruct((8, rows), jnp.float32)),
        in_specs=[VMEM, VMEM, ANY],
        out_specs=(ANY, VMEM),
        scratch_shapes=[vmem(2, tile, width), sems(2)],
        compiler_params=megabytes(SCOPED),
        cost_estimate=work(2 * rows * tokens * width),
        input_output_aliases={2: 0},
    )(left, right, in_hbm(grads))


BIAS_OUTPUT, BIAS_OUTER, GAIN_ONE, SHIFT_ONE, GAIN_TWO, SHIFT_TWO = range(6)


def row_of(vectors, i):
    return vectors[pl.ds(i, 1), :]


def mean_of(value):
    return jnp.mean(value, axis=-1, keepdims=True)


def widened(here, *refs):
    return sum(ref[here, :].astype(jnp.float32) for ref in refs)


def norm_one_step(here, vectors, x, mine, got, middle, scaled, inverse):
    hidden = widened(here, x, mine, got) + row_of(vectors, BIAS_OUTPUT)
    center = hidden - mean_of(hidden)
    factor = lax.rsqrt(mean_of(center * center) + 1e-05)
    normal = center * factor
    middle[here, :] = (
        normal * row_of(vectors, GAIN_ONE) + row_of(vectors, SHIFT_ONE)
    ).astype(LOW)
    scaled[here, :] = normal.astype(LOW)
    inverse[here, :] = jnp.broadcast_to(factor, (factor.shape[0], 128))
    return ()


def back_through(upstream, normal, factor, gain):
    gained = upstream * gain
    return factor * (gained - mean_of(gained) - normal * mean_of(gained * normal))


def norm_two_step(here, vectors, middle, mine, got, upstream, layer, dz):
    outer = widened(here, middle, mine, got) + row_of(vectors, BIAS_OUTER)
    center = outer - mean_of(outer)
    factor = lax.rsqrt(mean_of(center * center) + 1e-05)
    normal = center * factor
    gain = row_of(vectors, GAIN_TWO)
    layer[here, :] = (normal * gain + row_of(vectors, SHIFT_TWO)).astype(LOW)
    dy = widened(here, upstream)
    result = back_through(dy, normal, factor, gain)
    dz[here, :] = result.astype(LOW)
    return (result, dy * normal, dy)


def norm_back_step(here, vectors, dz, mine, got, scaled, inverse, dhidden):
    dy = widened(here, dz, mine, got)
    normal = widened(here, scaled)
    factor = inverse[here, :][:, :1]
    result = back_through(dy, normal, factor, row_of(vectors, GAIN_ONE))
    dhidden[here, :] = result.astype(LOW)
    return (result, dy * normal, dy)


def eight_rows(value):
    return sum(value[i : i + 8] for i in range(0, value.shape[0], 8))


def layer_kernel(
    x, mine, got, upstream, vectors, bias, w_own, w_other,
    layer, dhidden, sums, inner, g_own, g_other,
    x_in, mine_in, got_in, up_in, in_sems, act, slope, mid, normal, inverse, dz, acc, out,
    out_sems, one, one_sems, two, two_sems, tile_one, tile_one_sems, tile_two, tile_two_sems,
):
    rows = x.shape[0]
    half, tile = w_own.shape[0] // 2, one.shape[1]
    ones = [c for w in (w_own, w_other) for c in row_chunks(w, 0, half, tile)]
    twos = [c for w in (w_own, w_other) for c in row_chunks(w, half, half, tile)]
    arriving = [
        Rows(source, target, in_sems.at[i])
        for i, (source, target) in enumerate(
            ((x, x_in), (mine, mine_in), (got, got_in), (upstream, up_in))
        )
    ]
    for copies in arriving[:3]:
        copies.start()
    first, second = Stream(ones + ones, one, one_sems), Stream(twos + twos, two, two_sems)
    arriving[3].start()
    step = arriving[0].chunk
    places = [pl.ds(at, step) for at in range(0, rows, step)]

    for at in range(0, rows, FINE):
        for copies in arriving[:3]:
            copies.upto(at + FINE)
        norm_one_step(pl.ds(at, FINE), vectors, x_in, mine_in, got_in, mid, normal, inverse)

    before = product(mid[...], first.next()[...], 1, 1) + bias[:, pl.ds(0, tile)]
    for n in range(len(ones)):
        columns = pl.ds(n * tile, tile)
        down_weight = second.next()
        if n + 1 < len(ones):
            up_weight = first.next()
            after = product(mid[...], up_weight[...], 1, 1) + bias[:, pl.ds((n + 1) * tile, tile)]
        value, derivative = gelu_pair(before)
        before = after
        value = value.astype(LOW)
        act[:, columns] = value
        slope[:, columns] = derivative.astype(LOW)
        part = product(value, down_weight[...], 1, 0)
        if n:
            acc[...] += part
        else:
            acc[...] = part

    arriving[3].whole()
    leaving, totals = [], []
    for at in range(0, rows, FINE):
        here = pl.ds(at, FINE)
        outer = acc[here, :] + widened(here, mid) + row_of(vectors, BIAS_OUTER)
        center = outer - mean_of(outer)
        factor = lax.rsqrt(mean_of(center * center) + 1e-05)
        scaled = center * factor
        gain = row_of(vectors, GAIN_TWO)
        out[here, :] = (scaled * gain + row_of(vectors, SHIFT_TWO)).astype(LOW)
        dy = widened(here, up_in)
        result = back_through(dy, scaled, factor, gain)
        acc[here, :] = result
        dz[here, :] = result.astype(LOW)
        totals.append([eight_rows(v) for v in (result, dy * scaled, dy)])
        if (at + FINE) % step == 0:
            n = at // step
            leaving.append(
                pltpu.make_async_copy(out.at[places[n]], layer.at[places[n]], out_sems.at[n])
            )
            leaving[-1].start()

    grads_one, grads_two = Tiles(tile_one, tile_one_sems), Tiles(tile_two, tile_two_sems)
    for n in range(len(ones)):
        columns = pl.ds(n * tile, tile)
        target, begin = (g_own, n * tile) if n * tile < half else (g_other, n * tile - half)
        value = product(act[:, columns], dz[...], 0, 0)
        grads_two.put(value.astype(LOW), target.at[pl.ds(half + begin, tile), :])
        grad = product(dz[...], second.next()[...], 1, 1) * slope[:, columns].astype(jnp.float32)
        inner[:, columns] = jnp.broadcast_to(
            jnp.sum(grad, axis=0, keepdims=True), (inner.shape[0], tile)
        )
        slope[:, columns] = grad.astype(LOW)
        value = product(slope[:, columns], mid[...], 0, 0)
        grads_one.put(value.astype(LOW), target.at[pl.ds(begin, tile), :])
        acc[...] += product(slope[:, columns], first.next()[...], 1, 0)

    for at in range(0, rows, FINE):
        here = pl.ds(at, FINE)
        dy = acc[here, :]
        scaled = widened(here, normal)
        factor = inverse[here, :][:, :1]
        result = back_through(dy, scaled, factor, row_of(vectors, GAIN_ONE))
        got_in[here, :] = result.astype(LOW)
        totals.append([eight_rows(v) for v in (result, dy * scaled, dy)])
        if (at + FINE) % step == 0:
            n = at // step
            leaving.append(
                pltpu.make_async_copy(got_in.at[places[n]], dhidden.at[places[n]], in_sems.at[2, n])
            )
            leaving[-1].start()
    count = rows // FINE
    lines = [
        jnp.sum(sum(t[i] for t in part), axis=0, keepdims=True)
        for part in (totals[:count], totals[count:])
        for i in range(3)
    ]
    sums[...] = jnp.concatenate(lines + [jnp.zeros_like(lines[0])] * 2, axis=0)
    grads_one.drain()
    grads_two.drain()
    for copy in leaving:
        copy.wait()


def layer_part(x, mine, got, upstream, vectors, bias, w_own, w_other):
    rows, width = x.shape
    hidden = bias.shape[1]
    tile = WIDE
    low = jax.ShapeDtypeStruct((rows, width), LOW)
    grad = pltpu.HBM(w_own.shape, LOW)
    dma = pltpu.SemaphoreType.DMA
    return pl.pallas_call(
        layer_kernel,
        out_shape=(
            low,
            pltpu.HBM((rows, width), LOW),
            jax.ShapeDtypeStruct((8, width), jnp.float32),
            jax.ShapeDtypeStruct((8, hidden), jnp.float32),
            grad,
            grad,
        ),
        in_specs=[ANY] * 4 + [VMEM] * 2 + [ANY] * 2,
        out_specs=(ANY, ANY, VMEM, VMEM, ANY, ANY),
        scratch_shapes=[vmem(rows, width) for _ in range(4)]
        + [
            dma((4, 4)),
            vmem(rows, hidden),
            vmem(rows, hidden),
            vmem(rows, width),
            vmem(rows, width),
            vmem(rows, 128, dtype=jnp.float32),
            vmem(rows, width),
            vmem(rows, width, dtype=jnp.float32),
            vmem(rows, width),
            sems(4),
            vmem(2, tile, width),
            sems(2),
            vmem(2, tile, width),
            sems(2),
            vmem(1, tile, width),
            sems(1),
            vmem(1, tile, width),
            sems(1),
        ],
        compiler_params=megabytes(50),
        cost_estimate=work(12 * rows * hidden * width, 2**25, rows * hidden),
    )(in_hbm(x), in_hbm(mine), got, in_hbm(upstream), vectors, bias, in_hbm(w_own), in_hbm(w_other))


def rows_kernel(step, count, with_sums, vectors, *refs):
    inputs, outs = refs[:count], refs[count:]
    if with_sums:
        sums, outs = outs[-1], outs[:-1]
    rows = inputs[0].shape[0]
    tile = min(rows, 128)
    totals = 0
    for at in range(0, rows, tile):
        values = step(pl.ds(at, tile), vectors, *inputs, *outs)
        if with_sums:
            parts = [jnp.sum(value, axis=0, keepdims=True) for value in values]
            totals = totals + jnp.concatenate(parts + [jnp.zeros_like(parts[0])] * 5, axis=0)
    if with_sums:
        sums[...] = totals


def by_rows(step, inputs, vectors, outs, with_sums):
    rows, width = inputs[0].shape
    shapes = [jax.ShapeDtypeStruct((rows, n), dtype) for n, dtype in outs]
    if with_sums:
        shapes.append(jax.ShapeDtypeStruct((8, width), jnp.float32))
    return pl.pallas_call(
        partial(rows_kernel, step, len(inputs), with_sums),
        out_shape=tuple(shapes),
        in_specs=[VMEM] * (1 + len(inputs)),
        out_specs=(VMEM,) * len(shapes),
        compiler_params=megabytes(12),
        cost_estimate=work(40 * rows * width, 2**23, rows),
    )(vectors, *inputs)


def shampoo_blocks(scale, grad, left_root, right_root, left, right, weight, outs):
    new_left, new_right, new_weight = outs
    for i in range(grad.shape[0]):
        g = grad[i].astype(LOW)
        new_left[i] = 0.5 * left[i] + (0.5 * scale) * product(g, g, 0, 0)
        new_right[i] = 0.5 * right[i] + (0.5 * scale) * product(g, g, 1, 1)
        step = product(g, left_root[i].astype(LOW), 1, 1)
        step = product(right_root[i].astype(LOW), step.astype(LOW), 0, 0)
        here = weight[i]
        size = jnp.sqrt(jnp.mean(here * here, keepdims=True) + 1e-06)
        norm = jnp.sqrt(jnp.mean(step * step, keepdims=True) + 1e-06)
        new_weight[i] = here - (0.3 * size / norm) * step


def shampoo_kernel(scale, *refs):
    grad, inputs, outs = refs[0], refs[1:6], refs[6:]
    shampoo_blocks(scale, grad, *inputs, outs)


def last_kernel(scale, *refs):
    halves, running, inputs = (refs[:3], refs[3:6]), refs[6], refs[7:12]
    grad, extra, outs = refs[12], refs[13], refs[14:]
    blocks = grad.shape[0]
    at = pl.program_id(0)
    rows_a = halves[0][2].shape[0] - EXTRA
    steps_a = rows_a // (blocks * DH)

    def take(half, start, step):
        row = pl.multiple_of(step * blocks * DH, blocks * DH)
        value = total_rows(half, running, start, row, blocks * DH)
        grad[...] = value.reshape(blocks, DH, 128)

    @pl.when(at < steps_a)
    def _():
        take(halves[0], 0, at)

    @pl.when(at >= steps_a)
    def _():
        take(halves[1], rows_a + EXTRA, at - steps_a)

    extra[...] = total_rows(halves[0], running, 0, rows_a, EXTRA)
    shampoo_blocks(scale, grad, *inputs, outs)


def shampoo_specs(tile, values):
    return [pl.BlockSpec((tile,) + v.shape[1:], lambda i: (i, 0, 0)) for v in values]


def shampoo(scale, grad, *state):
    owned = grad.shape[0]
    tile = 8 if owned % 8 == 0 else owned
    return pl.pallas_call(
        partial(shampoo_kernel, scale),
        out_shape=tuple(jax.ShapeDtypeStruct(v.shape, jnp.float32) for v in state[2:]),
        grid=(owned // tile,),
        in_specs=shampoo_specs(tile, (grad, *state)),
        out_specs=tuple(shampoo_specs(tile, state[2:])),
        compiler_params=megabytes(16),
    )(grad, *state)


def last_step(scale, half_a, half_b, running, *state):
    owned = state[0].shape[0]
    tile = 8
    grad = jax.ShapeDtypeStruct((owned, DH, 128), jnp.float32)
    return pl.pallas_call(
        partial(last_kernel, scale),
        out_shape=(grad, jax.ShapeDtypeStruct((EXTRA, 128), jnp.float32))
        + tuple(jax.ShapeDtypeStruct(v.shape, jnp.float32) for v in state[2:]),
        grid=(owned // tile,),
        in_specs=[
            pl.BlockSpec(v.shape, lambda i: (0, 0)) for v in (*half_a, *half_b, running)
        ]
        + shampoo_specs(tile, state),
        out_specs=(
            *shampoo_specs(tile, (grad,)),
            pl.BlockSpec((EXTRA, 128), lambda i: (0, 0)),
            *shampoo_specs(tile, state[2:]),
        ),
        compiler_params=megabytes(32),
    )(*half_a, *half_b, running, *state)


class Fabric:
    def __init__(self, sizes, row_ways):
        self.batch, self.model = sizes
        self.ways = row_ways
        self.panels = self.model // row_ways
        self.wide = row_ways == 2 and self.panels == 2 and self.batch % 2 == 0
        self.row_groups = [
            list(range(i, i + row_ways)) for i in range(0, self.model, row_ways)
        ]
        self.same_groups = [list(range(t, self.model, row_ways)) for t in range(row_ways)]

    def send(self, value, move):
        pairs = []
        for d in range(self.batch):
            for m in range(self.model):
                e, n = move(d, m)
                pairs.append((d * self.model + m, (e % self.batch) * self.model + n))
        return lax.ppermute(value, BOTH, pairs)

    def to_core(self, value):
        return self.send(value, lambda d, m: (d, m ^ 1))

    def to_x(self, value):
        return self.send(value, lambda d, m: (d, m ^ 2))

    def to_y(self, value):
        return self.send(value, lambda d, m: (d ^ 1, m))

    def to_z(self, value):
        return self.send(value, lambda d, m: (d + 2, m))

    def row_gather(self, own):
        if self.wide:
            return self.join(self.share(own), 0)
        return lax.all_gather(own, "mp", axis=0, tiled=True, axis_index_groups=self.row_groups)

    def share(self, own):
        if self.wide:
            return [own, self.to_core(own)]
        return [self.row_gather(own)]

    def gather_back(self, parts):
        if self.wide:
            return parts[0].astype(LOW), self.to_core(parts[1].astype(LOW))
        mine = lax.psum_scatter(
            parts[0].astype(LOW),
            "mp",
            scatter_dimension=0,
            tiled=True,
            axis_index_groups=self.row_groups,
        )
        return mine, jnp.zeros(mine.shape, LOW)

    def cut(self, value, axis):
        if not self.wide:
            return [value]
        size = value.shape[axis] // 2
        core = lax.rem(lax.axis_index("mp"), 2)
        return [
            lax.dynamic_slice_in_dim(value, at * size, size, axis) for at in (core, 1 - core)
        ]

    def join(self, parts, axis):
        if not self.wide:
            return parts[0]
        own, other = parts
        first = lax.rem(lax.axis_index("mp"), 2) == 0
        return jnp.concatenate(
            [jnp.where(first, own, other), jnp.where(first, other, own)], axis=axis
        )

    def row_sum(self, value):
        if self.wide:
            return value + self.to_core(value)
        return lax.psum(value, "mp", axis_index_groups=self.row_groups)


def shards(
    sizes,
    x_in,
    out_grad,
    item_lengths,
    weight_store,
    owner_perm,
    left_roots,
    right_roots,
    left_stats,
    right_stats,
    head_vectors,
    head_first,
    head_second,
    shared_vectors,
    shared_first,
    shared_second,
):
    batch_ways, model_ways = sizes
    shard_rows, model_width = x_in.shape
    fabric = Fabric(sizes, SLOTS // shard_rows)
    ways, panels, wide = fabric.ways, fabric.panels, fabric.wide
    dp_at, mp_at = lax.axis_index("dp"), lax.axis_index("mp")
    row_at, place_at = lax.div(mp_at, ways), lax.rem(mp_at, ways)

    owned, row_block, col_block = weight_store.shape[1:]
    head_part, shared_part = head_vectors.shape[1], shared_vectors.shape[0]
    head_count, shared_count = head_part * batch_ways, shared_part * batch_ways * model_ways
    block_count = owner_perm.shape[1]
    row_groups = model_width // row_block
    head_width = model_width // model_ways
    ffn_total = shared_count - 6 * model_width
    ffn_width = ffn_total // model_ways
    heads64, ffn64 = head_width // DH, ffn_width // DH
    hidden_rows = panels * (4 * head_width + 2 * ffn_width)
    q_rows, f_rows = panels * head_width, panels * ffn_width
    panel_shape = (hidden_rows, model_width)
    panel_shapes = ((4 * q_rows, model_width), (2 * f_rows, model_width))
    half_a = (owned // 2) * DH + EXTRA
    blocks_a, blocks_b = owned // 2, owned - owned // 2

    def two_parts(value):
        high = lax.reduce_precision(value, 8, 7)
        return jnp.concatenate([high.astype(LOW), (value - high).astype(LOW)])

    blocks_low = jnp.swapaxes(weight_store[0], 1, 2).astype(LOW).reshape(owned * DH, 128)
    vectors = jnp.concatenate([two_parts(head_vectors[0]), two_parts(shared_vectors)])
    vectors = jnp.pad(vectors, (0, EXTRA * 128 - vectors.shape[0])).reshape(EXTRA, 128)
    own = jnp.concatenate(
        [blocks_low[: blocks_a * DH], vectors, blocks_low[blocks_a * DH :]], axis=0
    )

    layout = (heads64, ffn64, row_groups)
    perm = owner_perm.reshape(batch_ways, owned)
    if wide:
        perm_other = fabric.to_x(perm)
    else:
        perm_all = lax.all_gather(perm, "mp", axis=0, axis_index_groups=fabric.same_groups)
        panel_ids = jnp.arange(panels, dtype=jnp.int32)[:, None, None]
        places = places_of(perm_all, panel_ids, panels, *layout)

    if wide:
        rings = batch_ways // 2
        z_at, y_at = lax.div(dp_at, 2), lax.rem(dp_at, 2)
        table, table_back = tables(
            jnp.stack([z_at, y_at, row_at]), perm, perm_other, rings, layout
        )
        low_half, high_half = (0, 0, blocks_a), (half_a, blocks_a, blocks_b)
        at_extra = blocks_a * DH

        def piece(entry, *halves):
            return [(row, entry, first, count) for row, first, count in halves]

        def near_of(k):
            return [
                (value, piece(4 * k + i, low_half, high_half), at_extra)
                for i, value in enumerate((ring, by_x, by_y))
            ]

        def far_of(k):
            return [
                (far_a[k], piece(4 * k + 3, low_half), at_extra),
                (far_b[k], piece(4 * k + 3, (0, blocks_a, blocks_b)), None),
            ]

        near, far_a, far_b = [], [], []
        ring = own
        for k in range(rings):
            if k:
                deps = [table] if k == 1 else [far_a[k - 2], far_b[k - 2]]
                ring = gate(after, [by_x, by_y] + deps, pltpu.VMEM)
            after = fabric.to_z(ring) if k + 1 < rings else None
            by_x, by_y = fabric.to_x(ring), fabric.to_y(ring)
            near.append(near_of(k))
            if k:
                low, high = halves(*last, half_a, [ring])
                far_a.append(fabric.to_x(low))
                far_b.append(fabric.to_y(high))
            last = (by_y, by_x)
        placed = None
        for k in range(rings - 1):
            parts = near[k] + (far_of(k - 1) if k else [])
            placed = place(table, *zip(*parts), panel_shapes, placed, [low])
        low, high = halves(*last, half_a, [far_a[-1], far_b[-1], placed[2]])
        far_a.append(fabric.to_x(low))
        far_b.append(fabric.to_y(high))
        placed = place(
            table, *zip(*(near[-1] + far_of(rings - 2))), panel_shapes, placed, [low]
        )
        w_near, w_ffn, extras = place(table, *zip(*far_of(rings - 1)), panel_shapes, placed)
        extras = extras.astype(jnp.float32)
    else:
        gathered = lax.all_gather(own, "mp", axis=0, axis_index_groups=fabric.same_groups)
        gathered = lax.all_gather(gathered, "dp", axis=0)
        entries = batch_ways * panels
        table = places.transpose(1, 0, 2).reshape(entries, owned)
        index = jnp.arange(entries, dtype=jnp.int32)[:, None]
        table = jnp.concatenate([table, jnp.broadcast_to(index, (entries, 16))], axis=1)
        extras = gathered[:, :, blocks_a * DH : half_a].astype(jnp.float32)
        stride = own.shape[0]
        flat = gathered.reshape(-1, 128)
        pieces = []
        for i in range(batch_ways * panels):
            pieces += [(i * stride, i, 0, blocks_a), (i * stride + half_a, i, blocks_a, blocks_b)]
        w_near, w_ffn, _ = place(table, [flat], [pieces], [None], panel_shapes)
        weights = jnp.concatenate([w_near, w_ffn], axis=0)

    extras = extras.reshape(batch_ways, panels, EXTRA * 128)
    head_all = extras[:, :, :head_part] + extras[:, :, head_part : 2 * head_part]
    begin = 2 * head_part
    shared_all = (
        extras[:, :, begin : begin + shared_part]
        + extras[:, :, begin + shared_part : begin + 2 * shared_part]
    )
    head_all = head_all.transpose(1, 0, 2).reshape(panels, head_count)
    if wide:
        shared_other = fabric.to_core(shared_all)
        first = place_at == 0
        shared = jnp.stack(
            [
                jnp.where(first, shared_all, shared_other),
                jnp.where(first, shared_other, shared_all),
            ],
            axis=2,
        )
    else:
        shared = lax.all_gather(
            shared_all, "mp", axis=0, axis_index_groups=fabric.row_groups
        ).transpose(1, 2, 0, 3)
    shared = shared.reshape(shared_count)

    bias_query = head_all[:, :head_width].reshape(q_rows)
    bias_value = head_all[:, head_width:].reshape(q_rows)
    bias_qkv = jnp.concatenate([bias_query, jnp.zeros((q_rows,), jnp.float32), bias_value])
    vectors = jnp.pad(shared[: 6 * model_width].reshape(6, model_width), ((0, 2), (0, 0)))
    bias_inner = shared[6 * model_width :].reshape(panels, ways, ffn_width)
    bias_local = lax.dynamic_index_in_dim(bias_inner, place_at, 1, keepdims=False).reshape(f_rows)
    if wide:
        bias_other = lax.dynamic_index_in_dim(bias_inner, 1 - place_at, 1, keepdims=False)
        bias_both = jnp.concatenate([bias_local, bias_other.reshape(f_rows)])

    lengths = lax.dynamic_index_in_dim(item_lengths, row_at, 0, keepdims=False)
    starts = jnp.cumsum(lengths) - lengths

    def shared_sums(sums, inner_all):
        lines = [sums[i] for i in (3, 0, 4, 5, 1, 2)] + [inner_all.reshape(ffn_total)]
        whole = fabric.row_sum(jnp.concatenate(lines))
        whole = whole.reshape(batch_ways, panels, ways, shared_part)
        return lax.dynamic_index_in_dim(whole, place_at, 2, keepdims=False)

    x_row = fabric.row_gather(x_in)
    bias_qkv = jnp.broadcast_to(bias_qkv[None], (8, 3 * q_rows))
    qkv = project_in(w_near, x_row, bias_qkv).reshape(3, q_rows, SLOTS)
    context, log_total = attend(starts, lengths, qkv)
    if wide:
        w_ffn = gate(w_ffn, [x_row])
        w_ffn_other = fabric.to_core(w_ffn)
        mine, got = fabric.gather_back(
            project(place_at, context, w_near, 3 * q_rows, [vectors, bias_both])
        )
        layer_value, hidden_grad, sums, inner_sums, grad_ffn, grad_ffn_other = layer_part(
            x_in, mine, got, out_grad, vectors, bias_both[None], w_ffn, w_ffn_other
        )
        hidden_parts = fabric.share(hidden_grad)
        inner = [
            part.reshape(panels, ffn_width) for part in (inner_sums[0, :f_rows], inner_sums[0, f_rows:])
        ]
        inner_all = jnp.where(
            place_at == 0, jnp.stack(inner, axis=1), jnp.stack(inner[::-1], axis=1)
        )
        shared_grad = shared_sums(sums, inner_all)
        grad_ffn_got = fabric.to_core(gate(grad_ffn_other, [hidden_parts[1], shared_grad]))
        dcontext, grad_near = project_back(
            place_at, w_near, context, *hidden_parts, 3 * q_rows, [shared_grad]
        )
    else:
        w_out, w_qkv = w_near[3 * q_rows :], w_near[: 3 * q_rows]
        mine, got = fabric.gather_back([product(context, w_out, 0, 0)])
        low = (model_width, LOW)
        middle, middle_scaled, middle_inverse = by_rows(
            norm_one_step, (x_in, mine, got), vectors, (low, low, (128, jnp.float32)), False
        )
        middle_parts = fabric.share(middle)
        activated, slopes, results = ffn(middle_parts, weights, 4 * q_rows, bias_local[None])
        mine, got = fabric.gather_back(results)
        layer_value, resid_grad, sums_two = by_rows(
            norm_two_step, (middle, mine, got, out_grad), vectors, (low, low), True
        )
        resid_parts = fabric.share(resid_grad)
        before_grads, results, inner_sums = ffn_back(resid_parts, weights, 4 * q_rows, slopes)
        mine, got = fabric.gather_back(results)
        hidden_grad, sums_one = by_rows(
            norm_back_step,
            (resid_grad, mine, got, middle_scaled, middle_inverse),
            vectors,
            (low,),
            True,
        )
        grads = ffn_grad(
            activated, resid_parts, before_grads, middle_parts, panel_shape, 4 * q_rows
        )
        hidden_parts = fabric.share(hidden_grad)
        dcontext = product(w_out, hidden_parts[0], 1, 1).astype(LOW)
        part = product(context, hidden_parts[0], 1, 0).astype(LOW)
        grad_near = lax.dynamic_update_slice_in_dim(grads, part, 3 * q_rows, 0)
        sums = jnp.concatenate([sums_two[:3], sums_one[:3]], axis=0)
        inner_all = lax.dynamic_update_slice(
            jnp.zeros((panels, ways, ffn_width), jnp.float32),
            inner_sums[0].reshape(panels, 1, ffn_width),
            (0, place_at, 0),
        )
        shared_grad = shared_sums(sums, inner_all)
    qkv_grad = attend_back(starts, lengths, qkv, context, dcontext, log_total)
    qkv_grad = qkv_grad.reshape(3 * q_rows, SLOTS)
    grad_near, column_sums = last_grad(qkv_grad, x_row, grad_near)
    column_sums = column_sums[0]
    head_grad = jnp.concatenate(
        [
            column_sums[:q_rows].reshape(panels, head_width),
            column_sums[2 * q_rows :].reshape(panels, head_width),
        ],
        axis=1,
    )
    head_grad = head_grad.reshape(panels, batch_ways, head_part).transpose(1, 0, 2)
    extra_grad = jnp.concatenate([head_grad, shared_grad], axis=2).astype(LOW)
    extra_grad = jnp.pad(
        extra_grad, ((0, 0), (0, 0), (0, EXTRA * 128 - head_part - shared_part))
    ).reshape(batch_ways * panels, EXTRA, 128)

    if wide:
        half_b = blocks_b * DH

        def low_of(k, entries):
            parts = []
            for i, entry in enumerate(entries):
                parts.append((i * half_a, 4 * k + entry, 0, blocks_a))
                parts.append((i * half_a + blocks_a * DH, 4 * k + entry, 0, 0))
            return parts

        def high_of(k, entries):
            return [
                (i * half_b, 4 * k + entry, blocks_a, blocks_b) for i, entry in enumerate(entries)
            ]

        sent, kept, far, order = {}, {}, {}, []

        def gather(pieces):
            result = fetch(table_back, (grad_near, grad_ffn, grad_ffn_got), extra_grad, pieces, order)
            order[:] = [result[0]]
            return result

        def whole_of(k, entry):
            at = 4 * k + entry
            return [
                (0, at, 0, blocks_a),
                (blocks_a * DH, at, 0, 0),
                (half_a, at, blocks_a, blocks_b),
            ]

        def send(k, after):
            send_x, send_y = gather([low_of(k, (1, 3)), high_of(k, (2, 3))])
            got = fabric.to_x(gate(send_x, after)), fabric.to_y(gate(send_y, after))
            sent[k] = [(value, value) for value in got]

        def keep(k):
            kept[k] = gather([low_of(k, (0, 2)), high_of(k, (0, 1))])

        def pass_on(k):
            sum_a, sum_b = turn(kept[k][0], sent[k][0][1], kept[k][1], sent[k][1][1], order)
            far[k] = fabric.to_y(sum_a), fabric.to_x(sum_b)
            order[:] = [sum_a]

        def finish(k, running):
            half = [(kept[k][i], sent[k][i][0], far[k][i]) for i in range(2)]
            result = total(*half, running, order)
            order[:] = [result]
            return fabric.to_z(result)

        last = rings - 1
        (diagonal,) = gather([whole_of(last, 3)])
        diagonal = fabric.to_z(diagonal)
        send_x, send_y = gather([whole_of(last, 1), whole_of(last, 2)])
        got_x, got_y = fabric.to_x(send_x), fabric.to_y(send_y)
        near = gather([low_of(last - 1, (1,)), high_of(last - 1, (2,))])
        got_near = fabric.to_x(near[0]), fabric.to_y(near[1])
        send_x, send_y = gather([low_of(last - 1, (3,)), high_of(last - 1, (3,))])
        (here,) = gather([whole_of(last, 0)])
        keep(last - 1)
        mine, theirs = project(place_at, qkv_grad, w_near, 0, order, TINY)
        running, send_x, send_y = merge(
            send_x, send_y, diagonal, [here, got_x, got_y], [theirs, *got_near]
        )
        order[:] = [send_x]
        running = fabric.to_z(running)
        got_far = fabric.to_x(send_x), fabric.to_y(send_y)
        sent[last - 1] = list(zip(got_near, got_far))
        for k in range(last - 1, -1, -1):
            pass_on(k)
            if k:
                send(k - 1, far[k])
                running = finish(k, running)
                keep(k - 1)
        final = [(kept[0][i], sent[0][i][0], far[0][i]) for i in range(2)]
    else:
        pieces = []
        for i in range(batch_ways * panels):
            base = i * own.shape[0]
            pieces += [
                (base, i, 0, blocks_a),
                (base + blocks_a * DH, i, 0, 0),
                (base + half_a, i, blocks_a, blocks_b),
            ]
        chunks = fetch_all(table, grad_near, extra_grad, pieces)
        chunks = chunks.reshape(batch_ways, panels, own.shape[0], 128)
        chunks = lax.psum_scatter(chunks, "dp", scatter_dimension=0, tiled=False)
        reduced = lax.psum_scatter(
            chunks,
            "mp",
            scatter_dimension=0,
            tiled=False,
            axis_index_groups=fabric.same_groups,
        ).astype(jnp.float32)

        block_grads = jnp.concatenate([reduced[: blocks_a * DH], reduced[half_a:]], axis=0)
        vector_grads = reduced[blocks_a * DH : half_a]

    scale = 1.0 / (shard_rows * model_ways * batch_ways)
    state = (
        left_roots[0],
        right_roots[0],
        left_stats[0],
        right_stats[0],
        jnp.swapaxes(weight_store[0], 1, 2),
    )
    if wide:
        block_grads, vector_grads, *renewed = last_step(scale, *final, running, *state)
        mine, got = fabric.gather_back((mine, theirs))
    else:
        block_grads = block_grads.reshape(owned, DH, 128)
        renewed = shampoo(scale, block_grads, *state)
        mine, got = fabric.gather_back([product(qkv_grad, w_qkv, 0, 0)])
    new_left, new_right, new_weights = renewed
    input_grad = sum(v.astype(jnp.float32) for v in (hidden_grad, mine, got))
    vector_grads = vector_grads.reshape(EXTRA * 128)
    head_grad_mine = vector_grads[:head_part]
    shared_grad_mine = vector_grads[head_part : head_part + shared_part]

    head_one, head_two, head_new = adam_update(
        head_vectors[0], head_first[0], head_second[0], head_grad_mine
    )
    shared_one, shared_two, shared_new = adam_update(
        shared_vectors, shared_first, shared_second, shared_grad_mine
    )
    return (
        layer_value,
        input_grad,
        jnp.swapaxes(block_grads, 1, 2)[None],
        new_left[None],
        new_right[None],
        jnp.swapaxes(new_weights, 1, 2)[None],
        head_one[None],
        head_two[None],
        head_new[None],
        shared_one,
        shared_two,
        shared_new,
    )


def solution(mesh):
    rows, blocks, vector, head = P(BOTH, None), P("mp", "dp", None, None), P(BOTH), P("mp", "dp")
    return jax.shard_map(
        partial(shards, (mesh.shape["dp"], mesh.shape["mp"])),
        mesh=mesh,
        in_specs=(rows, rows, P("dp", None), blocks, P("mp", None))
        + (blocks,) * 4
        + (head,) * 3
        + (vector,) * 3,
        out_specs=(rows, rows) + (blocks,) * 4 + (head,) * 3 + (vector,) * 3,
        check_vma=False,
    )
```

```python
from functools import partial

import jax
import jax.numpy as jnp
from jax import lax
from jax.experimental import pallas as pl
from jax.experimental.pallas import tpu as pltpu
from jax.sharding import PartitionSpec as P

DH = 64
SLOTS = 1024
STEP = 10
SHORT = 128
LONG = 512
EXTRA = 16
SCOPED = 14
FINE = 32
WIDE = 1024
WHOLE = 2048
LOW = jnp.bfloat16
BOTH = ("dp", "mp")
ANY = pl.BlockSpec(memory_space=pl.ANY)
VMEM = pl.BlockSpec(memory_space=pltpu.VMEM)
SMEM = pl.BlockSpec(memory_space=pltpu.SMEM)
FREE = pl.CostEstimate(flops=0, bytes_accessed=0, transcendentals=0)
TINY = pl.CostEstimate(flops=10**6, bytes_accessed=10**4, transcendentals=0)
MOVE = pl.CostEstimate(flops=0, bytes_accessed=2**24, transcendentals=0)


def sems(n):
    return pltpu.SemaphoreType.DMA((n,))


def in_hbm(value):
    return pltpu.with_memory_space_constraint(value, pltpu.HBM)


def product(left, right, left_dim, right_dim):
    return lax.dot_general(
        left, right, (((left_dim,), (right_dim,)), ((), ())), preferred_element_type=jnp.float32
    )


def adam_update(current, moment_one, moment_two, gradient):
    first_new = 0.9 * moment_one + 0.1 * gradient
    second_new = 0.999 * moment_two + 0.001 * gradient * gradient
    stepped = first_new / (1.0 - 0.9**STEP) / (jnp.sqrt(second_new / (1.0 - 0.999**STEP)) + 1e-08)
    return (first_new, second_new, current - 0.3 * stepped)


def gelu_pair(before):
    below = 0.5 + 0.5 * lax.erf(before * 0.5**0.5)
    slope = below + before * jnp.exp(before * before * -0.5) * 0.3989422804014327
    return before * below, slope


def attend_kernel(start_ref, length_ref, qkv_ref, ctx_ref, lse_ref):
    def item(begin, size):
        here = pl.ds(begin, size)
        for g in range(lse_ref.shape[0]):
            head = pl.ds(g * DH, DH)
            scores = product(qkv_ref[1, head, here], qkv_ref[0, head, here], 0, 0)
            top = jnp.max(scores, axis=0, keepdims=True)
            expo = jnp.exp(scores - top)
            total = jnp.sum(expo, axis=0, keepdims=True)
            ctx = product(qkv_ref[2, head, here], expo.astype(LOW), 1, 0) / total
            ctx_ref[head, here] = ctx.astype(LOW)
            lse_ref[g, :, here] = top + jnp.log(total)

    each_item(start_ref, length_ref, item)


def each_item(start_ref, length_ref, item):
    @pl.loop(0, start_ref.shape[0])
    def _(i):
        begin = pl.multiple_of(start_ref[i], SHORT)

        @pl.when(length_ref[i] == LONG)
        def _():
            item(begin, LONG)

        @pl.when(length_ref[i] == SHORT)
        def _():
            item(begin, SHORT)


def attend_back_kernel(
    start_ref, length_ref, qkv_ref, ctx_ref, dctx_ref, lse_ref, out_ref
):
    def item(begin, size):
        here = pl.ds(begin, size)
        for g in range(lse_ref.shape[0]):
            head = pl.ds(g * DH, DH)
            queries, keys, values = (qkv_ref[i, head, here] for i in range(3))
            dctx = dctx_ref[head, here]
            probs = jnp.exp(product(keys, queries, 0, 0) - lse_ref[g, :, here])
            dprobs = product(values, dctx, 0, 0)
            delta = jnp.sum(
                dctx.astype(jnp.float32) * ctx_ref[head, here].astype(jnp.float32),
                axis=0,
                keepdims=True,
            )
            dscores = (probs * (dprobs - delta)).astype(LOW)
            out_ref[0, head, here] = (product(keys, dscores, 1, 0) * DH**-0.5).astype(LOW)
            out_ref[1, head, here] = product(queries, dscores, 1, 1).astype(LOW)
            out_ref[2, head, here] = product(dctx, probs.astype(LOW), 1, 1).astype(LOW)

    each_item(start_ref, length_ref, item)


def attend(starts, lengths, qkv):
    heads = qkv.shape[1] // DH
    group = min(heads, 8)
    return pl.pallas_call(
        attend_kernel,
        out_shape=(
            jax.ShapeDtypeStruct(qkv.shape[1:], LOW),
            jax.ShapeDtypeStruct((heads, 1, SLOTS), jnp.float32),
        ),
        grid_spec=pltpu.PrefetchScalarGridSpec(
            num_scalar_prefetch=2,
            grid=(heads // group,),
            in_specs=[pl.BlockSpec((3, group * DH, SLOTS), lambda h, *_: (0, h, 0))],
            out_specs=(
                pl.BlockSpec((group * DH, SLOTS), lambda h, *_: (h, 0)),
                pl.BlockSpec((group, 1, SLOTS), lambda h, *_: (h, 0, 0)),
            ),
        ),
        compiler_params=pltpu.CompilerParams(vmem_limit_bytes=28 * 2**20),
        cost_estimate=pl.CostEstimate(
            flops=heads * SLOTS * LONG * 1024, bytes_accessed=2**22, transcendentals=heads * 2**19
        ),
    )(starts, lengths, qkv)


def attend_back(starts, lengths, qkv, ctx, dctx, lse):
    heads = qkv.shape[1] // DH
    group = min(heads, 4)
    one = pl.BlockSpec((group * DH, SLOTS), lambda h, *_: (h, 0))
    three = pl.BlockSpec((3, group * DH, SLOTS), lambda h, *_: (0, h, 0))
    return pl.pallas_call(
        attend_back_kernel,
        out_shape=jax.ShapeDtypeStruct(qkv.shape, LOW),
        grid_spec=pltpu.PrefetchScalarGridSpec(
            num_scalar_prefetch=2,
            grid=(heads // group,),
            in_specs=[three, one, one, pl.BlockSpec((group, 1, SLOTS), lambda h, *_: (h, 0, 0))],
            out_specs=three,
        ),
        compiler_params=pltpu.CompilerParams(vmem_limit_bytes=28 * 2**20),
        cost_estimate=pl.CostEstimate(
            flops=heads * SLOTS * LONG * 2560, bytes_accessed=2**23, transcendentals=heads * 2**19
        ),
    )(starts, lengths, qkv, ctx, dctx, lse)


def tile_at(ref, place, groups):
    shift = groups.bit_length() - 1
    row = pl.multiple_of(lax.shift_right_logical(place, shift) * DH, DH)
    col = pl.multiple_of((place & (groups - 1)) * 128, 128)
    return ref.at[pl.ds(row, DH), pl.ds(col, 128)]


def place_kernel(pieces, extra_rows, count, more, table_ref, *refs):
    sources, refs = refs[:count], refs[count + more :]
    near_ref, ffn_ref, extra_ref = refs[:3]
    buffers, sems = refs[3:-1], refs[-1]
    arriving = [
        pltpu.make_async_copy(source, buffer, sems.at[2 * count + i])
        for i, (source, buffer) in enumerate(zip(sources, buffers))
    ]
    for copy in arriving:
        copy.start()
    groups = near_ref.shape[1] // 128
    bound = near_ref.shape[0] // DH * groups
    owned = table_ref.shape[1] - 16
    for i, (source, parts) in enumerate(zip(buffers, pieces)):
        arriving[i].wait()
        for row, entry, first, blocks in parts:

            @pl.loop(0, blocks, unroll=min(blocks, 8))
            def _(j):
                at = table_ref[entry, first + j]
                block = source.at[pl.ds(pl.multiple_of(row + j * DH, 16), DH), :]

                @pl.when(at < bound)
                def _():
                    target = tile_at(near_ref, at, groups)
                    pltpu.make_async_copy(block, target, sems.at[i]).start()

                @pl.when(at >= bound)
                def _():
                    target = tile_at(ffn_ref, at - bound, groups)
                    pltpu.make_async_copy(block, target, sems.at[i]).start()

        if extra_rows[i] is not None:
            pltpu.make_async_copy(
                source.at[pl.ds(extra_rows[i], EXTRA), :],
                extra_ref.at[table_ref[parts[0][1], owned]],
                sems.at[count + i],
            ).start()

    for i, parts in enumerate(pieces):
        total = sum(part[3] for part in parts) * DH
        if total <= ffn_ref.shape[0]:
            landed = [ffn_ref.at[pl.ds(0, total), pl.ds(0, 128)]]
        else:
            landed = [near_ref, ffn_ref]
        for ref in landed:
            pltpu.make_async_copy(ref, ref, sems.at[i]).wait()
        if extra_rows[i] is not None:
            pltpu.make_async_copy(extra_ref.at[0], extra_ref.at[0], sems.at[count + i]).wait()


def place(table, sources, pieces, extra_rows, shapes, previous=None, deps=()):
    chained = previous is not None
    more = [in_hbm(v) for v in previous] if chained else []
    count = len(sources)
    return pl.pallas_call(
        partial(place_kernel, pieces, extra_rows, count, len(more) + len(deps)),
        out_shape=tuple(pltpu.HBM(shape, LOW) for shape in shapes)
        + (pltpu.HBM((table.shape[0], EXTRA, 128), LOW),),
        grid_spec=pltpu.PrefetchScalarGridSpec(
            num_scalar_prefetch=1,
            grid=(),
            in_specs=[ANY] * (count + len(more) + len(deps)),
            out_specs=(ANY,) * 3,
            scratch_shapes=[pltpu.VMEM(v.shape, LOW) for v in sources] + [sems(3 * count)],
        ),
        cost_estimate=FREE,
        compiler_params=pltpu.CompilerParams(vmem_limit_bytes=12 * 2**20),
        input_output_aliases={1 + count + i: i for i in range(3)} if chained else {},
    )(table, *[v if v.shape[0] < WHOLE else in_hbm(v) for v in sources], *more, *deps)


def gate_kernel(*refs):
    pass


def gate(value, deps, space=None):
    shape = jax.ShapeDtypeStruct(value.shape, value.dtype)
    return pl.pallas_call(
        gate_kernel,
        out_shape=space(value.shape, value.dtype) if space else shape,
        in_specs=[ANY] * (1 + len(deps)),
        out_specs=ANY,
        cost_estimate=FREE,
        input_output_aliases={0: 0},
    )(pltpu.with_memory_space_constraint(value, space) if space else value, *deps)


def halves_kernel(low, high, *refs):
    out_low, out_high = refs[-2:]
    out_low[...] = low[pl.ds(0, out_low.shape[0])]
    out_high[...] = high[pl.ds(low.shape[0] - out_high.shape[0], out_high.shape[0])]


def halves(low, high, rows, deps=()):
    rest = high.shape[0] - rows
    return pl.pallas_call(
        halves_kernel,
        out_shape=tuple(jax.ShapeDtypeStruct((n, 128), LOW) for n in (rows, rest)),
        in_specs=[VMEM] * 2 + [ANY] * len(deps),
        out_specs=(VMEM,) * 2,
        cost_estimate=FREE,
        compiler_params=pltpu.CompilerParams(vmem_limit_bytes=12 * 2**20),
    )(low, high, *deps)


def fetch_kernel(pieces, deps, table_ref, near_ref, ffn_ref, other_ref, zero_ref, extra_ref, *refs):
    count = len(pieces)
    outs, others, sems = refs[deps : deps + count], refs[deps + count : -1], refs[-1]
    groups = near_ref.shape[1] // 128
    bound = near_ref.shape[0] // DH * groups
    owned = table_ref.shape[1] - 16
    for i, parts in enumerate(pieces):
        for row, entry, first, blocks in parts:
            if blocks == 0:
                pltpu.make_async_copy(
                    extra_ref.at[table_ref[entry, owned]],
                    outs[i].at[pl.ds(row, EXTRA), :],
                    sems.at[i],
                ).start()
                continue

            @pl.loop(0, blocks, unroll=min(blocks, 8))
            def _(j):
                at = table_ref[entry, first + j]
                here = pl.ds(pl.multiple_of(row + j * DH, 16), DH)

                def take(source, other):
                    pltpu.make_async_copy(source, outs[i].at[here, :], sems.at[i]).start()
                    pltpu.make_async_copy(
                        other, others[i].at[here, :], sems.at[count + i]
                    ).start()

                @pl.when(at < bound)
                def _():
                    take(tile_at(near_ref, at, groups), zero_ref)

                @pl.when(at >= bound)
                def _():
                    take(
                        tile_at(ffn_ref, at - bound, groups),
                        tile_at(other_ref, at - bound, groups),
                    )

    for i, parts in enumerate(pieces):
        pltpu.make_async_copy(outs[i], outs[i], sems.at[i]).wait()
        rows = sum(part[3] for part in parts) * DH
        landed = others[i].at[pl.ds(0, rows), :]
        pltpu.make_async_copy(landed, landed, sems.at[count + i]).wait()
        for row, _, _, blocks in parts:
            if blocks:
                here = pl.ds(row, blocks * DH)
                value = outs[i][here].astype(jnp.float32) + others[i][here].astype(jnp.float32)
                outs[i][here] = value.astype(LOW)


def fetch(table, grads, extra, pieces, deps=()):
    rows = [sum(part[3] * DH or EXTRA for part in parts) for parts in pieces]
    zero = jnp.zeros((DH, 128), LOW)
    return pl.pallas_call(
        partial(fetch_kernel, pieces, len(deps)),
        out_shape=tuple(jax.ShapeDtypeStruct((n, 128), LOW) for n in rows),
        grid_spec=pltpu.PrefetchScalarGridSpec(
            num_scalar_prefetch=1,
            grid=(),
            in_specs=[ANY] * (5 + len(deps)),
            out_specs=(VMEM,) * len(pieces),
            scratch_shapes=[pltpu.VMEM((n, 128), LOW) for n in rows]
            + [pltpu.SemaphoreType.DMA((2 * len(pieces),))],
        ),
        cost_estimate=FREE,
        compiler_params=pltpu.CompilerParams(vmem_limit_bytes=12 * 2**20),
    )(table, *[in_hbm(g) for g in grads], zero, extra, *deps)


def fetch_all_kernel(pieces, table_ref, grad_ref, extra_ref, out, sem):
    groups = grad_ref.shape[1] // 128
    owned = table_ref.shape[1] - 16
    for row, entry, first, blocks in pieces:
        if blocks == 0:
            pltpu.make_async_copy(
                extra_ref.at[table_ref[entry, owned]], out.at[pl.ds(row, EXTRA), :], sem.at[0]
            ).start()
            continue

        @pl.loop(0, blocks)
        def _(j):
            pltpu.make_async_copy(
                tile_at(grad_ref, table_ref[entry, first + j], groups),
                out.at[pl.ds(pl.multiple_of(row + j * DH, 16), DH), :],
                sem.at[0],
            ).start()

    pltpu.make_async_copy(out, out, sem.at[0]).wait()


def fetch_all(table, grad, extra, pieces):
    rows = sum(part[3] * DH or EXTRA for part in pieces)
    return pl.pallas_call(
        partial(fetch_all_kernel, pieces),
        out_shape=jax.ShapeDtypeStruct((rows, 128), LOW),
        grid_spec=pltpu.PrefetchScalarGridSpec(
            num_scalar_prefetch=1,
            grid=(),
            in_specs=[ANY] * 2,
            out_specs=VMEM,
            scratch_shapes=[pltpu.SemaphoreType.DMA((1,))],
        ),
        compiler_params=pltpu.CompilerParams(vmem_limit_bytes=16 * 2**20),
    )(table, in_hbm(grad), extra)


def turn_kernel(deps, keep_a, got_a, keep_b, got_b, *refs):
    for keep, got, out in zip((keep_a, keep_b), (got_a, got_b), refs[deps:]):
        size = out.shape[0]
        parts = [ref[pl.ds(ref.shape[0] - size, size)] for ref in (keep, got)]
        out[...] = sum(part.astype(jnp.float32) for part in parts).astype(LOW)


def turn(keep_a, got_a, keep_b, got_b, deps=()):
    return pl.pallas_call(
        partial(turn_kernel, len(deps)),
        out_shape=tuple(
            jax.ShapeDtypeStruct((keep.shape[0] // 2, 128), LOW) for keep in (keep_a, keep_b)
        ),
        in_specs=[VMEM] * 4 + [ANY] * len(deps),
        out_specs=(VMEM,) * 2,
        cost_estimate=FREE,
        compiler_params=pltpu.CompilerParams(vmem_limit_bytes=12 * 2**20),
    )(keep_a, got_a, keep_b, got_b, *deps)


def merge_kernel(deps, first, second, more, one, two, three, *refs):
    total, *outs = refs[deps:]
    row = 0
    for ref, out in zip((first, second), outs):
        size = ref.shape[0]
        value = ref[...].astype(jnp.float32) + more[pl.ds(row, size)].astype(jnp.float32)
        out[...] = value.astype(LOW)
        row += size
    total[...] = sum(ref[...].astype(jnp.float32) for ref in (one, two, three)).astype(LOW)


def merge(first, second, more, parts, deps):
    return pl.pallas_call(
        partial(merge_kernel, len(deps)),
        out_shape=tuple(jax.ShapeDtypeStruct(v.shape, LOW) for v in (parts[0], first, second)),
        in_specs=[VMEM] * 6 + [ANY] * len(deps),
        out_specs=(VMEM,) * 3,
        cost_estimate=FREE,
        compiler_params=pltpu.CompilerParams(vmem_limit_bytes=12 * 2**20),
    )(first, second, more, *parts, *deps)


def total_rows(half, running, start, row, rows):
    here = pl.ds(row, rows)
    result = sum(ref[here].astype(jnp.float32) for ref in half)
    if running is not None:
        result = result + running[pl.ds(start + row, rows)].astype(jnp.float32)
    return result


def total_kernel(chained, deps, *refs):
    running = refs[6] if chained else None
    out = refs[6 + chained + deps]
    start = 0
    for half in (refs[:3], refs[3:6]):
        size = half[2].shape[0]
        result = total_rows(half, running, start, 0, size)
        out[pl.ds(start, size)] = result.astype(out.dtype)
        start += size


def total(half_a, half_b, running, deps=()):
    chain = [] if running is None else [running]
    return pl.pallas_call(
        partial(total_kernel, len(chain), len(deps)),
        out_shape=jax.ShapeDtypeStruct((half_a[2].shape[0] + half_b[2].shape[0], 128), LOW),
        in_specs=[VMEM] * (6 + len(chain)) + [ANY] * len(deps),
        out_specs=VMEM,
        cost_estimate=FREE,
        compiler_params=pltpu.CompilerParams(vmem_limit_bytes=12 * 2**20),
    )(*half_a, *half_b, *chain, *deps)


def divided(value, by):
    shift = by.bit_length() - 1
    assert by == 1 << shift
    return lax.shift_right_logical(value, jnp.full_like(value, shift)), value & (by - 1)


def places_of(perm, panel, panels, heads64, ffn64, row_groups):
    col, row = divided(perm, row_groups)
    in_ffn = jnp.maximum(col - 4 * heads64, 0)
    kind, at = divided(col, heads64)
    ffn_kind, ffn_at = divided(in_ffn, ffn64)
    at_head = (kind * panels + panel) * heads64 + at
    at_ffn = 4 * heads64 * panels + (ffn_kind * panels + panel) * ffn64 + ffn_at
    return jnp.where(col < 4 * heads64, at_head, at_ffn) * row_groups + row


def tables_kernel(rings, sizes, at_ref, own_ref, other_ref, come_ref, go_ref):
    z_at, y_at, x_at = at_ref[0], at_ref[1], at_ref[2]
    owned = own_ref.shape[1]
    for sign, out in ((-1, come_ref), (1, go_ref)):
        for k in range(rings):
            z = lax.rem(z_at + sign * k + rings, rings)
            for y in range(2):
                dp = z * 2 + (y_at ^ y)
                for x, perm in enumerate((own_ref, other_ref)):
                    panel = x_at ^ x
                    entry = 4 * k + 2 * y + x
                    out[pl.ds(entry, 1), :] = jnp.full((1, out.shape[1]), dp * 2 + panel, jnp.int32)
                    out[pl.ds(entry, 1), pl.ds(0, owned)] = places_of(
                        perm[pl.ds(dp, 1), :], panel, 2, *sizes
                    )


def tables(at, own, other, rings, sizes):
    shape = jax.ShapeDtypeStruct((rings * 4, own.shape[1] + 16), jnp.int32)
    return pl.pallas_call(
        partial(tables_kernel, rings, sizes),
        out_shape=(shape, shape),
        in_specs=[SMEM, VMEM, VMEM],
        out_specs=(VMEM, VMEM),
        cost_estimate=FREE,
    )(at, own, other)


class Rows:
    def __init__(self, source, target, sems, first=0):
        rows = min(source.shape[0], target.shape[0])
        self.chunk = rows // sems.shape[0]
        self.copies = []
        for i in range(sems.shape[0]):
            here = pl.ds(i * self.chunk, self.chunk)
            there = pl.ds(first + i * self.chunk, self.chunk)
            self.copies.append(pltpu.make_async_copy(source.at[there], target.at[here], sems.at[i]))
        self.done = 0

    def start(self):
        for copy in self.copies:
            copy.start()
        return self

    def upto(self, rows):
        while self.done * self.chunk < rows and self.done < len(self.copies):
            self.copies[self.done].wait()
            self.done += 1

    def whole(self):
        self.upto(self.chunk * len(self.copies))


class Stream:
    def __init__(self, chunks, buffer, sems):
        slots = buffer.shape[0]
        self.buffer = buffer
        self.copies = [
            pltpu.make_async_copy(chunk, buffer.at[i % slots], sems.at[i % slots])
            for i, chunk in enumerate(chunks)
        ]
        self.used = 0
        for copy in self.copies[:slots]:
            copy.start()

    def next(self):
        slots = self.buffer.shape[0]
        ahead = self.used - 1 + slots
        if self.used and ahead < len(self.copies):
            self.copies[ahead].start()
        self.copies[self.used].wait()
        self.used += 1
        return self.buffer.at[(self.used - 1) % slots]


def row_chunks(weight, row, rows, size):
    return [weight.at[pl.ds(row + at, size), :] for at in range(0, rows, size)]


def column_chunks(weight, row, rows, size):
    return [weight.at[pl.ds(row, rows), pl.ds(at, size)] for at in range(0, weight.shape[1], size)]


class Tiles:
    def __init__(self, buffer, sems):
        self.buffer, self.sems, self.under_way = buffer, sems, []

    def put(self, value, target):
        slots = self.buffer.shape[0]
        slot = len(self.under_way) % slots
        if len(self.under_way) >= slots:
            self.under_way[-slots].wait()
        self.buffer[slot] = value
        copy = pltpu.make_async_copy(self.buffer.at[slot], target, self.sems.at[slot])
        copy.start()
        self.under_way.append(copy)

    def drain(self):
        for copy in self.under_way[-self.buffer.shape[0] :]:
            copy.wait()


def vmem(*shape, dtype=LOW):
    return pltpu.VMEM(shape, dtype)


def megabytes(n):
    return pltpu.CompilerParams(vmem_limit_bytes=n * 2**20)


def work(flops, moved=2**22, transcendentals=0):
    return pl.CostEstimate(flops=flops, bytes_accessed=moved, transcendentals=transcendentals)


def project_in_kernel(q_rows, weight, x, bias, out, w, w_sems):
    rows, tile = out.shape[0], w.shape[1]
    chunks = Stream(row_chunks(weight, 0, rows, tile), w, w_sems)
    for at in range(0, rows, tile):
        here = pl.ds(at, tile)
        value = product(chunks.next()[...], x[...], 1, 1) + jnp.transpose(bias[:, here])[:, :1]
        out[here, :] = (value * (DH**-0.5 if at < q_rows else 1.0)).astype(LOW)


def project_in(weights, x, bias):
    rows, width = bias.shape[1], weights.shape[1]
    return pl.pallas_call(
        partial(project_in_kernel, rows // 3),
        out_shape=jax.ShapeDtypeStruct((rows, x.shape[0]), LOW),
        in_specs=[ANY, VMEM, VMEM],
        out_specs=VMEM,
        scratch_shapes=[vmem(3, min(rows // 3, 512), width), sems(3)],
        compiler_params=megabytes(12),
        cost_estimate=work(2 * rows * x.shape[0] * x.shape[1]),
    )(in_hbm(weights), x, bias)


def project_kernel(row, deps, where_ref, context, weight, *refs):
    mine, theirs, w, w_sems, tiles, tile_sems = refs[deps:]
    loader = Rows(weight, w, w_sems, row).start()
    loader.whole()
    half = mine.shape[0]
    leaving = Tiles(tiles, tile_sems)
    for i, out in ((1, theirs), (0, mine)):
        at = pl.multiple_of((where_ref[0] ^ i) * half, half)
        leaving.put(product(context[:, pl.ds(at, half)], w[...], 0, 0).astype(LOW), out)
    leaving.drain()


def project(where, context, weights, row, deps=(), cost=None):
    features, tokens = context.shape
    width = weights.shape[1]
    out = pltpu.HBM((tokens // 2, width), LOW)
    return pl.pallas_call(
        partial(project_kernel, row, len(deps)),
        out_shape=(out, out),
        in_specs=[SMEM, VMEM, ANY] + [ANY] * len(deps),
        out_specs=(ANY, ANY),
        scratch_shapes=[
            vmem(features, width),
            sems(4),
            vmem(2, tokens // 2, width),
            sems(2),
        ],
        compiler_params=megabytes(14),
        cost_estimate=cost or work(2 * features * tokens * width),
    )(where[None], context, in_hbm(weights), *deps)


def ffn_kernel(parts, row, *refs):
    inputs, (weight, bias), refs = refs[:parts], refs[parts : parts + 2], refs[parts + 2 :]
    values, slopes, outs = refs[:parts], refs[parts : 2 * parts], refs[2 * parts : 3 * parts]
    first, first_sems, second, second_sems = refs[3 * parts :]
    hidden, tile = bias.shape[1], first.shape[1]
    chunks = Stream(row_chunks(weight, row, hidden, tile), first, first_sems)
    columns = Stream(
        column_chunks(weight, row + hidden, hidden, second.shape[2]), second, second_sems
    )
    for at in range(0, hidden, tile):
        here = pl.ds(at, tile)
        w = chunks.next()
        for i, x in enumerate(inputs):
            before = product(x[...], w[...], 1, 1) + bias[:, here]
            result, derivative = gelu_pair(before)
            values[i][:, here] = result.astype(LOW)
            slopes[i][:, here] = derivative.astype(LOW)
    finish_ffn(columns, values, outs)


def finish_ffn(columns, values, outs):
    tile = columns.buffer.shape[2]
    for at in range(0, outs[0].shape[1], tile):
        w = columns.next()
        for value, out in zip(values, outs):
            out[:, pl.ds(at, tile)] = product(value[...], w[...], 1, 0).astype(LOW)


def ffn_shapes(parts, hidden, width):
    tokens = parts[0].shape[0]
    low = [jax.ShapeDtypeStruct((tokens, hidden), LOW)] * len(parts)
    outs = [jax.ShapeDtypeStruct((tokens, width), LOW)] * len(parts)
    scratch = [vmem(2, min(hidden, 512), width), sems(2), vmem(2, hidden, 256), sems(2)]
    return low, outs, scratch


def ffn(parts, weights, row, bias):
    hidden, width, n = bias.shape[1], weights.shape[1], len(parts)
    low, outs, scratch = ffn_shapes(parts, hidden, width)
    result = pl.pallas_call(
        partial(ffn_kernel, n, row),
        out_shape=tuple(low + low + outs),
        in_specs=[VMEM] * n + [ANY, VMEM],
        out_specs=(VMEM,) * (3 * n),
        scratch_shapes=scratch,
        compiler_params=megabytes(SCOPED),
        cost_estimate=work(4 * SLOTS * hidden * width, 2**24, SLOTS * hidden),
    )(*parts, in_hbm(weights), bias)
    return result[:n], result[n : 2 * n], result[2 * n :]


def ffn_back_kernel(parts, row, *refs):
    inputs, weight, slopes = refs[:parts], refs[parts], refs[parts + 1 : 2 * parts + 1]
    refs = refs[2 * parts + 1 :]
    grads, outs, sums = refs[:parts], refs[parts : 2 * parts], refs[2 * parts]
    first, first_sems, second, second_sems = refs[2 * parts + 1 :]
    hidden, tile = sums.shape[1], first.shape[1]
    chunks = Stream(row_chunks(weight, row + hidden, hidden, tile), first, first_sems)
    columns = Stream(column_chunks(weight, row, hidden, second.shape[2]), second, second_sems)
    for at in range(0, hidden, tile):
        here = pl.ds(at, tile)
        w = chunks.next()
        total = 0.0
        for x, slope, grad in zip(inputs, slopes, grads):
            result = product(x[...], w[...], 1, 1) * slope[:, here].astype(jnp.float32)
            grad[:, here] = result.astype(LOW)
            total = total + jnp.sum(result, axis=0, keepdims=True)
        sums[:, here] = jnp.broadcast_to(total, (sums.shape[0], tile))
    finish_ffn(columns, grads, outs)


def ffn_back(parts, weights, row, slopes):
    hidden, width, n = slopes[0].shape[1], weights.shape[1], len(parts)
    low, outs, scratch = ffn_shapes(parts, hidden, width)
    result = pl.pallas_call(
        partial(ffn_back_kernel, n, row),
        out_shape=tuple(low + outs) + (jax.ShapeDtypeStruct((8, hidden), jnp.float32),),
        in_specs=[VMEM] * n + [ANY] + [VMEM] * n,
        out_specs=(VMEM,) * (2 * n + 1),
        scratch_shapes=scratch,
        compiler_params=megabytes(SCOPED),
        cost_estimate=work(4 * SLOTS * hidden * width, 2**24),
    )(*parts, in_hbm(weights), *slopes)
    return result[:n], result[n : 2 * n], result[-1]


def ffn_grad_kernel(parts, row, *refs):
    values, upper, grads, lower = (refs[i * parts : (i + 1) * parts] for i in range(4))
    out, tiles, tile_sems = refs[4 * parts :]
    leaving = Tiles(tiles, tile_sems)
    hidden, tile = values[0].shape[1], tiles.shape[1]
    for lefts, rights, begin in ((values, upper, row + hidden), (grads, lower, row)):
        for at in range(0, hidden, tile):
            here = pl.ds(at, tile)
            value = sum(product(a[:, here], b[...], 0, 0) for a, b in zip(lefts, rights))
            leaving.put(value.astype(LOW), out.at[pl.ds(begin + at, tile), :])
    leaving.drain()


def ffn_grad(values, upper, grads, lower, shape, row):
    n, hidden, width = len(values), values[0].shape[1], shape[1]
    return pl.pallas_call(
        partial(ffn_grad_kernel, n, row),
        out_shape=pltpu.HBM(shape, LOW),
        in_specs=[VMEM] * (4 * n),
        out_specs=ANY,
        scratch_shapes=[vmem(2, min(hidden, 512), width), sems(2)],
        compiler_params=megabytes(SCOPED),
        cost_estimate=work(4 * SLOTS * hidden * width, 2**24),
    )(*values, *upper, *grads, *lower)


def project_back_kernel(
    row, deps, where_ref, weight, context, own, other, *refs
):
    out, grad, w, w_sems, h, h_sems, c, c_sems, b, sem = refs[deps:]
    loader = Rows(weight, w, w_sems, row).start()
    hidden = [Rows(part, h.at[i], h_sems.at[i]).start() for i, part in enumerate((own, other))]
    context_rows = Rows(context, c, c_sems).start()
    half = own.shape[0]
    columns = [pl.ds(pl.multiple_of((where_ref[0] ^ i) * half, half), half) for i in range(2)]
    loader.whole()
    for i in range(2):
        hidden[i].whole()
        out[:, columns[i]] = product(w[...], h[i], 1, 1).astype(LOW)
    context_rows.whole()
    b[...] = sum(product(c[:, columns[i]], h[i], 1, 0) for i in range(2)).astype(LOW)
    copy = pltpu.make_async_copy(b, grad.at[pl.ds(row, b.shape[0]), :], sem.at[0])
    copy.start()
    copy.wait()


def project_back(where, weights, context, own, other, row, deps=()):
    features, tokens = context.shape
    width = own.shape[1]
    return pl.pallas_call(
        partial(project_back_kernel, row, len(deps)),
        out_shape=(
            jax.ShapeDtypeStruct((features, tokens), LOW),
            pltpu.HBM(weights.shape, LOW),
        ),
        in_specs=[SMEM] + [ANY] * (4 + len(deps)),
        out_specs=(VMEM, ANY),
        scratch_shapes=[
            vmem(features, width),
            sems(2),
            vmem(2, tokens // 2, width),
            pltpu.SemaphoreType.DMA((2, 2)),
            vmem(features, tokens),
            sems(2),
            vmem(features, width),
            sems(1),
        ],
        compiler_params=megabytes(SCOPED),
        cost_estimate=work(4 * features * tokens * width),
    )(where[None], *[in_hbm(v) for v in (weights, context, own, other)], *deps)


def last_grad_kernel(left, right, _, out, sums, tiles, tile_sems):
    leaving = Tiles(tiles, tile_sems)
    tile = tiles.shape[1]
    for at in range(0, left.shape[0], tile):
        here = pl.ds(at, tile)
        leaving.put(product(left[here, :], right[...], 1, 0).astype(LOW), out.at[here, :])
    sums[...] = product(jnp.ones((sums.shape[0], left.shape[1]), LOW), left[...], 1, 1)
    leaving.drain()


def last_grad(left, right, grads):
    rows, tokens = left.shape
    width = right.shape[1]
    tile = rows // 2
    return pl.pallas_call(
        last_grad_kernel,
        out_shape=(pltpu.HBM(grads.shape, LOW), jax.ShapeDtypeStruct((8, rows), jnp.float32)),
        in_specs=[VMEM, VMEM, ANY],
        out_specs=(ANY, VMEM),
        scratch_shapes=[vmem(2, tile, width), sems(2)],
        compiler_params=megabytes(SCOPED),
        cost_estimate=work(2 * rows * tokens * width),
        input_output_aliases={2: 0},
    )(left, right, in_hbm(grads))


BIAS_OUTPUT, BIAS_OUTER, GAIN_ONE, SHIFT_ONE, GAIN_TWO, SHIFT_TWO = range(6)


def row_of(vectors, i):
    return vectors[pl.ds(i, 1), :]


def mean_of(value):
    return jnp.mean(value, axis=-1, keepdims=True)


def widened(here, *refs):
    return sum(ref[here, :].astype(jnp.float32) for ref in refs)


def norm_one_step(here, vectors, x, mine, got, middle, scaled, inverse):
    hidden = widened(here, x, mine, got) + row_of(vectors, BIAS_OUTPUT)
    center = hidden - mean_of(hidden)
    factor = lax.rsqrt(mean_of(center * center) + 1e-05)
    normal = center * factor
    middle[here, :] = (
        normal * row_of(vectors, GAIN_ONE) + row_of(vectors, SHIFT_ONE)
    ).astype(LOW)
    scaled[here, :] = normal.astype(LOW)
    inverse[here, :] = jnp.broadcast_to(factor, (factor.shape[0], 128))
    return ()


def back_through(upstream, normal, factor, gain):
    gained = upstream * gain
    return factor * (gained - mean_of(gained) - normal * mean_of(gained * normal))


def norm_two_step(here, vectors, middle, mine, got, upstream, layer, dz):
    outer = widened(here, middle, mine, got) + row_of(vectors, BIAS_OUTER)
    center = outer - mean_of(outer)
    factor = lax.rsqrt(mean_of(center * center) + 1e-05)
    normal = center * factor
    gain = row_of(vectors, GAIN_TWO)
    layer[here, :] = (normal * gain + row_of(vectors, SHIFT_TWO)).astype(LOW)
    dy = widened(here, upstream)
    result = back_through(dy, normal, factor, gain)
    dz[here, :] = result.astype(LOW)
    return (result, dy * normal, dy)


def norm_back_step(here, vectors, dz, mine, got, scaled, inverse, dhidden):
    dy = widened(here, dz, mine, got)
    normal = widened(here, scaled)
    factor = inverse[here, :][:, :1]
    result = back_through(dy, normal, factor, row_of(vectors, GAIN_ONE))
    dhidden[here, :] = result.astype(LOW)
    return (result, dy * normal, dy)


def eight_rows(value):
    return sum(value[i : i + 8] for i in range(0, value.shape[0], 8))


def layer_kernel(
    x, mine, got, upstream, vectors, bias, w_own, w_other,
    layer, dhidden, sums, inner, g_own, g_other,
    x_in, mine_in, got_in, up_in, in_sems, act, slope, mid, normal, inverse, dz, acc, out,
    out_sems, one, one_sems, two, two_sems, tile_one, tile_one_sems, tile_two, tile_two_sems,
):
    rows = x.shape[0]
    half, tile = w_own.shape[0] // 2, one.shape[1]
    ones = [c for w in (w_own, w_other) for c in row_chunks(w, 0, half, tile)]
    twos = [c for w in (w_own, w_other) for c in row_chunks(w, half, half, tile)]
    arriving = [
        Rows(source, target, in_sems.at[i])
        for i, (source, target) in enumerate(
            ((x, x_in), (mine, mine_in), (got, got_in), (upstream, up_in))
        )
    ]
    for copies in arriving[:3]:
        copies.start()
    first, second = Stream(ones + ones, one, one_sems), Stream(twos + twos, two, two_sems)
    arriving[3].start()
    step = arriving[0].chunk
    places = [pl.ds(at, step) for at in range(0, rows, step)]

    for at in range(0, rows, FINE):
        for copies in arriving[:3]:
            copies.upto(at + FINE)
        norm_one_step(pl.ds(at, FINE), vectors, x_in, mine_in, got_in, mid, normal, inverse)

    before = product(mid[...], first.next()[...], 1, 1) + bias[:, pl.ds(0, tile)]
    for n in range(len(ones)):
        columns = pl.ds(n * tile, tile)
        down_weight = second.next()
        if n + 1 < len(ones):
            up_weight = first.next()
            after = product(mid[...], up_weight[...], 1, 1) + bias[:, pl.ds((n + 1) * tile, tile)]
        value, derivative = gelu_pair(before)
        before = after
        value = value.astype(LOW)
        act[:, columns] = value
        slope[:, columns] = derivative.astype(LOW)
        part = product(value, down_weight[...], 1, 0)
        if n:
            acc[...] += part
        else:
            acc[...] = part

    arriving[3].whole()
    leaving, totals = [], []
    for at in range(0, rows, FINE):
        here = pl.ds(at, FINE)
        outer = acc[here, :] + widened(here, mid) + row_of(vectors, BIAS_OUTER)
        center = outer - mean_of(outer)
        factor = lax.rsqrt(mean_of(center * center) + 1e-05)
        scaled = center * factor
        gain = row_of(vectors, GAIN_TWO)
        out[here, :] = (scaled * gain + row_of(vectors, SHIFT_TWO)).astype(LOW)
        dy = widened(here, up_in)
        result = back_through(dy, scaled, factor, gain)
        acc[here, :] = result
        dz[here, :] = result.astype(LOW)
        totals.append([eight_rows(v) for v in (result, dy * scaled, dy)])
        if (at + FINE) % step == 0:
            n = at // step
            leaving.append(
                pltpu.make_async_copy(out.at[places[n]], layer.at[places[n]], out_sems.at[n])
            )
            leaving[-1].start()

    grads_one, grads_two = Tiles(tile_one, tile_one_sems), Tiles(tile_two, tile_two_sems)
    for n in range(len(ones)):
        columns = pl.ds(n * tile, tile)
        target, begin = (g_own, n * tile) if n * tile < half else (g_other, n * tile - half)
        value = product(act[:, columns], dz[...], 0, 0)
        grads_two.put(value.astype(LOW), target.at[pl.ds(half + begin, tile), :])
        grad = product(dz[...], second.next()[...], 1, 1) * slope[:, columns].astype(jnp.float32)
        inner[:, columns] = jnp.broadcast_to(
            jnp.sum(grad, axis=0, keepdims=True), (inner.shape[0], tile)
        )
        slope[:, columns] = grad.astype(LOW)
        value = product(slope[:, columns], mid[...], 0, 0)
        grads_one.put(value.astype(LOW), target.at[pl.ds(begin, tile), :])
        acc[...] += product(slope[:, columns], first.next()[...], 1, 0)

    for at in range(0, rows, FINE):
        here = pl.ds(at, FINE)
        dy = acc[here, :]
        scaled = widened(here, normal)
        factor = inverse[here, :][:, :1]
        result = back_through(dy, scaled, factor, row_of(vectors, GAIN_ONE))
        got_in[here, :] = result.astype(LOW)
        totals.append([eight_rows(v) for v in (result, dy * scaled, dy)])
        if (at + FINE) % step == 0:
            n = at // step
            leaving.append(
                pltpu.make_async_copy(got_in.at[places[n]], dhidden.at[places[n]], in_sems.at[2, n])
            )
            leaving[-1].start()
    count = rows // FINE
    lines = [
        jnp.sum(sum(t[i] for t in part), axis=0, keepdims=True)
        for part in (totals[:count], totals[count:])
        for i in range(3)
    ]
    sums[...] = jnp.concatenate(lines + [jnp.zeros_like(lines[0])] * 2, axis=0)
    grads_one.drain()
    grads_two.drain()
    for copy in leaving:
        copy.wait()


def layer_part(x, mine, got, upstream, vectors, bias, w_own, w_other):
    rows, width = x.shape
    hidden = bias.shape[1]
    tile = WIDE
    low = jax.ShapeDtypeStruct((rows, width), LOW)
    grad = pltpu.HBM(w_own.shape, LOW)
    dma = pltpu.SemaphoreType.DMA
    return pl.pallas_call(
        layer_kernel,
        out_shape=(
            low,
            pltpu.HBM((rows, width), LOW),
            jax.ShapeDtypeStruct((8, width), jnp.float32),
            jax.ShapeDtypeStruct((8, hidden), jnp.float32),
            grad,
            grad,
        ),
        in_specs=[ANY] * 4 + [VMEM] * 2 + [ANY] * 2,
        out_specs=(ANY, ANY, VMEM, VMEM, ANY, ANY),
        scratch_shapes=[vmem(rows, width) for _ in range(4)]
        + [
            dma((4, 4)),
            vmem(rows, hidden),
            vmem(rows, hidden),
            vmem(rows, width),
            vmem(rows, width),
            vmem(rows, 128, dtype=jnp.float32),
            vmem(rows, width),
            vmem(rows, width, dtype=jnp.float32),
            vmem(rows, width),
            sems(4),
            vmem(2, tile, width),
            sems(2),
            vmem(2, tile, width),
            sems(2),
            vmem(1, tile, width),
            sems(1),
            vmem(1, tile, width),
            sems(1),
        ],
        compiler_params=megabytes(50),
        cost_estimate=work(12 * rows * hidden * width, 2**25, rows * hidden),
    )(in_hbm(x), in_hbm(mine), got, in_hbm(upstream), vectors, bias, in_hbm(w_own), in_hbm(w_other))


def rows_kernel(step, count, with_sums, vectors, *refs):
    inputs, outs = refs[:count], refs[count:]
    if with_sums:
        sums, outs = outs[-1], outs[:-1]
    rows = inputs[0].shape[0]
    tile = min(rows, 128)
    totals = 0
    for at in range(0, rows, tile):
        values = step(pl.ds(at, tile), vectors, *inputs, *outs)
        if with_sums:
            parts = [jnp.sum(value, axis=0, keepdims=True) for value in values]
            totals = totals + jnp.concatenate(parts + [jnp.zeros_like(parts[0])] * 5, axis=0)
    if with_sums:
        sums[...] = totals


def by_rows(step, inputs, vectors, outs, with_sums):
    rows, width = inputs[0].shape
    shapes = [jax.ShapeDtypeStruct((rows, n), dtype) for n, dtype in outs]
    if with_sums:
        shapes.append(jax.ShapeDtypeStruct((8, width), jnp.float32))
    return pl.pallas_call(
        partial(rows_kernel, step, len(inputs), with_sums),
        out_shape=tuple(shapes),
        in_specs=[VMEM] * (1 + len(inputs)),
        out_specs=(VMEM,) * len(shapes),
        compiler_params=megabytes(12),
        cost_estimate=work(40 * rows * width, 2**23, rows),
    )(vectors, *inputs)


def shampoo_blocks(scale, grad, left_root, right_root, left, right, weight, outs):
    new_left, new_right, new_weight = outs
    for i in range(grad.shape[0]):
        g = grad[i].astype(LOW)
        new_left[i] = 0.5 * left[i] + (0.5 * scale) * product(g, g, 0, 0)
        new_right[i] = 0.5 * right[i] + (0.5 * scale) * product(g, g, 1, 1)
        step = product(g, left_root[i].astype(LOW), 1, 1)
        step = product(right_root[i].astype(LOW), step.astype(LOW), 0, 0)
        here = weight[i]
        size = jnp.sqrt(jnp.mean(here * here, keepdims=True) + 1e-06)
        norm = jnp.sqrt(jnp.mean(step * step, keepdims=True) + 1e-06)
        new_weight[i] = here - (0.3 * size / norm) * step


def shampoo_kernel(scale, *refs):
    grad, inputs, outs = refs[0], refs[1:6], refs[6:]
    shampoo_blocks(scale, grad, *inputs, outs)


def last_kernel(scale, *refs):
    halves, running, inputs = (refs[:3], refs[3:6]), refs[6], refs[7:12]
    grad, extra, outs = refs[12], refs[13], refs[14:]
    blocks = grad.shape[0]
    at = pl.program_id(0)
    rows_a = halves[0][2].shape[0] - EXTRA
    steps_a = rows_a // (blocks * DH)

    def take(half, start, step):
        row = pl.multiple_of(step * blocks * DH, blocks * DH)
        value = total_rows(half, running, start, row, blocks * DH)
        grad[...] = value.reshape(blocks, DH, 128)

    @pl.when(at < steps_a)
    def _():
        take(halves[0], 0, at)

    @pl.when(at >= steps_a)
    def _():
        take(halves[1], rows_a + EXTRA, at - steps_a)

    extra[...] = total_rows(halves[0], running, 0, rows_a, EXTRA)
    shampoo_blocks(scale, grad, *inputs, outs)


def shampoo_specs(tile, values):
    return [pl.BlockSpec((tile,) + v.shape[1:], lambda i: (i, 0, 0)) for v in values]


def shampoo(scale, grad, *state):
    owned = grad.shape[0]
    tile = 8 if owned % 8 == 0 else owned
    return pl.pallas_call(
        partial(shampoo_kernel, scale),
        out_shape=tuple(jax.ShapeDtypeStruct(v.shape, jnp.float32) for v in state[2:]),
        grid=(owned // tile,),
        in_specs=shampoo_specs(tile, (grad, *state)),
        out_specs=tuple(shampoo_specs(tile, state[2:])),
        compiler_params=megabytes(16),
    )(grad, *state)


def last_step(scale, half_a, half_b, running, *state):
    owned = state[0].shape[0]
    tile = 8
    grad = jax.ShapeDtypeStruct((owned, DH, 128), jnp.float32)
    return pl.pallas_call(
        partial(last_kernel, scale),
        out_shape=(grad, jax.ShapeDtypeStruct((EXTRA, 128), jnp.float32))
        + tuple(jax.ShapeDtypeStruct(v.shape, jnp.float32) for v in state[2:]),
        grid=(owned // tile,),
        in_specs=[
            pl.BlockSpec(v.shape, lambda i: (0, 0)) for v in (*half_a, *half_b, running)
        ]
        + shampoo_specs(tile, state),
        out_specs=(
            *shampoo_specs(tile, (grad,)),
            pl.BlockSpec((EXTRA, 128), lambda i: (0, 0)),
            *shampoo_specs(tile, state[2:]),
        ),
        compiler_params=megabytes(32),
    )(*half_a, *half_b, running, *state)


class Fabric:
    def __init__(self, sizes, row_ways):
        self.batch, self.model = sizes
        self.ways = row_ways
        self.panels = self.model // row_ways
        self.wide = row_ways == 2 and self.panels == 2 and self.batch % 2 == 0
        self.row_groups = [
            list(range(i, i + row_ways)) for i in range(0, self.model, row_ways)
        ]
        self.same_groups = [list(range(t, self.model, row_ways)) for t in range(row_ways)]

    def send(self, value, move):
        pairs = []
        for d in range(self.batch):
            for m in range(self.model):
                e, n = move(d, m)
                pairs.append((d * self.model + m, (e % self.batch) * self.model + n))
        return lax.ppermute(value, BOTH, pairs)

    def to_core(self, value):
        return self.send(value, lambda d, m: (d, m ^ 1))

    def to_x(self, value):
        return self.send(value, lambda d, m: (d, m ^ 2))

    def to_y(self, value):
        return self.send(value, lambda d, m: (d ^ 1, m))

    def to_z(self, value):
        return self.send(value, lambda d, m: (d + 2, m))

    def row_gather(self, own):
        if self.wide:
            return self.join(self.share(own), 0)
        return lax.all_gather(own, "mp", axis=0, tiled=True, axis_index_groups=self.row_groups)

    def share(self, own):
        if self.wide:
            return [own, self.to_core(own)]
        return [self.row_gather(own)]

    def gather_back(self, parts):
        if self.wide:
            return parts[0].astype(LOW), self.to_core(parts[1].astype(LOW))
        mine = lax.psum_scatter(
            parts[0].astype(LOW),
            "mp",
            scatter_dimension=0,
            tiled=True,
            axis_index_groups=self.row_groups,
        )
        return mine, jnp.zeros(mine.shape, LOW)

    def cut(self, value, axis):
        if not self.wide:
            return [value]
        size = value.shape[axis] // 2
        core = lax.rem(lax.axis_index("mp"), 2)
        return [
            lax.dynamic_slice_in_dim(value, at * size, size, axis) for at in (core, 1 - core)
        ]

    def join(self, parts, axis):
        if not self.wide:
            return parts[0]
        own, other = parts
        first = lax.rem(lax.axis_index("mp"), 2) == 0
        return jnp.concatenate(
            [jnp.where(first, own, other), jnp.where(first, other, own)], axis=axis
        )

    def row_sum(self, value):
        if self.wide:
            return value + self.to_core(value)
        return lax.psum(value, "mp", axis_index_groups=self.row_groups)


def shards(
    sizes,
    x_in,
    out_grad,
    item_lengths,
    weight_store,
    owner_perm,
    left_roots,
    right_roots,
    left_stats,
    right_stats,
    head_vectors,
    head_first,
    head_second,
    shared_vectors,
    shared_first,
    shared_second,
):
    batch_ways, model_ways = sizes
    shard_rows, model_width = x_in.shape
    fabric = Fabric(sizes, SLOTS // shard_rows)
    ways, panels, wide = fabric.ways, fabric.panels, fabric.wide
    dp_at, mp_at = lax.axis_index("dp"), lax.axis_index("mp")
    row_at, place_at = lax.div(mp_at, ways), lax.rem(mp_at, ways)

    owned, row_block, col_block = weight_store.shape[1:]
    head_part, shared_part = head_vectors.shape[1], shared_vectors.shape[0]
    head_count, shared_count = head_part * batch_ways, shared_part * batch_ways * model_ways
    block_count = owner_perm.shape[1]
    row_groups = model_width // row_block
    head_width = model_width // model_ways
    ffn_total = shared_count - 6 * model_width
    ffn_width = ffn_total // model_ways
    heads64, ffn64 = head_width // DH, ffn_width // DH
    hidden_rows = panels * (4 * head_width + 2 * ffn_width)
    q_rows, f_rows = panels * head_width, panels * ffn_width
    panel_shape = (hidden_rows, model_width)
    panel_shapes = ((4 * q_rows, model_width), (2 * f_rows, model_width))
    half_a = (owned // 2) * DH + EXTRA
    blocks_a, blocks_b = owned // 2, owned - owned // 2

    def two_parts(value):
        high = lax.reduce_precision(value, 8, 7)
        return jnp.concatenate([high.astype(LOW), (value - high).astype(LOW)])

    blocks_low = jnp.swapaxes(weight_store[0], 1, 2).astype(LOW).reshape(owned * DH, 128)
    vectors = jnp.concatenate([two_parts(head_vectors[0]), two_parts(shared_vectors)])
    vectors = jnp.pad(vectors, (0, EXTRA * 128 - vectors.shape[0])).reshape(EXTRA, 128)
    own = jnp.concatenate(
        [blocks_low[: blocks_a * DH], vectors, blocks_low[blocks_a * DH :]], axis=0
    )

    layout = (heads64, ffn64, row_groups)
    perm = owner_perm.reshape(batch_ways, owned)
    if wide:
        perm_other = fabric.to_x(perm)
    else:
        perm_all = lax.all_gather(perm, "mp", axis=0, axis_index_groups=fabric.same_groups)
        panel_ids = jnp.arange(panels, dtype=jnp.int32)[:, None, None]
        places = places_of(perm_all, panel_ids, panels, *layout)

    if wide:
        rings = batch_ways // 2
        z_at, y_at = lax.div(dp_at, 2), lax.rem(dp_at, 2)
        table, table_back = tables(
            jnp.stack([z_at, y_at, row_at]), perm, perm_other, rings, layout
        )
        low_half, high_half = (0, 0, blocks_a), (half_a, blocks_a, blocks_b)
        at_extra = blocks_a * DH

        def piece(entry, *halves):
            return [(row, entry, first, count) for row, first, count in halves]

        def near_of(k):
            return [
                (value, piece(4 * k + i, low_half, high_half), at_extra)
                for i, value in enumerate((ring, by_x, by_y))
            ]

        def far_of(k):
            return [
                (far_a[k], piece(4 * k + 3, low_half), at_extra),
                (far_b[k], piece(4 * k + 3, (0, blocks_a, blocks_b)), None),
            ]

        near, far_a, far_b = [], [], []
        ring = own
        for k in range(rings):
            if k:
                deps = [table] if k == 1 else [far_a[k - 2], far_b[k - 2]]
                ring = gate(after, [by_x, by_y] + deps, pltpu.VMEM)
            after = fabric.to_z(ring) if k + 1 < rings else None
            by_x, by_y = fabric.to_x(ring), fabric.to_y(ring)
            near.append(near_of(k))
            if k:
                low, high = halves(*last, half_a, [ring])
                far_a.append(fabric.to_x(low))
                far_b.append(fabric.to_y(high))
            last = (by_y, by_x)
        placed = None
        for k in range(rings - 1):
            parts = near[k] + (far_of(k - 1) if k else [])
            placed = place(table, *zip(*parts), panel_shapes, placed, [low])
        low, high = halves(*last, half_a, [far_a[-1], far_b[-1], placed[2]])
        far_a.append(fabric.to_x(low))
        far_b.append(fabric.to_y(high))
        placed = place(
            table, *zip(*(near[-1] + far_of(rings - 2))), panel_shapes, placed, [low]
        )
        w_near, w_ffn, extras = place(table, *zip(*far_of(rings - 1)), panel_shapes, placed)
        extras = extras.astype(jnp.float32)
    else:
        gathered = lax.all_gather(own, "mp", axis=0, axis_index_groups=fabric.same_groups)
        gathered = lax.all_gather(gathered, "dp", axis=0)
        entries = batch_ways * panels
        table = places.transpose(1, 0, 2).reshape(entries, owned)
        index = jnp.arange(entries, dtype=jnp.int32)[:, None]
        table = jnp.concatenate([table, jnp.broadcast_to(index, (entries, 16))], axis=1)
        extras = gathered[:, :, blocks_a * DH : half_a].astype(jnp.float32)
        stride = own.shape[0]
        flat = gathered.reshape(-1, 128)
        pieces = []
        for i in range(batch_ways * panels):
            pieces += [(i * stride, i, 0, blocks_a), (i * stride + half_a, i, blocks_a, blocks_b)]
        w_near, w_ffn, _ = place(table, [flat], [pieces], [None], panel_shapes)
        weights = jnp.concatenate([w_near, w_ffn], axis=0)

    extras = extras.reshape(batch_ways, panels, EXTRA * 128)
    head_all = extras[:, :, :head_part] + extras[:, :, head_part : 2 * head_part]
    begin = 2 * head_part
    shared_all = (
        extras[:, :, begin : begin + shared_part]
        + extras[:, :, begin + shared_part : begin + 2 * shared_part]
    )
    head_all = head_all.transpose(1, 0, 2).reshape(panels, head_count)
    if wide:
        shared_other = fabric.to_core(shared_all)
        first = place_at == 0
        shared = jnp.stack(
            [
                jnp.where(first, shared_all, shared_other),
                jnp.where(first, shared_other, shared_all),
            ],
            axis=2,
        )
    else:
        shared = lax.all_gather(
            shared_all, "mp", axis=0, axis_index_groups=fabric.row_groups
        ).transpose(1, 2, 0, 3)
    shared = shared.reshape(shared_count)

    bias_query = head_all[:, :head_width].reshape(q_rows)
    bias_value = head_all[:, head_width:].reshape(q_rows)
    bias_qkv = jnp.concatenate([bias_query, jnp.zeros((q_rows,), jnp.float32), bias_value])
    vectors = jnp.pad(shared[: 6 * model_width].reshape(6, model_width), ((0, 2), (0, 0)))
    bias_inner = shared[6 * model_width :].reshape(panels, ways, ffn_width)
    bias_local = lax.dynamic_index_in_dim(bias_inner, place_at, 1, keepdims=False).reshape(f_rows)
    if wide:
        bias_other = lax.dynamic_index_in_dim(bias_inner, 1 - place_at, 1, keepdims=False)
        bias_both = jnp.concatenate([bias_local, bias_other.reshape(f_rows)])

    lengths = lax.dynamic_index_in_dim(item_lengths, row_at, 0, keepdims=False)
    starts = jnp.cumsum(lengths) - lengths

    def shared_sums(sums, inner_all):
        lines = [sums[i] for i in (3, 0, 4, 5, 1, 2)] + [inner_all.reshape(ffn_total)]
        whole = fabric.row_sum(jnp.concatenate(lines))
        whole = whole.reshape(batch_ways, panels, ways, shared_part)
        return lax.dynamic_index_in_dim(whole, place_at, 2, keepdims=False)

    x_row = fabric.row_gather(x_in)
    bias_qkv = jnp.broadcast_to(bias_qkv[None], (8, 3 * q_rows))
    qkv = project_in(w_near, x_row, bias_qkv).reshape(3, q_rows, SLOTS)
    context, log_total = attend(starts, lengths, qkv)
    if wide:
        w_ffn = gate(w_ffn, [x_row])
        w_ffn_other = fabric.to_core(w_ffn)
        mine, got = fabric.gather_back(
            project(place_at, context, w_near, 3 * q_rows, [vectors, bias_both])
        )
        layer_value, hidden_grad, sums, inner_sums, grad_ffn, grad_ffn_other = layer_part(
            x_in, mine, got, out_grad, vectors, bias_both[None], w_ffn, w_ffn_other
        )
        hidden_parts = fabric.share(hidden_grad)
        inner = [
            part.reshape(panels, ffn_width) for part in (inner_sums[0, :f_rows], inner_sums[0, f_rows:])
        ]
        inner_all = jnp.where(
            place_at == 0, jnp.stack(inner, axis=1), jnp.stack(inner[::-1], axis=1)
        )
        shared_grad = shared_sums(sums, inner_all)
        grad_ffn_got = fabric.to_core(gate(grad_ffn_other, [hidden_parts[1], shared_grad]))
        dcontext, grad_near = project_back(
            place_at, w_near, context, *hidden_parts, 3 * q_rows, [shared_grad]
        )
    else:
        w_out, w_qkv = w_near[3 * q_rows :], w_near[: 3 * q_rows]
        mine, got = fabric.gather_back([product(context, w_out, 0, 0)])
        low = (model_width, LOW)
        middle, middle_scaled, middle_inverse = by_rows(
            norm_one_step, (x_in, mine, got), vectors, (low, low, (128, jnp.float32)), False
        )
        middle_parts = fabric.share(middle)
        activated, slopes, results = ffn(middle_parts, weights, 4 * q_rows, bias_local[None])
        mine, got = fabric.gather_back(results)
        layer_value, resid_grad, sums_two = by_rows(
            norm_two_step, (middle, mine, got, out_grad), vectors, (low, low), True
        )
        resid_parts = fabric.share(resid_grad)
        before_grads, results, inner_sums = ffn_back(resid_parts, weights, 4 * q_rows, slopes)
        mine, got = fabric.gather_back(results)
        hidden_grad, sums_one = by_rows(
            norm_back_step,
            (resid_grad, mine, got, middle_scaled, middle_inverse),
            vectors,
            (low,),
            True,
        )
        grads = ffn_grad(
            activated, resid_parts, before_grads, middle_parts, panel_shape, 4 * q_rows
        )
        hidden_parts = fabric.share(hidden_grad)
        dcontext = product(w_out, hidden_parts[0], 1, 1).astype(LOW)
        part = product(context, hidden_parts[0], 1, 0).astype(LOW)
        grad_near = lax.dynamic_update_slice_in_dim(grads, part, 3 * q_rows, 0)
        sums = jnp.concatenate([sums_two[:3], sums_one[:3]], axis=0)
        inner_all = lax.dynamic_update_slice(
            jnp.zeros((panels, ways, ffn_width), jnp.float32),
            inner_sums[0].reshape(panels, 1, ffn_width),
            (0, place_at, 0),
        )
        shared_grad = shared_sums(sums, inner_all)
    qkv_grad = attend_back(starts, lengths, qkv, context, dcontext, log_total)
    qkv_grad = qkv_grad.reshape(3 * q_rows, SLOTS)
    grad_near, column_sums = last_grad(qkv_grad, x_row, grad_near)
    column_sums = column_sums[0]
    head_grad = jnp.concatenate(
        [
            column_sums[:q_rows].reshape(panels, head_width),
            column_sums[2 * q_rows :].reshape(panels, head_width),
        ],
        axis=1,
    )
    head_grad = head_grad.reshape(panels, batch_ways, head_part).transpose(1, 0, 2)
    extra_grad = jnp.concatenate([head_grad, shared_grad], axis=2).astype(LOW)
    extra_grad = jnp.pad(
        extra_grad, ((0, 0), (0, 0), (0, EXTRA * 128 - head_part - shared_part))
    ).reshape(batch_ways * panels, EXTRA, 128)

    if wide:
        half_b = blocks_b * DH

        def low_of(k, entries):
            parts = []
            for i, entry in enumerate(entries):
                parts.append((i * half_a, 4 * k + entry, 0, blocks_a))
                parts.append((i * half_a + blocks_a * DH, 4 * k + entry, 0, 0))
            return parts

        def high_of(k, entries):
            return [
                (i * half_b, 4 * k + entry, blocks_a, blocks_b) for i, entry in enumerate(entries)
            ]

        sent, kept, far, order = {}, {}, {}, []

        def gather(pieces):
            result = fetch(table_back, (grad_near, grad_ffn, grad_ffn_got), extra_grad, pieces, order)
            order[:] = [result[0]]
            return result

        def whole_of(k, entry):
            at = 4 * k + entry
            return [
                (0, at, 0, blocks_a),
                (blocks_a * DH, at, 0, 0),
                (half_a, at, blocks_a, blocks_b),
            ]

        def send(k, after):
            send_x, send_y = gather([low_of(k, (1, 3)), high_of(k, (2, 3))])
            got = fabric.to_x(gate(send_x, after)), fabric.to_y(gate(send_y, after))
            sent[k] = [(value, value) for value in got]

        def keep(k):
            kept[k] = gather([low_of(k, (0, 2)), high_of(k, (0, 1))])

        def pass_on(k):
            sum_a, sum_b = turn(kept[k][0], sent[k][0][1], kept[k][1], sent[k][1][1], order)
            far[k] = fabric.to_y(sum_a), fabric.to_x(sum_b)
            order[:] = [sum_a]

        def finish(k, running):
            half = [(kept[k][i], sent[k][i][0], far[k][i]) for i in range(2)]
            result = total(*half, running, order)
            order[:] = [result]
            return fabric.to_z(result)

        last = rings - 1
        (diagonal,) = gather([whole_of(last, 3)])
        diagonal = fabric.to_z(diagonal)
        send_x, send_y = gather([whole_of(last, 1), whole_of(last, 2)])
        got_x, got_y = fabric.to_x(send_x), fabric.to_y(send_y)
        near = gather([low_of(last - 1, (1,)), high_of(last - 1, (2,))])
        got_near = fabric.to_x(near[0]), fabric.to_y(near[1])
        send_x, send_y = gather([low_of(last - 1, (3,)), high_of(last - 1, (3,))])
        (here,) = gather([whole_of(last, 0)])
        keep(last - 1)
        mine, theirs = project(place_at, qkv_grad, w_near, 0, order, TINY)
        running, send_x, send_y = merge(
            send_x, send_y, diagonal, [here, got_x, got_y], [theirs, *got_near]
        )
        order[:] = [send_x]
        running = fabric.to_z(running)
        got_far = fabric.to_x(send_x), fabric.to_y(send_y)
        sent[last - 1] = list(zip(got_near, got_far))
        for k in range(last - 1, -1, -1):
            pass_on(k)
            if k:
                send(k - 1, far[k])
                running = finish(k, running)
                keep(k - 1)
        final = [(kept[0][i], sent[0][i][0], far[0][i]) for i in range(2)]
    else:
        pieces = []
        for i in range(batch_ways * panels):
            base = i * own.shape[0]
            pieces += [
                (base, i, 0, blocks_a),
                (base + blocks_a * DH, i, 0, 0),
                (base + half_a, i, blocks_a, blocks_b),
            ]
        chunks = fetch_all(table, grad_near, extra_grad, pieces)
        chunks = chunks.reshape(batch_ways, panels, own.shape[0], 128)
        chunks = lax.psum_scatter(chunks, "dp", scatter_dimension=0, tiled=False)
        reduced = lax.psum_scatter(
            chunks,
            "mp",
            scatter_dimension=0,
            tiled=False,
            axis_index_groups=fabric.same_groups,
        ).astype(jnp.float32)

        block_grads = jnp.concatenate([reduced[: blocks_a * DH], reduced[half_a:]], axis=0)
        vector_grads = reduced[blocks_a * DH : half_a]

    scale = 1.0 / (shard_rows * model_ways * batch_ways)
    state = (
        left_roots[0],
        right_roots[0],
        left_stats[0],
        right_stats[0],
        jnp.swapaxes(weight_store[0], 1, 2),
    )
    if wide:
        block_grads, vector_grads, *renewed = last_step(scale, *final, running, *state)
        mine, got = fabric.gather_back((mine, theirs))
    else:
        block_grads = block_grads.reshape(owned, DH, 128)
        renewed = shampoo(scale, block_grads, *state)
        mine, got = fabric.gather_back([product(qkv_grad, w_qkv, 0, 0)])
    new_left, new_right, new_weights = renewed
    input_grad = sum(v.astype(jnp.float32) for v in (hidden_grad, mine, got))
    vector_grads = vector_grads.reshape(EXTRA * 128)
    head_grad_mine = vector_grads[:head_part]
    shared_grad_mine = vector_grads[head_part : head_part + shared_part]

    head_one, head_two, head_new = adam_update(
        head_vectors[0], head_first[0], head_second[0], head_grad_mine
    )
    shared_one, shared_two, shared_new = adam_update(
        shared_vectors, shared_first, shared_second, shared_grad_mine
    )
    return (
        layer_value,
        input_grad,
        jnp.swapaxes(block_grads, 1, 2)[None],
        new_left[None],
        new_right[None],
        jnp.swapaxes(new_weights, 1, 2)[None],
        head_one[None],
        head_two[None],
        head_new[None],
        shared_one,
        shared_two,
        shared_new,
    )


def solution(mesh):
    rows, blocks, vector, head = P(BOTH, None), P("mp", "dp", None, None), P(BOTH), P("mp", "dp")
    return jax.shard_map(
        partial(shards, (mesh.shape["dp"], mesh.shape["mp"])),
        mesh=mesh,
        in_specs=(rows, rows, P("dp", None), blocks, P("mp", None))
        + (blocks,) * 4
        + (head,) * 3
        + (vector,) * 3,
        out_specs=(rows, rows) + (blocks,) * 4 + (head,) * 3 + (vector,) * 3,
        check_vma=False,
    )
```
